32 devices in a mesh: row: 4 (over x, core), col: 8 (over z, y).
Axes of the slice: x: 2, y: 2, z: 4, core: 2. Of those that a mesh axis runs over, the one named last changes fastest.
Arguments:
- currents: bfloat16 [12288, 256], P(('row', 'col')), may hold values from -6 to 6
- incidence: int32 [2, 12288], P(None, ('row', 'col')), may hold values from 0 to 8191, as said below
- centroids: int32 [3, 8192], P(None, ('row', 'col')), may hold values from 0 to 255, as said below
- sweep_weights: float32 [2], replicated, may hold values from 0.2 to 0.6
Outputs:
- updated: bfloat16 [12288, 256], P(('row', 'col'))
- potentials: bfloat16 [8192, 256], P(('row', 'col'))
The draws below stay inside these ranges and needn't reach their ends.
Inputs may be any that keep to these rules, and one draw needn't show every extreme that they name: `incidence`: triangles o * 256 to (o + 1) * 256 - 1 form owner block o. Counting both rows, the edges of one device name at most 64 triangles of any one owner block, and exactly 64 of some block on every device. `centroids`: first two rows from 0 to 255, third row from 0 to 3.
All inputs are finite; a program needn't handle non-finite values.
Results may differ from the reference program's by a relative error of at most 0.006.
Values may be sent and summed in bfloat16 or wider, within the bound.
No kernel may reach another device: no remote copies, remote signals or barrier semaphores. Data moves between devices by JAX's collectives and lax.ppermute only.
A program may use at most 128 MiB of HBM per device.

```python
import math
import jax
import jax.numpy as jnp
from jax import lax

TRI_DEV = 256
EXC = 128
SWEEPS = 2
GRID = 256
DEPTH = 4
EDGE_DEV = 384
CAP = 64
TRIANGLES = 8192
EDGES = 12288
DEVICES = 32


def draw_incidence(key, part):
    cells = DEVICES * CAP
    contributions = 2 * EDGE_DEV
    n_hot = max(1, DEVICES // 16)
    hot_order = jax.random.permutation(jax.random.fold_in(key, 11), DEVICES)
    hot_flag = jnp.zeros((DEVICES,), jnp.int32).at[hot_order[:n_hot]].set(1)
    owner_of_cell = jnp.arange(cells, dtype=jnp.int32) // CAP
    spread = max(1, 2 ** 28 // cells)

    def one_device(device_key):
        key_full, key_base, key_perm, key_local = jax.random.split(device_key, 4)
        full_owner = jax.random.randint(key_full, (), 0, DEVICES)
        base = jax.random.randint(key_base, (cells,), 0, spread) * cells + jnp.arange(cells, dtype=jnp.int32)
        score = base + hot_flag[owner_of_cell] * 2 ** 28 + (owner_of_cell == full_owner).astype(jnp.int32) * 2 ** 29
        _, chosen = lax.top_k(score, contributions)
        order = jax.random.permutation(key_perm, contributions)
        chosen = chosen[order]
        local = jax.random.randint(key_local, (contributions,), 0, TRI_DEV)
        triangle = chosen // CAP * TRI_DEV + local
        return triangle.reshape(2, EDGE_DEV)
    device_keys = jax.random.split(jax.random.fold_in(key, 5), DEVICES)
    per_device = jax.vmap(one_device)(device_keys)
    return jnp.transpose(per_device, (1, 0, 2)).reshape(2, DEVICES * EDGE_DEV).astype(jnp.int32)


def draw_centroids(key, part):
    key_x, key_y, key_z = jax.random.split(jax.random.fold_in(key, 3), 3)
    first = jax.random.randint(key_x, (TRIANGLES,), 0, GRID)
    second = jax.random.randint(key_y, (TRIANGLES,), 0, GRID)
    third = jax.random.randint(key_z, (TRIANGLES,), 0, DEPTH)
    return jnp.stack([first, second, third]).astype(jnp.int32)


def level_of(stream_key, extent, cuts, smallest, top_value):
    def one(position, shards_of):
        draws = jax.random.uniform(jax.random.fold_in(jax.random.fold_in(stream_key, 6), position), (shards_of,), jnp.float32, smallest / len(cuts), top_value / len(cuts))
        return jnp.repeat(jnp.exp(draws), extent[position] // shards_of).reshape((-1,) + (1,) * (len(extent) - position - 1))

    factor_of = one(*cuts[0])
    for cut in cuts[1:]:
        factor_of = factor_of * one(*cut)
    return factor_of


def scatter_about(rng, extent, width, limit, shards=(), held_as=jnp.bfloat16):
    level = level_of(rng, extent, shards, -0.22, 0.18) if shards else 1.0
    entries = jax.random.normal(rng, extent, jnp.float32) * width * level
    return jnp.minimum(jnp.maximum(entries, -limit), limit).astype(held_as)


def setup_inputs(seed: int = 0) -> dict:
    arg_keys = jax.random.split(jax.random.key(seed), 5)
    currents = scatter_about(arg_keys[0], (EDGES, 2 * EXC), 1.0, 6.0, ((0, 32),))
    incidence = draw_incidence(jax.random.fold_in(arg_keys[4], 71), 0)
    centroids = draw_centroids(jax.random.fold_in(arg_keys[4], 71), 0)
    sweep_weights = jnp.clip(jnp.exp(jax.random.uniform(arg_keys[3], (SWEEPS,), jnp.float32, math.log(0.2), math.log(0.6))), 0.2, 0.6)
    return {"currents": currents, "incidence": incidence, "centroids": centroids, "sweep_weights": sweep_weights}


WAVE = 0.19634954084936207
SOFT = 1.0
SPACING = 0.2

def tile_pair(row_pts, col_pts):
    dx = (row_pts[0][:, None] - col_pts[0][None, :]).astype(jnp.float32)
    dy = (row_pts[1][:, None] - col_pts[1][None, :]).astype(jnp.float32)
    dz = (row_pts[2][:, None] - col_pts[2][None, :]).astype(jnp.float32)
    radius = jnp.sqrt(dx * dx + dy * dy + dz * dz + SOFT * SOFT)
    scaled = SPACING / radius
    return ((scaled * jnp.cos(WAVE * radius)).astype(jnp.bfloat16), (-scaled * jnp.sin(WAVE * radius)).astype(jnp.bfloat16))

def blend(real_part, imag_part):
    half = real_part.shape[1] // 2
    return jnp.concatenate([real_part[:, :half] - imag_part[:, half:], real_part[:, half:] + imag_part[:, :half]], 1)

def potentials_of(charges, centroids):
    total = centroids.shape[1]
    block = min(512, total)

    def one_block(index):
        points = lax.dynamic_slice_in_dim(centroids, index * block, block, 1)
        g_real, g_imag = tile_pair(points, centroids)
        return blend(jnp.dot(g_real, charges, preferred_element_type=jnp.float32), jnp.dot(g_imag, charges, preferred_element_type=jnp.float32))
    blocks = lax.map(one_block, jnp.arange(total // block, dtype=jnp.int32))
    return blocks.reshape(total, charges.shape[1])

def reference(currents, incidence, centroids, sweep_weights):
    total = centroids.shape[1]
    current = currents
    potential = None
    for sweep in range(SWEEPS):
        flow = current.astype(jnp.float32)
        charges = jnp.zeros((total, flow.shape[1]), jnp.float32)
        charges = charges.at[incidence[0]].add(flow).at[incidence[1]].add(-flow)
        charges = charges.astype(jnp.bfloat16)
        potential = potentials_of(charges, centroids).astype(jnp.bfloat16)
        slope = potential[incidence[0]].astype(jnp.float32) - potential[incidence[1]].astype(jnp.float32)
        current = (flow - sweep_weights[sweep] * slope).astype(jnp.bfloat16)
    return (current, potential)
```

```python
import functools

import jax
import jax.numpy as jnp
from jax import lax
from jax.experimental import pallas as pl
from jax.experimental.pallas import tpu as pltpu
from jax.sharding import PartitionSpec as P

SPACING = 0.2
TURNS = 32.0
AXES = ("row", "col")
ROUND = 12582912.0
COS = (
    0.9999992107823218,
    -19.738980355763992,
    64.92865742103312,
    -85.27162153429882,
    58.79049212013072,
    -21.07110562764302,
)
SIN = (
    6.283184916495431,
    -41.34158923268858,
    81.59994332978287,
    -76.61447253124996,
    41.342882354568324,
    -12.471243535026977,
)
VMEM_LIMIT = 48 * 2**20


def poly(coefs, scale, u):
    value = jnp.full_like(u, coefs[-1] * scale)
    for coef in coefs[-2::-1]:
        value = value * u + coef * scale
    return value


def tile_kernel(row_ref, col_ref, real_ref, imag_ref):
    square = jnp.dot(row_ref[...], col_ref[...], preferred_element_type=jnp.float32)
    inverse = lax.rsqrt(square)
    turns = square * inverse
    frac = turns - ((turns + ROUND) - ROUND)
    u = frac * frac
    real_ref[...] = (poly(COS, SPACING / TURNS, u) * inverse).astype(jnp.bfloat16)
    imag_ref[...] = (poly(SIN, -SPACING / TURNS, u) * (frac * inverse)).astype(jnp.bfloat16)


def build_tiles(row_points, col_points, block=512):
    rows, cols = row_points.shape[1], col_points.shape[1]
    block = min(block, cols)

    def norms(points):
        total = jnp.sum(points * points, axis=0)
        return total & 255, total & 0xFF00, total & 0xFF0000

    one_row = jnp.ones((rows,), jnp.int32)
    one_col = jnp.ones((cols,), jnp.int32)
    r0, r1, r2 = norms(row_points)
    c0, c1, c2 = norms(col_points)
    row_features = jnp.stack(
        [-2 * row_points[0], -2 * row_points[1], -2 * row_points[2], r0, r1, r2]
        + [one_row] * 4
        + [0 * one_row] * 6,
        axis=1,
    )
    col_features = jnp.stack(
        [col_points[0], col_points[1], col_points[2], one_col, one_col, one_col]
        + [c0, c1, c2, one_col]
        + [0 * one_col] * 6,
        axis=0,
    )
    row_features = (row_features.astype(jnp.float32) / (TURNS * TURNS)).astype(jnp.bfloat16)
    col_features = col_features.astype(jnp.bfloat16)
    depth = row_features.shape[1]
    return pl.pallas_call(
        tile_kernel,
        grid=(cols // block,),
        in_specs=[
            pl.BlockSpec((rows, depth), lambda j: (0, 0)),
            pl.BlockSpec((depth, block), lambda j: (0, j)),
        ],
        out_specs=[pl.BlockSpec((rows, block), lambda j: (0, j))] * 2,
        out_shape=[jax.ShapeDtypeStruct((rows, cols), jnp.bfloat16)] * 2,
        compiler_params=pltpu.CompilerParams(vmem_limit_bytes=VMEM_LIMIT),
        cost_estimate=pl.CostEstimate(
            flops=rows * cols * 60, bytes_accessed=rows * cols * 4, transcendentals=rows * cols
        ),
    )(row_features, col_features)


def adjacency_kernel(chunk, mark_ref, other_ref, out_ref):
    rows, block = out_ref.shape
    ends = other_ref.shape[0]
    base = pl.program_id(0) * block
    lane = lax.broadcasted_iota(jnp.int32, (chunk, block), 1) + base
    wanted = lax.broadcasted_iota(jnp.int32, (rows, chunk), 0) + 1

    def step(k, total):
        marks = mark_ref[:, pl.ds(pl.multiple_of(k * chunk, chunk), chunk)]
        others = other_ref[pl.ds(pl.multiple_of(k * chunk, chunk), chunk), :]
        pick = (marks == wanted).astype(jnp.float32).astype(jnp.bfloat16)
        spread = (others == lane).astype(jnp.float32).astype(jnp.bfloat16)
        return total + jnp.dot(pick, spread, preferred_element_type=jnp.float32)

    total = lax.fori_loop(0, ends // chunk, step, jnp.zeros((rows, block), jnp.float32))
    out_ref[...] = total.astype(jnp.bfloat16)


def build_adjacency(marks, others, rows, cols, block=512, chunk=256):
    ends = marks.shape[0]
    block = min(block, cols)
    return pl.pallas_call(
        functools.partial(adjacency_kernel, chunk),
        grid=(cols // block,),
        in_specs=[
            pl.BlockSpec((1, ends), lambda j: (0, 0)),
            pl.BlockSpec((ends, 1), lambda j: (0, 0)),
        ],
        out_specs=pl.BlockSpec((rows, block), lambda j: (0, j)),
        out_shape=jax.ShapeDtypeStruct((rows, cols), jnp.bfloat16),
        compiler_params=pltpu.CompilerParams(vmem_limit_bytes=VMEM_LIMIT),
        cost_estimate=pl.CostEstimate(
            flops=2 * rows * cols * ends, bytes_accessed=rows * cols * 2, transcendentals=0
        ),
    )(marks.reshape(1, ends), others.reshape(ends, 1))


def blend(real_part, imag_part):
    half = real_part.shape[1] // 2
    return jnp.concatenate(
        [real_part[:, :half] - imag_part[:, half:], real_part[:, half:] + imag_part[:, :half]], 1
    )


def per_device(currents, incidence, centroids, sweep_weights):
    devices = lax.axis_size("row") * lax.axis_size("col")
    me = lax.axis_index(AXES)
    tri_dev = centroids.shape[1]
    edge_dev, width = currents.shape
    slots = 8 * tri_dev // devices
    cells = devices * slots
    sweeps = sweep_weights.shape[0]
    triangles = devices * tri_dev

    numbers = jnp.concatenate([incidence.reshape(-1), centroids.reshape(-1)])
    numbers = lax.all_gather(numbers, AXES, axis=0, tiled=False)
    ends = numbers[:, : 2 * edge_dev].reshape(devices, 2, edge_dev)
    plus, minus = ends[:, 0].reshape(1, -1), ends[:, 1].reshape(1, -1)
    points = numbers[:, 2 * edge_dev :].reshape(devices, 3, tri_dev)
    points = points.transpose(1, 0, 2).reshape(3, triangles)
    all_currents = lax.all_gather(currents, AXES, axis=0, tiled=True)

    triangle = incidence.reshape(-1)
    other = incidence[::-1].reshape(-1)
    owner = triangle // tri_dev
    local = triangle % tri_dev
    hits = (owner[:, None] == jnp.arange(devices, dtype=jnp.int32)[None, :]).astype(jnp.int32)
    rank = jnp.sum(hits * jnp.cumsum(hits, axis=0), axis=1) - 1
    slot = owner * slots + rank
    packed = other * (2 * tri_dev) + local + 1
    outgoing = jnp.zeros((cells,), jnp.int32).at[slot].set(packed)
    arrived = lax.all_to_all(
        outgoing.reshape(devices, slots), AXES, split_axis=0, concat_axis=0, tiled=True
    ).reshape(cells)
    marks = arrived % (2 * tri_dev)
    others = arrived // (2 * tri_dev)

    real_tile, imag_tile = build_tiles(centroids, points)
    mine = (me * tri_dev + jnp.arange(tri_dev, dtype=jnp.int32))[:, None]
    signs = (plus == mine).astype(jnp.bfloat16) - (minus == mine).astype(jnp.bfloat16)
    charge = jnp.dot(signs, all_currents, preferred_element_type=jnp.float32)
    neighbours = build_adjacency(marks, others, tri_dev, triangles)
    degree = jnp.sum((marks[None, :] == jnp.arange(1, tri_dev + 1)[:, None]).astype(jnp.float32), 1)

    current = currents
    potential = None
    for sweep in range(sweeps):
        piece = lax.all_gather(charge.astype(jnp.bfloat16), AXES, axis=0, tiled=True)
        potential = blend(
            jnp.dot(real_tile, piece, preferred_element_type=jnp.float32),
            jnp.dot(imag_tile, piece, preferred_element_type=jnp.float32),
        ).astype(jnp.bfloat16)
        everywhere = lax.all_gather(potential, AXES, axis=0, tiled=True)
        if sweep + 1 < sweeps:
            around = jnp.dot(neighbours, everywhere, preferred_element_type=jnp.float32)
            change = degree[:, None] * potential.astype(jnp.float32) - around
            charge = charge - sweep_weights[sweep] * change
        picked = everywhere[triangle]
        slope = picked[:edge_dev].astype(jnp.float32) - picked[edge_dev:].astype(jnp.float32)
        current = (current.astype(jnp.float32) - sweep_weights[sweep] * slope).astype(jnp.bfloat16)
    return current, potential


def solution(mesh):
    in_specs = (P(AXES, None), P(None, AXES), P(None, AXES), P())
    out_specs = (P(AXES, None), P(AXES, None))
    return jax.shard_map(
        per_device, mesh=mesh, in_specs=in_specs, out_specs=out_specs, check_vma=False
    )
```

```python
import functools
import math

import jax
import jax.numpy as jnp
from jax import lax
from jax.experimental import pallas as pl
from jax.experimental.pallas import tpu as pltpu
from jax.sharding import PartitionSpec as P

SPACING = 0.2
TURNS = 32.0
AXES = ("row", "col")
ROUND = 12582912.0
COS = (
    0.9999992107823218,
    -19.738980355763992,
    64.92865742103312,
    -85.27162153429882,
    58.79049212013072,
    -21.07110562764302,
)
SIN = (
    6.283184916495431,
    -41.34158923268858,
    81.59994332978287,
    -76.61447253124996,
    41.342882354568324,
    -12.471243535026977,
)
PARAMS = pltpu.CompilerParams(vmem_limit_bytes=48 * 2**20)
F32, BF16, I32 = jnp.float32, jnp.bfloat16, jnp.int32


def whole():
    return pl.BlockSpec(memory_space=pltpu.VMEM)


def iota(shape, dim):
    return lax.broadcasted_iota(I32, shape, dim)


def ones_where(mask):
    return jnp.where(mask, jnp.ones((), F32), jnp.zeros((), F32)).astype(BF16)


def matmul(a, b):
    return jnp.dot(a, b, preferred_element_type=F32)


def matmul_nt(a, b):
    return lax.dot_general(a, b, (((1,), (1,)), ((), ())), preferred_element_type=F32)


class Layout:
    def __init__(self, n_row, n_col):
        self.core = 2 if n_row % 2 == 0 else 1
        self.x = n_row // self.core
        self.y = math.gcd(n_col, self.x)
        self.z = n_col // self.y
        self.devices = n_row * n_col
        self.plane = [(dx, dy) for dx in range(self.x) for dy in range(self.y)]

    def digits(self, index):
        y = index % self.y
        z = index // self.y % self.z
        core = index // (self.y * self.z) % self.core
        return index // (self.y * self.z * self.core), core, z, y

    def shift(self, value, dx=0, dc=0, dz=0, dy=0):
        pairs = []
        for i in range(self.devices):
            x, c, z, y = self.digits(i)
            x, c = (x + dx) % self.x, (c + dc) % self.core
            z, y = (z + dz) % self.z, (y + dy) % self.y
            pairs.append((i, ((x * self.core + c) * self.z + z) * self.y + y))
        return lax.ppermute(value, AXES, pairs)

    def line(self, value):
        along = [value] + [self.shift(value, dz=-dz) for dz in range(1, self.z)]
        pieces = []
        for piece in along:
            pieces.append(piece)
            pieces += [self.shift(piece, dc=-dc) for dc in range(1, self.core)]
        return pieces

    def across(self, value):
        return [value] + [self.shift(value, dx=-dx, dy=-dy) for dx, dy in self.plane[1:]]

    def give(self, blocks):
        return [
            self.shift(block, dx=dx, dy=dy)
            for block, (dx, dy) in zip(blocks, self.plane[1:])
        ]

    def place(self, triangle, tri_dev, me):
        x, core, z, y = self.digits(triangle // tri_dev)
        mx, mcore, mz, my = self.digits(me)
        block = (z - mz) % self.z * self.core + (core - mcore) % self.core
        inside = (x == mx) & (y == my)
        return jnp.where(inside, block * tri_dev + triangle % tri_dev, -1)


def route_kernel(tri_dev, slots, tri_ref, other_ref, cur_ref, out_ref, label_ref):
    ends, edges = tri_ref.shape[1], cur_ref.shape[0]
    cells = out_ref.shape[0]
    devices = cells // slots
    chunk = min(256, cells)
    tri, other = tri_ref[...], other_ref[...]
    owner = tri // tri_dev
    hits = iota((devices, ends), 0) == owner
    upper = ones_where(iota((ends, ends), 0) <= iota((ends, ends), 1))
    count = matmul(ones_where(hits), upper)
    rank = jnp.sum(jnp.where(hits, count, 0.0), axis=0, keepdims=True)
    slot = owner * slots + rank.astype(I32) - 1
    digits = jnp.concatenate(
        [tri % tri_dev + 1, other & 255, other >> 8, jnp.zeros((5, ends), I32)], axis=0
    )
    digits = digits.astype(F32).astype(BF16)
    for base in range(0, cells, chunk):
        mask = jnp.where(iota((chunk, ends), 0) + base == slot, 1.0, 0.0).astype(F32)
        signed = (mask[:, :edges] - mask[:, edges:]).astype(BF16)
        out_ref[base : base + chunk, :] = matmul(signed, cur_ref[...]).astype(BF16)
        label = matmul_nt(digits, mask.astype(BF16)).astype(I32)
        label_ref[:, base : base + chunk] = (label[2:3] * 256 + label[1:2]) * (
            2 * tri_dev
        ) + label[0:1]


def route(incidence, currents, tri_dev, slots, cells):
    edges, width = currents.shape
    return pl.pallas_call(
        functools.partial(route_kernel, tri_dev, slots),
        in_specs=[whole()] * 3,
        out_specs=[whole()] * 2,
        out_shape=[
            jax.ShapeDtypeStruct((cells, width), BF16),
            jax.ShapeDtypeStruct((1, cells), I32),
        ],
        compiler_params=PARAMS,
    )(incidence.reshape(1, -1), incidence[::-1].reshape(1, -1), currents)


def features(points, scale, first):
    rows, count = points.shape
    square = jnp.sum(points * points, axis=0, keepdims=True)
    norms = [square & 255, square & 0xFF00, square & 0xFF0000]
    ones = [jnp.ones_like(square)] * 3
    zeros = [jnp.zeros((16 - rows - 7, count), I32)]
    if first:
        parts = [-2 * points] + norms + ones + [ones[0]] + zeros
    else:
        parts = [points] + ones + norms + [ones[0]] + zeros
    return (jnp.concatenate(parts, axis=0).astype(F32) * scale).astype(BF16)


def poly(coefs, scale, u):
    value = jnp.full_like(u, coefs[-1] * scale)
    for coef in coefs[-2::-1]:
        value = value * u + coef * scale
    return value


def tile_kernel(row_ref, col_ref, real_ref, imag_ref):
    row = features(row_ref[...], 1.0 / (TURNS * TURNS), True)
    col = features(col_ref[...], 1.0, False)
    square = lax.dot_general(row, col, (((0,), (0,)), ((), ())), preferred_element_type=F32)
    inverse = lax.rsqrt(square)
    turns = square * inverse
    frac = turns - ((turns + ROUND) - ROUND)
    u = frac * frac
    real_ref[...] = (poly(COS, SPACING / TURNS, u) * inverse).astype(BF16)
    imag_ref[...] = (poly(SIN, -SPACING / TURNS, u) * (frac * inverse)).astype(BF16)


def build_tiles(row_points, col_points, tri_dev):
    rows, cols = row_points.shape[1], col_points.shape[1]
    block = min(512, cols)
    return pl.pallas_call(
        tile_kernel,
        grid=(rows // tri_dev, cols // block),
        in_specs=[
            pl.BlockSpec((3, tri_dev), lambda i, j: (0, i)),
            pl.BlockSpec((3, block), lambda i, j: (0, j)),
        ],
        out_specs=[pl.BlockSpec((tri_dev, block), lambda i, j: (i, j))] * 2,
        out_shape=[jax.ShapeDtypeStruct((rows, cols), BF16)] * 2,
        compiler_params=PARAMS,
        cost_estimate=pl.CostEstimate(
            flops=rows * cols * 60, bytes_accessed=rows * cols * 4, transcendentals=rows * cols
        ),
    )(row_points, col_points)


def pick(row, base, count):
    low = jnp.where((row >= base) & (row < base + count), row - base, -1)
    wanted = iota((count, row.shape[1]), 0).astype(F32).astype(BF16)
    same = wanted == low.astype(F32).astype(BF16)
    return jnp.where(same, jnp.ones((), BF16), jnp.zeros((), BF16))


def adjacency_kernel(mark_ref, place_ref, out_ref):
    rows, cols = out_ref.shape
    mark, place = mark_ref[0], place_ref[0]
    low = pick(jnp.where(place >= 0, place % rows, -1), 0, rows)
    for base in range(0, cols, rows):
        inside = (place >= base) & (place < base + rows)
        here = pick(jnp.where(inside, mark - 1, -1), 0, rows)
        out_ref[:, base : base + rows] = matmul_nt(here, low).astype(BF16)


def build_adjacency(marks, places, rows, cols):
    count, _, ends = marks.shape
    return pl.pallas_call(
        adjacency_kernel,
        grid=(count,),
        in_specs=[pl.BlockSpec((1, 1, ends), lambda j: (j, 0, 0))] * 2,
        out_specs=pl.BlockSpec((rows, cols), lambda j: (j, 0)),
        out_shape=jax.ShapeDtypeStruct((count * rows, cols), BF16),
        compiler_params=PARAMS,
        cost_estimate=pl.CostEstimate(
            flops=2 * count * rows * cols * ends, bytes_accessed=0, transcendentals=0
        ),
    )(marks, places)


def incidence_kernel(tri_dev, place_ref, out_ref):
    edges, cols = out_ref.shape
    plus, minus = place_ref[0, :, :edges], place_ref[0, :, edges:]
    eye = ones_where(iota((edges, edges), 0) == iota((edges, edges), 1))
    for base in range(0, cols, tri_dev):
        signed = pick(plus, base, tri_dev) - pick(minus, base, tri_dev)
        out_ref[:, base : base + tri_dev] = matmul_nt(eye, signed).astype(BF16)


def build_incidence(places, tri_dev, cols):
    count, _, ends = places.shape
    edges = ends // 2
    return pl.pallas_call(
        functools.partial(incidence_kernel, tri_dev),
        grid=(count,),
        in_specs=[pl.BlockSpec((1, 1, ends), lambda j: (j, 0, 0))],
        out_specs=pl.BlockSpec((edges, cols), lambda j: (j, 0)),
        out_shape=jax.ShapeDtypeStruct((count * edges, cols), BF16),
        compiler_params=PARAMS,
        cost_estimate=pl.CostEstimate(
            flops=2 * count * edges * cols * edges, bytes_accessed=0, transcendentals=0
        ),
    )(places)


def collect_kernel(mark_ref, value_ref, charge_ref, degree_ref):
    here = pick(mark_ref[...] - 1, 0, charge_ref.shape[0])
    charge_ref[...] = matmul(here, value_ref[...])
    degree_ref[...] = matmul(here, jnp.ones((here.shape[1], degree_ref.shape[1]), BF16))


def collect(marks, values, tri_dev):
    return pl.pallas_call(
        collect_kernel,
        in_specs=[whole()] * 2,
        out_specs=[whole()] * 2,
        out_shape=[
            jax.ShapeDtypeStruct((tri_dev, values.shape[1]), F32),
            jax.ShapeDtypeStruct((tri_dev, 128), F32),
        ],
        compiler_params=PARAMS,
    )(marks, values)


def apply_kernel(mats, count, *refs):
    matrices, pieces, outs = refs[:mats], refs[mats:-count], refs[-count:]
    block = pieces[0].shape[0]
    half = pieces[0].shape[1] // 2
    sums = []
    for matrix in matrices:
        total = None
        for k, piece in enumerate(pieces):
            term = matmul(matrix[:, k * block : (k + 1) * block], piece[...])
            total = term if total is None else total + term
        sums.append(total)
    value = sums[0]
    if mats == 2:
        real, imag = sums
        value = jnp.concatenate(
            [real[:, :half] - imag[:, half:], real[:, half:] + imag[:, :half]], axis=1
        )
    for k, out in enumerate(outs):

        @pl.when(pl.program_id(0) == k)
        def _(out=out):
            out[...] = value.astype(out.dtype)


def apply(matrices, pieces, count):
    rows, cols = matrices[0].shape
    block = rows // count
    size, width = pieces[0].shape
    return pl.pallas_call(
        functools.partial(apply_kernel, len(matrices), count),
        grid=(count,),
        in_specs=[pl.BlockSpec((block, cols), lambda j: (j, 0))] * len(matrices)
        + [pl.BlockSpec((size, width), lambda j: (0, 0))] * len(pieces),
        out_specs=[pl.BlockSpec((block, width), lambda j: (0, 0))] * count,
        out_shape=[
            jax.ShapeDtypeStruct((block, width), F32 if k == 0 else BF16) for k in range(count)
        ],
        compiler_params=PARAMS,
        cost_estimate=pl.CostEstimate(
            flops=2 * len(matrices) * rows * cols * width,
            bytes_accessed=2 * len(matrices) * rows * cols,
            transcendentals=0,
        ),
    )(*matrices, *pieces)


def total_of(layout, blocks):
    total = blocks[0]
    for part in layout.give(blocks[1:]):
        total = total + part.astype(F32)
    return total


def per_device(currents, incidence, centroids, sweep_weights):
    layout = Layout(lax.axis_size("row"), lax.axis_size("col"))
    devices = layout.devices
    me = lax.axis_index(AXES)
    tri_dev = centroids.shape[1]
    edge_dev, width = currents.shape
    slots = 8 * tri_dev // devices
    cells = devices * slots
    sweeps = sweep_weights.shape[0]
    count = len(layout.plane)
    cols = layout.z * layout.core * tri_dev

    outgoing, labels = route(incidence, currents, tri_dev, slots, cells)
    labels = lax.all_to_all(
        labels.reshape(devices, slots), AXES, split_axis=0, concat_axis=0, tiled=True
    ).reshape(1, cells)
    arrived = lax.all_to_all(
        outgoing.reshape(devices, slots, width), AXES, split_axis=0, concat_axis=0, tiled=True
    ).reshape(cells, width)

    line_points = jnp.concatenate(layout.line(centroids), axis=1)
    numbers = jnp.concatenate([incidence.reshape(-1), centroids.reshape(-1)])
    numbers = jnp.stack(layout.across(numbers))
    ends = numbers[:, : 2 * edge_dev].reshape(count, 1, 2 * edge_dev)
    plane_points = numbers[:, 2 * edge_dev :].reshape(count, 3, tri_dev)
    plane_points = plane_points.transpose(1, 0, 2).reshape(3, count * tri_dev)
    tiles = build_tiles(plane_points, line_points, tri_dev)
    slopes_of = build_incidence(layout.place(ends, tri_dev, me), tri_dev, cols)
    all_labels = jnp.stack(layout.across(labels))
    marks, others = all_labels % (2 * tri_dev), all_labels // (2 * tri_dev)
    places = jnp.where(marks > 0, layout.place(others, tri_dev, me), -1)
    neighbours = build_adjacency(marks, places, tri_dev, cols)

    charge, degree = collect(labels % (2 * tri_dev), arrived, tri_dev)
    current = currents
    potential = None
    for sweep in range(sweeps):
        pieces = layout.line(charge.astype(BF16))
        potential = total_of(layout, apply(tiles, pieces, count)).astype(BF16)
        pieces = layout.line(potential)
        if sweep + 1 < sweeps:
            around = total_of(layout, apply([neighbours], pieces, count))
            change = degree[:, :1] * potential.astype(F32) - around
            charge = charge - sweep_weights[sweep] * change
        slope = total_of(layout, apply([slopes_of], pieces, count))
        current = (current.astype(F32) - sweep_weights[sweep] * slope).astype(BF16)
    return current, potential


def solution(mesh):
    in_specs = (P(AXES, None), P(None, AXES), P(None, AXES), P())
    out_specs = (P(AXES, None), P(AXES, None))
    return jax.shard_map(
        per_device, mesh=mesh, in_specs=in_specs, out_specs=out_specs, check_vma=False
    )
```

```python
import functools
import math

import jax
import jax.numpy as jnp
from jax import lax
from jax.experimental import pallas as pl
from jax.experimental.pallas import tpu as pltpu
from jax.sharding import PartitionSpec as P

SPACING = 0.2
TURNS = 32.0
AXES = ("row", "col")
ROUND = 12582912.0
COS = (
    0.9999992107823218,
    -19.738980355763992,
    64.92865742103312,
    -85.27162153429882,
    58.79049212013072,
    -21.07110562764302,
)
SIN = (
    6.283184916495431,
    -41.34158923268858,
    81.59994332978287,
    -76.61447253124996,
    41.342882354568324,
    -12.471243535026977,
)
PARAMS = pltpu.CompilerParams(vmem_limit_bytes=24 * 2**20)
PEAK = 1.15e15
F32, BF16, I32 = jnp.float32, jnp.bfloat16, jnp.int32


def whole():
    return pl.BlockSpec(memory_space=pltpu.VMEM)


def anywhere():
    return pl.BlockSpec(memory_space=pl.ANY)


def cost(microseconds):
    return pl.CostEstimate(
        flops=int(microseconds * 1e-6 * PEAK), bytes_accessed=0, transcendentals=0
    )


def iota(shape, dim):
    return lax.broadcasted_iota(I32, shape, dim)


def ones_where(mask):
    return jnp.where(mask, jnp.ones((), F32), jnp.zeros((), F32)).astype(BF16)


def matmul(a, b):
    return jnp.dot(a, b, preferred_element_type=F32)


def matmul_nt(a, b):
    return lax.dot_general(a, b, (((1,), (1,)), ((), ())), preferred_element_type=F32)


class Layout:
    def __init__(self, n_row, n_col):
        self.core = 2 if n_row % 2 == 0 else 1
        self.x = n_row // self.core
        self.y = math.gcd(n_col, self.x)
        self.z = n_col // self.y
        self.devices = n_row * n_col
        self.plane = [(dx, dy) for dx in range(self.x) for dy in range(self.y)]

    def digits(self, index):
        y = index % self.y
        z = index // self.y % self.z
        core = index // (self.y * self.z) % self.core
        return index // (self.y * self.z * self.core), core, z, y

    def shift(self, value, dx=0, dc=0, dz=0, dy=0):
        pairs = []
        for i in range(self.devices):
            x, c, z, y = self.digits(i)
            x, c = (x + dx) % self.x, (c + dc) % self.core
            z, y = (z + dz) % self.z, (y + dy) % self.y
            pairs.append((i, ((x * self.core + c) * self.z + z) * self.y + y))
        return lax.ppermute(value, AXES, pairs)

    def line(self, value):
        along = [value] + [self.shift(value, dz=-dz) for dz in range(1, self.z)]
        pieces = []
        for piece in along:
            pieces.append(piece)
            pieces += [self.shift(piece, dc=-dc) for dc in range(1, self.core)]
        return pieces

    def across(self, value):
        return [value] + [self.shift(value, dx=-dx, dy=-dy) for dx, dy in self.plane[1:]]

    def give(self, blocks):
        return [
            self.shift(block, dx=dx, dy=dy)
            for block, (dx, dy) in zip(blocks, self.plane[1:])
        ]

    def place(self, triangle, tri_dev, me):
        x, core, z, y = self.digits(triangle // tri_dev)
        mx, mcore, mz, my = self.digits(me)
        block = (z - mz) % self.z * self.core + (core - mcore) % self.core
        inside = (x == mx) & (y == my)
        return jnp.where(inside, block * tri_dev + triangle % tri_dev, -1)


def tie_kernel(*refs):
    del refs


def tie(value, *others):
    return pl.pallas_call(
        tie_kernel,
        in_specs=[anywhere()] * (1 + len(others)),
        out_specs=anywhere(),
        out_shape=jax.ShapeDtypeStruct(value.shape, value.dtype),
        input_output_aliases={0: 0},
    )(value, *others)


def route_kernel(slots, inc_ref, points_ref, cur_ref, out_ref, label_ref, number_ref):
    edges, tri_dev = inc_ref.shape[1], points_ref.shape[1]
    ends, cells = 2 * edges, out_ref.shape[0]
    devices = cells // slots
    chunk = min(256, cells)
    number_ref[...] = jnp.zeros(number_ref.shape, I32)
    number_ref[0:2, :edges] = inc_ref[...]
    number_ref[2:5, :tri_dev] = points_ref[...]
    plus, minus = inc_ref[0:1, :], inc_ref[1:2, :]
    tri = jnp.concatenate([plus, minus], axis=1)
    other = jnp.concatenate([minus, plus], axis=1)
    owner = tri // tri_dev
    hits = iota((devices, ends), 0) == owner
    upper = ones_where(iota((ends, ends), 0) <= iota((ends, ends), 1))
    count = matmul(ones_where(hits), upper)
    rank = jnp.sum(jnp.where(hits, count, 0.0), axis=0, keepdims=True).astype(I32) - 1
    slot = owner * slots + rank
    order = ones_where(iota((slots, ends), 0) == rank)
    label = jnp.zeros((devices, slots), I32)
    for digit, weight in ((tri % tri_dev + 1, 1), (other & 255, 2 * tri_dev), (other >> 8, 512 * tri_dev)):
        spread = jnp.where(hits, digit.astype(F32), 0.0).astype(BF16)
        label = label + matmul_nt(spread, order).astype(I32) * weight
    label_ref[...] = label
    for base in range(0, cells, chunk):
        mask = jnp.where(iota((chunk, ends), 0) + base == slot, 1.0, 0.0).astype(F32)
        signed = (mask[:, :edges] - mask[:, edges:]).astype(BF16)
        out_ref[base : base + chunk, :] = matmul(signed, cur_ref[...]).astype(BF16)


def route(incidence, centroids, currents, slots, devices):
    edges, width = currents.shape
    lanes = max(edges, centroids.shape[1])
    return pl.pallas_call(
        functools.partial(route_kernel, slots),
        in_specs=[whole()] * 3,
        out_specs=[whole()] * 3,
        out_shape=[
            jax.ShapeDtypeStruct((devices * slots, width), BF16),
            jax.ShapeDtypeStruct((devices, slots), I32),
            jax.ShapeDtypeStruct((8, lanes), I32),
        ],
        compiler_params=PARAMS,
        cost_estimate=cost(3),
    )(incidence, centroids, currents)


def features(points, scale, first):
    rows, count = points.shape
    square = jnp.sum(points * points, axis=0, keepdims=True)
    norms = [square & 255, square & 0xFF00, square & 0xFF0000]
    ones = [jnp.ones_like(square)] * 3
    zeros = [jnp.zeros((16 - rows - 7, count), I32)]
    if first:
        parts = [-2 * points] + norms + ones + [ones[0]] + zeros
    else:
        parts = [points] + ones + norms + [ones[0]] + zeros
    return (jnp.concatenate(parts, axis=0).astype(F32) * scale).astype(BF16)


def poly(coefs, scale, u):
    value = jnp.full_like(u, coefs[-1] * scale)
    for coef in coefs[-2::-1]:
        value = value * u + coef * scale
    return value


def tile_kernel(count, block, tri_dev, *refs):
    plane, line = refs[:count], refs[count:-4]
    real_ref, imag_ref, row_ref, col_ref = refs[-4:]

    @pl.when(pl.program_id(0) == 0)
    def _():
        for k, ref in enumerate(plane):
            row_ref[k] = features(ref[2:5, :tri_dev], 1.0 / (TURNS * TURNS), True)
        for k, ref in enumerate(line):
            col_ref[:, k * tri_dev : (k + 1) * tri_dev] = features(ref[2:5, :tri_dev], 1.0, False)

    row = row_ref[pl.program_id(0)]
    for base in range(0, col_ref.shape[1], block):
        cols = slice(base, base + block)
        square = lax.dot_general(
            row, col_ref[:, cols], (((0,), (0,)), ((), ())), preferred_element_type=F32
        )
        inverse = lax.rsqrt(square)
        turns = square * inverse
        frac = turns - ((turns + ROUND) - ROUND)
        u = frac * frac
        real_ref[:, cols] = (poly(COS, SPACING / TURNS, u) * inverse).astype(BF16)
        imag_ref[:, cols] = (poly(SIN, -SPACING / TURNS, u) * (frac * inverse)).astype(BF16)


def build_tiles(plane, line, tri_dev):
    count, cols = len(plane), len(line) * tri_dev
    shape = plane[0].shape
    return pl.pallas_call(
        functools.partial(tile_kernel, count, min(512, cols), tri_dev),
        grid=(count,),
        in_specs=[pl.BlockSpec(shape, lambda i: (0, 0))] * (count + len(line)),
        out_specs=[pl.BlockSpec((tri_dev, cols), lambda i: (i, 0))] * 2,
        out_shape=[jax.ShapeDtypeStruct((count * tri_dev, cols), BF16)] * 2,
        scratch_shapes=[pltpu.VMEM((count, 16, tri_dev), BF16), pltpu.VMEM((16, cols), BF16)],
        compiler_params=PARAMS,
        cost_estimate=cost(12),
    )(*plane, *line)


def pick(row, base, count):
    low = jnp.where((row >= base) & (row < base + count), row - base, -1)
    wanted = iota((count, row.shape[1]), 0).astype(F32).astype(BF16)
    same = wanted == low.astype(F32).astype(BF16)
    return jnp.where(same, jnp.ones((), BF16), jnp.zeros((), BF16))


def adjacency_kernel(layout, tri_dev, me_ref, *refs):
    labels, out_ref = refs[:-1], refs[-1]
    rows, cols = out_ref.shape
    for k, label_ref in enumerate(labels):

        @pl.when(pl.program_id(0) == k)
        def _(label_ref=label_ref):
            label = label_ref[...]
            mark = label % (2 * tri_dev) - 1
            place = layout.place(label // (2 * tri_dev), tri_dev, me_ref[0])
            place = jnp.where(mark >= 0, place, -1)
            low = pick(jnp.where(place >= 0, place % rows, -1), 0, rows)
            for base in range(0, cols, rows):
                inside = (place >= base) & (place < base + rows)
                here = pick(jnp.where(inside, mark, -1), 0, rows)
                out_ref[:, base : base + rows] = matmul_nt(here, low).astype(BF16)


def build_adjacency(layout, me, labels, rows, cols):
    count, shape = len(labels), labels[0].shape
    return pl.pallas_call(
        functools.partial(adjacency_kernel, layout, rows),
        grid=(count,),
        in_specs=[pl.BlockSpec(memory_space=pltpu.SMEM)]
        + [pl.BlockSpec(shape, lambda j: (0, 0))] * count,
        out_specs=pl.BlockSpec((rows, cols), lambda j: (j, 0)),
        out_shape=jax.ShapeDtypeStruct((count * rows, cols), BF16),
        compiler_params=PARAMS,
        cost_estimate=cost(10),
    )(me, *labels)


def incidence_kernel(layout, tri_dev, me_ref, *refs):
    numbers, out_ref = refs[:-1], refs[-1]
    edges, cols = out_ref.shape
    for k, number_ref in enumerate(numbers):

        @pl.when(pl.program_id(0) == k)
        def _(number_ref=number_ref):
            places = layout.place(number_ref[0:2, :edges], tri_dev, me_ref[0])
            plus, minus = places[0:1], places[1:2]
            eye = ones_where(iota((edges, edges), 0) == iota((edges, edges), 1))
            for base in range(0, cols, tri_dev):
                signed = pick(plus, base, tri_dev) - pick(minus, base, tri_dev)
                out_ref[:, base : base + tri_dev] = matmul_nt(eye, signed).astype(BF16)


def build_incidence(layout, me, numbers, edges, tri_dev, cols):
    count, shape = len(numbers), numbers[0].shape
    return pl.pallas_call(
        functools.partial(incidence_kernel, layout, tri_dev),
        grid=(count,),
        in_specs=[pl.BlockSpec(memory_space=pltpu.SMEM)]
        + [pl.BlockSpec(shape, lambda j: (0, 0))] * count,
        out_specs=pl.BlockSpec((edges, cols), lambda j: (j, 0)),
        out_shape=jax.ShapeDtypeStruct((count * edges, cols), BF16),
        compiler_params=PARAMS,
        cost_estimate=cost(6),
    )(me, *numbers)


def collect_kernel(tri_dev, label_ref, value_ref, *refs):
    charge_ref, rounded_ref, degree_ref = refs[-3:]
    here = pick(label_ref[...] % (2 * tri_dev) - 1, 0, tri_dev)
    charge = matmul(here, value_ref[...])
    charge_ref[...] = charge
    rounded_ref[...] = charge.astype(BF16)
    degree_ref[...] = matmul(here, jnp.ones((here.shape[1], degree_ref.shape[1]), BF16))


def collect(labels, values, tri_dev, after):
    width = values.shape[1]
    return pl.pallas_call(
        functools.partial(collect_kernel, tri_dev),
        in_specs=[whole()] * 2 + [anywhere()] * len(after),
        out_specs=[whole()] * 3,
        out_shape=[
            jax.ShapeDtypeStruct((tri_dev, width), F32),
            jax.ShapeDtypeStruct((tri_dev, width), BF16),
            jax.ShapeDtypeStruct((tri_dev, 128), F32),
        ],
        compiler_params=PARAMS,
        cost_estimate=cost(1),
    )(labels, values, *after)


def apply_kernel(mats, fed, count, *refs):
    matrices, pieces, outs = refs[:mats], refs[mats : mats + fed], refs[-count:]
    block = pieces[0].shape[0]
    half = pieces[0].shape[1] // 2
    sums = []
    for matrix in matrices:
        total = None
        for k, piece in enumerate(pieces):
            term = matmul(matrix[:, k * block : (k + 1) * block], piece[...])
            total = term if total is None else total + term
        sums.append(total)
    value = sums[0]
    if mats == 2:
        real, imag = sums
        value = jnp.concatenate(
            [real[:, :half] - imag[:, half:], real[:, half:] + imag[:, :half]], axis=1
        )
    for k, out in enumerate(outs):

        @pl.when(pl.program_id(0) == k)
        def _(out=out):
            out[...] = value.astype(out.dtype)


def apply(matrices, pieces, count, after=()):
    rows, cols = matrices[0].shape
    block = rows // count
    size, width = pieces[0].shape
    return pl.pallas_call(
        functools.partial(apply_kernel, len(matrices), len(pieces), count),
        grid=(count,),
        in_specs=[pl.BlockSpec((block, cols), lambda j: (j, 0))] * len(matrices)
        + [pl.BlockSpec((size, width), lambda j: (0, 0))] * len(pieces)
        + [anywhere()] * len(after),
        out_specs=[pl.BlockSpec((block, width), lambda j: (0, 0))] * count,
        out_shape=[
            jax.ShapeDtypeStruct((block, width), F32 if k == 0 else BF16) for k in range(count)
        ],
        compiler_params=PARAMS,
        cost_estimate=cost(2 * len(matrices)),
    )(*matrices, *pieces, *after)


def total_of(layout, blocks):
    total = blocks[0]
    for part in layout.give(blocks[1:]):
        total = total + part.astype(F32)
    return total


def per_device(currents, incidence, centroids, sweep_weights):
    layout = Layout(lax.axis_size("row"), lax.axis_size("col"))
    devices = layout.devices
    me = lax.axis_index(AXES)
    tri_dev = centroids.shape[1]
    edge_dev, width = currents.shape
    slots = 8 * tri_dev // devices
    cells = devices * slots
    sweeps = sweep_weights.shape[0]
    count = len(layout.plane)
    cols = layout.z * layout.core * tri_dev

    outgoing, labels, numbers = route(incidence, centroids, currents, slots, devices)
    plane = layout.across(numbers)
    line = layout.line(numbers)
    labels = lax.all_to_all(labels, AXES, split_axis=0, concat_axis=0, tiled=True)
    labels = labels.reshape(1, cells)
    outgoing = tie(outgoing, labels, *plane[1:], *line[1:])
    arrived = lax.all_to_all(
        outgoing.reshape(devices, slots, width), AXES, split_axis=0, concat_axis=0, tiled=True
    ).reshape(cells, width)
    where = me.astype(I32).reshape(1)
    tiles = build_tiles(plane, line, tri_dev)
    slopes_of = build_incidence(layout, where, plane, edge_dev, tri_dev, cols)
    neighbours = build_adjacency(layout, where, layout.across(labels), tri_dev, cols)

    charge, rounded, degree = collect(
        labels, arrived, tri_dev, (*tiles, slopes_of, neighbours)
    )
    current = currents
    potential = None
    slopes = ()
    for sweep in range(sweeps):
        pieces = layout.line(rounded)
        blocks = apply(tiles, pieces, count, slopes)
        if sweep > 0:
            change = sweep_weights[sweep - 1] * total_of(layout, slopes)
            current = (current.astype(F32) - change).astype(BF16)
        potential = total_of(layout, blocks).astype(BF16)
        pieces = layout.line(potential)
        if sweep + 1 < sweeps:
            around = total_of(layout, apply([neighbours], pieces, count))
            change = degree[:, :1] * potential.astype(F32) - around
            charge = charge - sweep_weights[sweep] * change
            rounded = charge.astype(BF16)
        slopes = apply([slopes_of], pieces, count)
    change = sweep_weights[sweeps - 1] * total_of(layout, slopes)
    return (current.astype(F32) - change).astype(BF16), potential


def solution(mesh):
    in_specs = (P(AXES, None), P(None, AXES), P(None, AXES), P())
    out_specs = (P(AXES, None), P(AXES, None))
    return jax.shard_map(
        per_device, mesh=mesh, in_specs=in_specs, out_specs=out_specs, check_vma=False
    )
```

```python
import functools
import math

import jax
import jax.numpy as jnp
from jax import lax
from jax.experimental import pallas as pl
from jax.experimental.pallas import tpu as pltpu
from jax.sharding import PartitionSpec as P

SPACING = 0.2
TURNS = 32.0
AXES = ("row", "col")
ROUND = 12582912.0
COS = (
    0.9999992107823218,
    -19.738980355763992,
    64.92865742103312,
    -85.27162153429882,
    58.79049212013072,
    -21.07110562764302,
)
SIN = (
    6.283184916495431,
    -41.34158923268858,
    81.59994332978287,
    -76.61447253124996,
    41.342882354568324,
    -12.471243535026977,
)
PARAMS = pltpu.CompilerParams(vmem_limit_bytes=24 * 2**20)
PEAK = 1.15e15
F32, BF16, I32 = jnp.float32, jnp.bfloat16, jnp.int32


def whole():
    return pl.BlockSpec(memory_space=pltpu.VMEM)


def cost(microseconds):
    return pl.CostEstimate(
        flops=int(microseconds * 1e-6 * PEAK), bytes_accessed=0, transcendentals=0
    )


TOKEN = jax.ShapeDtypeStruct((8, 128), F32)


def token_spec():
    return pl.BlockSpec((8, 128), lambda *_: (0, 0))


def iota(shape, dim):
    return lax.broadcasted_iota(I32, shape, dim)


def ones_where(mask):
    return jnp.where(mask, jnp.ones((), F32), jnp.zeros((), F32)).astype(BF16)


def matmul(a, b):
    return jnp.dot(a, b, preferred_element_type=F32)


def matmul_nt(a, b):
    return lax.dot_general(a, b, (((1,), (1,)), ((), ())), preferred_element_type=F32)


class Layout:
    def __init__(self, n_row, n_col):
        self.core = 2 if n_row % 2 == 0 else 1
        self.x = n_row // self.core
        self.y = math.gcd(n_col, self.x)
        self.z = n_col // self.y
        self.devices = n_row * n_col
        self.plane = [(dx, dy) for dx in range(self.x) for dy in range(self.y)]

    def digits(self, index):
        y = index % self.y
        z = index // self.y % self.z
        core = index // (self.y * self.z) % self.core
        return index // (self.y * self.z * self.core), core, z, y

    def shift(self, value, dx=0, dc=0, dz=0, dy=0):
        pairs = []
        for i in range(self.devices):
            x, c, z, y = self.digits(i)
            x, c = (x + dx) % self.x, (c + dc) % self.core
            z, y = (z + dz) % self.z, (y + dy) % self.y
            pairs.append((i, ((x * self.core + c) * self.z + z) * self.y + y))
        return lax.ppermute(value, AXES, pairs)

    def along(self, value):
        return [value] + [self.shift(value, dz=-dz) for dz in range(1, self.z)]

    def swapped(self, values):
        pieces = []
        for value in values:
            pieces.append(value)
            pieces += [self.shift(value, dc=-dc) for dc in range(1, self.core)]
        return pieces

    def across(self, value):
        return [value] + [self.shift(value, dx=-dx, dy=-dy) for dx, dy in self.plane[1:]]

    def given(self, blocks):
        return [blocks[0]] + [
            self.shift(block, dx=dx, dy=dy)
            for block, (dx, dy) in zip(blocks[1:], self.plane[1:])
        ]

    def place(self, triangle, tri_dev, me):
        x, core, z, y = self.digits(triangle // tri_dev)
        mx, mcore, mz, my = self.digits(me)
        block = (z - mz) % self.z * self.core + (core - mcore) % self.core
        inside = (x == mx) & (y == my)
        return jnp.where(inside, block * tri_dev + triangle % tri_dev, -1)


def number_kernel(slots, inc_ref, points_ref, label_ref, slot_ref, number_ref):
    edges, tri_dev = inc_ref.shape[1], points_ref.shape[1]
    ends, devices = 2 * edges, label_ref.shape[0]
    number_ref[...] = jnp.zeros(number_ref.shape, I32)
    number_ref[0:2, :edges] = inc_ref[...]
    number_ref[2:5, :tri_dev] = points_ref[...]
    plus, minus = inc_ref[0:1, :], inc_ref[1:2, :]
    tri = jnp.concatenate([plus, minus], axis=1)
    other = jnp.concatenate([minus, plus], axis=1)
    owner = tri // tri_dev
    hits = iota((devices, ends), 0) == owner
    upper = ones_where(iota((ends, ends), 0) <= iota((ends, ends), 1))
    count = matmul(ones_where(hits), upper)
    rank = jnp.sum(jnp.where(hits, count, 0.0), axis=0, keepdims=True).astype(I32) - 1
    slot_ref[...] = owner * slots + rank
    order = ones_where(iota((slots, ends), 0) == rank)
    label = jnp.zeros((devices, slots), I32)
    digits = (
        (tri % tri_dev + 1, 1),
        (other & 255, 2 * tri_dev),
        (other >> 8, 512 * tri_dev),
    )
    for digit, weight in digits:
        spread = jnp.where(hits, digit.astype(F32), 0.0).astype(BF16)
        label = label + matmul_nt(spread, order).astype(I32) * weight
    label_ref[...] = label


def number(incidence, centroids, slots, devices):
    edges = incidence.shape[1]
    lanes = max(edges, centroids.shape[1])
    return pl.pallas_call(
        functools.partial(number_kernel, slots),
        in_specs=[whole()] * 2,
        out_specs=[whole()] * 3,
        out_shape=[
            jax.ShapeDtypeStruct((devices, slots), I32),
            jax.ShapeDtypeStruct((1, 2 * edges), I32),
            jax.ShapeDtypeStruct((8, lanes), I32),
        ],
        compiler_params=PARAMS,
        cost_estimate=cost(1),
    )(incidence, centroids)


def route_kernel(slot_ref, cur_ref, *refs):
    out_ref, token_ref = refs[-2:]
    token_ref[...] = jnp.zeros_like(token_ref)
    edges, cells = cur_ref.shape[0], out_ref.shape[0]
    chunk = min(256, cells)
    slot = slot_ref[...]
    for base in range(0, cells, chunk):
        mask = jnp.where(iota((chunk, 2 * edges), 0) + base == slot, 1.0, 0.0).astype(F32)
        signed = (mask[:, :edges] - mask[:, edges:]).astype(BF16)
        out_ref[base : base + chunk, :] = matmul(signed, cur_ref[...]).astype(BF16)


def route(slot, currents, cells, after):
    return pl.pallas_call(
        route_kernel,
        in_specs=[whole()] * (2 + len(after)),
        out_specs=[whole()] * 2,
        out_shape=[jax.ShapeDtypeStruct((cells, currents.shape[1]), BF16), TOKEN],
        compiler_params=PARAMS,
        cost_estimate=cost(1),
    )(slot, currents, *after)


def features(points, scale, first):
    rows, count = points.shape
    square = jnp.sum(points * points, axis=0, keepdims=True)
    norms = [square & 255, square & 0xFF00, square & 0xFF0000]
    ones = [jnp.ones_like(square)] * 3
    zeros = [jnp.zeros((16 - rows - 7, count), I32)]
    if first:
        parts = [-2 * points] + norms + ones + [ones[0]] + zeros
    else:
        parts = [points] + ones + norms + [ones[0]] + zeros
    return (jnp.concatenate(parts, axis=0).astype(F32) * scale).astype(BF16)


def poly(coefs, scale, u):
    value = jnp.full_like(u, coefs[-1] * scale)
    for coef in coefs[-2::-1]:
        value = value * u + coef * scale
    return value


def tile_kernel(count, block, tri_dev, *refs):
    plane, line = refs[:count], refs[count:-6]
    real_ref, imag_ref, token_ref, row_ref, col_ref = refs[-5:]
    token_ref[...] = jnp.zeros_like(token_ref)

    @pl.when(pl.program_id(0) == 0)
    def _():
        for k, ref in enumerate(plane):
            row_ref[k] = features(ref[2:5, :tri_dev], 1.0 / (TURNS * TURNS), True)
        for k, ref in enumerate(line):
            col_ref[:, k * tri_dev : (k + 1) * tri_dev] = features(ref[2:5, :tri_dev], 1.0, False)

    row = row_ref[pl.program_id(0)]
    for base in range(0, col_ref.shape[1], block):
        cols = slice(base, base + block)
        square = lax.dot_general(
            row, col_ref[:, cols], (((0,), (0,)), ((), ())), preferred_element_type=F32
        )
        inverse = lax.rsqrt(square)
        turns = square * inverse
        frac = turns - ((turns + ROUND) - ROUND)
        u = frac * frac
        real_ref[:, cols] = (poly(COS, SPACING / TURNS, u) * inverse).astype(BF16)
        imag_ref[:, cols] = (poly(SIN, -SPACING / TURNS, u) * (frac * inverse)).astype(BF16)


def build_tiles(plane, line, tri_dev, after):
    count, cols = len(plane), len(line) * tri_dev
    shape = plane[0].shape
    return pl.pallas_call(
        functools.partial(tile_kernel, count, min(512, cols), tri_dev),
        grid=(count,),
        in_specs=[pl.BlockSpec(shape, lambda i: (0, 0))] * (count + len(line)) + [token_spec()],
        out_specs=[pl.BlockSpec((tri_dev, cols), lambda i: (i, 0))] * 2 + [token_spec()],
        out_shape=[jax.ShapeDtypeStruct((count * tri_dev, cols), BF16)] * 2 + [TOKEN],
        scratch_shapes=[pltpu.VMEM((count, 16, tri_dev), BF16), pltpu.VMEM((16, cols), BF16)],
        compiler_params=PARAMS,
        cost_estimate=cost(12),
    )(*plane, *line, after)


def pick(row, base, count):
    low = jnp.where((row >= base) & (row < base + count), row - base, -1)
    wanted = iota((count, row.shape[1]), 0).astype(F32).astype(BF16)
    same = wanted == low.astype(F32).astype(BF16)
    return jnp.where(same, jnp.ones((), BF16), jnp.zeros((), BF16))


def adjacency_kernel(layout, tri_dev, me_ref, *refs):
    labels, (out_ref, token_ref) = refs[:-3], refs[-2:]
    token_ref[...] = jnp.zeros_like(token_ref)
    rows, cols = out_ref.shape
    for k, label_ref in enumerate(labels):

        @pl.when(pl.program_id(0) == k)
        def _(label_ref=label_ref):
            label = label_ref[...]
            mark = label % (2 * tri_dev) - 1
            place = layout.place(label // (2 * tri_dev), tri_dev, me_ref[0])
            place = jnp.where(mark >= 0, place, -1)
            low = pick(jnp.where(place >= 0, place % rows, -1), 0, rows)
            for base in range(0, cols, rows):
                inside = (place >= base) & (place < base + rows)
                here = pick(jnp.where(inside, mark, -1), 0, rows)
                out_ref[:, base : base + rows] = matmul_nt(here, low).astype(BF16)


def build_adjacency(layout, me, labels, rows, cols, after):
    count, shape = len(labels), labels[0].shape
    return pl.pallas_call(
        functools.partial(adjacency_kernel, layout, rows),
        grid=(count,),
        in_specs=[pl.BlockSpec(memory_space=pltpu.SMEM)]
        + [pl.BlockSpec(shape, lambda j: (0, 0))] * count
        + [token_spec()],
        out_specs=[pl.BlockSpec((rows, cols), lambda j: (j, 0)), token_spec()],
        out_shape=[jax.ShapeDtypeStruct((count * rows, cols), BF16), TOKEN],
        compiler_params=PARAMS,
        cost_estimate=cost(10),
    )(me, *labels, after)


def incidence_kernel(layout, tri_dev, me_ref, *refs):
    numbers, (out_ref, token_ref) = refs[:-3], refs[-2:]
    token_ref[...] = jnp.zeros_like(token_ref)
    edges, cols = out_ref.shape
    for k, number_ref in enumerate(numbers):

        @pl.when(pl.program_id(0) == k)
        def _(number_ref=number_ref):
            places = layout.place(number_ref[0:2, :edges], tri_dev, me_ref[0])
            plus, minus = places[0:1], places[1:2]
            eye = ones_where(iota((edges, edges), 0) == iota((edges, edges), 1))
            for base in range(0, cols, tri_dev):
                signed = pick(plus, base, tri_dev) - pick(minus, base, tri_dev)
                out_ref[:, base : base + tri_dev] = matmul_nt(eye, signed).astype(BF16)


def build_incidence(layout, me, numbers, edges, tri_dev, cols, after):
    count, shape = len(numbers), numbers[0].shape
    return pl.pallas_call(
        functools.partial(incidence_kernel, layout, tri_dev),
        grid=(count,),
        in_specs=[pl.BlockSpec(memory_space=pltpu.SMEM)]
        + [pl.BlockSpec(shape, lambda j: (0, 0))] * count
        + [token_spec()],
        out_specs=[pl.BlockSpec((edges, cols), lambda j: (j, 0)), token_spec()],
        out_shape=[jax.ShapeDtypeStruct((count * edges, cols), BF16), TOKEN],
        compiler_params=PARAMS,
        cost_estimate=cost(6),
    )(me, *numbers, after)


def collect_kernel(tri_dev, label_ref, value_ref, *refs):
    charge_ref, rounded_ref, degree_ref = refs[-3:]
    here = pick(label_ref[...] % (2 * tri_dev) - 1, 0, tri_dev)
    charge = matmul(here, value_ref[...])
    charge_ref[...] = charge
    rounded_ref[...] = charge.astype(BF16)
    degree_ref[...] = matmul(here, jnp.ones((here.shape[1], degree_ref.shape[1]), BF16))


def collect(labels, values, tri_dev, after):
    width = values.shape[1]
    return pl.pallas_call(
        functools.partial(collect_kernel, tri_dev),
        in_specs=[whole()] * (2 + len(after)),
        out_specs=[whole()] * 3,
        out_shape=[
            jax.ShapeDtypeStruct((tri_dev, width), F32),
            jax.ShapeDtypeStruct((tri_dev, width), BF16),
            jax.ShapeDtypeStruct((tri_dev, 128), F32),
        ],
        compiler_params=PARAMS,
        cost_estimate=cost(1),
    )(labels, values, *after)


def apply_kernel(mats, fed, count, *refs):
    matrices, pieces, outs = refs[:mats], refs[mats : mats + fed], refs[-count - 1 : -1]
    refs[-1][...] = jnp.zeros_like(refs[-1])
    block = pieces[0].shape[0]
    half = pieces[0].shape[1] // 2
    sums = []
    for matrix in matrices:
        total = None
        for k, piece in enumerate(pieces):
            term = matmul(matrix[:, k * block : (k + 1) * block], piece[...])
            total = term if total is None else total + term
        sums.append(total)
    value = sums[0]
    if mats == 2:
        real, imag = sums
        value = jnp.concatenate(
            [real[:, :half] - imag[:, half:], real[:, half:] + imag[:, :half]], axis=1
        )
    for k, out in enumerate(outs):

        @pl.when(pl.program_id(0) == k)
        def _(out=out):
            out[...] = value.astype(out.dtype)


def apply(matrices, pieces, count, after=()):
    rows, cols = matrices[0].shape
    block = rows // count
    size, width = pieces[0].shape
    return pl.pallas_call(
        functools.partial(apply_kernel, len(matrices), len(pieces), count),
        grid=(count,),
        in_specs=[pl.BlockSpec((block, cols), lambda j: (j, 0))] * len(matrices)
        + [pl.BlockSpec((size, width), lambda j: (0, 0))] * len(pieces)
        + [token_spec()] * len(after),
        out_specs=[pl.BlockSpec((block, width), lambda j: (0, 0))] * count + [token_spec()],
        out_shape=[
            jax.ShapeDtypeStruct((block, width), F32 if k == 0 else BF16) for k in range(count)
        ]
        + [TOKEN],
        compiler_params=PARAMS,
        cost_estimate=cost(2 * len(matrices)),
    )(*matrices, *pieces, *after)


def potential_kernel(count, own_ref, *refs):
    total = own_ref[...]
    for ref in refs[:count]:
        total = total + ref[...].astype(F32)
    refs[-1][...] = total.astype(BF16)


def potential_of(blocks, after):
    got = blocks[1:]
    return pl.pallas_call(
        functools.partial(potential_kernel, len(got)),
        in_specs=[whole()] * (len(blocks) + len(after)),
        out_specs=whole(),
        out_shape=jax.ShapeDtypeStruct(blocks[0].shape, BF16),
        compiler_params=PARAMS,
        cost_estimate=cost(1),
    )(*blocks, *after)


def charge_kernel(count, weight_ref, charge_ref, degree_ref, potential_ref, own_ref, *refs):
    around = own_ref[...]
    for ref in refs[:count]:
        around = around + ref[...].astype(F32)
    out_ref, rounded_ref = refs[-2:]
    change = degree_ref[:, 0:1] * potential_ref[...].astype(F32) - around
    value = charge_ref[...] - weight_ref[0] * change
    out_ref[...] = value
    rounded_ref[...] = value.astype(BF16)


def charge_of(weight, charge, degree, potential, blocks):
    return pl.pallas_call(
        functools.partial(charge_kernel, len(blocks) - 1),
        in_specs=[pl.BlockSpec(memory_space=pltpu.SMEM)] + [whole()] * (3 + len(blocks)),
        out_specs=[whole()] * 2,
        out_shape=[
            jax.ShapeDtypeStruct(charge.shape, F32),
            jax.ShapeDtypeStruct(charge.shape, BF16),
        ],
        compiler_params=PARAMS,
        cost_estimate=cost(1),
    )(weight, charge, degree, potential, *blocks)


def current_kernel(count, weight_ref, current_ref, own_ref, *refs):
    slope = own_ref[...]
    for ref in refs[:count]:
        slope = slope + ref[...].astype(F32)
    out_ref, token_ref = refs[-2:]
    out_ref[...] = (current_ref[...].astype(F32) - weight_ref[0] * slope).astype(BF16)
    token_ref[...] = jnp.zeros_like(token_ref)


def current_of(weight, current, blocks):
    return pl.pallas_call(
        functools.partial(current_kernel, len(blocks) - 1),
        in_specs=[pl.BlockSpec(memory_space=pltpu.SMEM)] + [whole()] * (1 + len(blocks)),
        out_specs=[whole()] * 2,
        out_shape=[jax.ShapeDtypeStruct(current.shape, BF16), TOKEN],
        compiler_params=PARAMS,
        cost_estimate=cost(1),
    )(weight, current, *blocks)


def per_device(currents, incidence, centroids, sweep_weights):
    layout = Layout(lax.axis_size("row"), lax.axis_size("col"))
    devices = layout.devices
    me = lax.axis_index(AXES)
    tri_dev = centroids.shape[1]
    edge_dev, width = currents.shape
    slots = 8 * tri_dev // devices
    cells = devices * slots
    sweeps = sweep_weights.shape[0]
    count = len(layout.plane)
    cols = layout.z * layout.core * tri_dev

    labels, slot, numbers = number(incidence, centroids, slots, devices)
    along = layout.along(numbers)
    plane = layout.across(numbers)
    outgoing, token = route(slot, currents, cells, (*along[1:], *plane[1:]))
    arrived = lax.all_to_all(
        outgoing.reshape(devices, slots, width), AXES, split_axis=0, concat_axis=0, tiled=True
    ).reshape(cells, width)
    labels = lax.all_to_all(labels, AXES, split_axis=0, concat_axis=0, tiled=True)
    labels = labels.reshape(1, cells)
    where = me.astype(I32).reshape(1)
    slopes_of, token_1 = build_incidence(layout, where, plane, edge_dev, tri_dev, cols, token)
    *tiles, token_2 = build_tiles(plane, layout.swapped(along), tri_dev, token)
    neighbours, token_3 = build_adjacency(
        layout, where, layout.across(labels), tri_dev, cols, token
    )

    charge, rounded, degree = collect(labels, arrived, tri_dev, (token_1, token_2, token_3))
    current = currents
    potential = None
    slopes, after = None, ()
    for sweep in range(sweeps):
        weight = sweep_weights[sweep].reshape(1)
        pieces = layout.swapped(layout.along(rounded))
        *blocks, _ = apply(tiles, pieces, count, after)
        after = ()
        if slopes is not None:
            current, token = current_of(last_weight, current, layout.given(slopes))
            after = (token,)
        potential = potential_of(layout.given(blocks), after)
        pieces = layout.swapped(layout.along(potential))
        if sweep + 1 < sweeps:
            *blocks, _ = apply([neighbours], pieces, count)
            charge, rounded = charge_of(
                weight, charge, degree, potential, layout.given(blocks)
            )
        *slopes, token = apply([slopes_of], pieces, count)
        after, last_weight = (token,), weight
    current, _ = current_of(last_weight, current, layout.given(slopes))
    return current, potential


def solution(mesh):
    in_specs = (P(AXES, None), P(None, AXES), P(None, AXES), P())
    out_specs = (P(AXES, None), P(AXES, None))
    return jax.shard_map(
        per_device, mesh=mesh, in_specs=in_specs, out_specs=out_specs, check_vma=False
    )
```

```python
import functools
import math

import jax
import jax.numpy as jnp
from jax import lax
from jax.experimental import pallas as pl
from jax.experimental.pallas import tpu as pltpu
from jax.sharding import PartitionSpec as P

SPACING = 0.2
TURNS = 32.0
AXES = ("row", "col")
ROUND = 12582912.0
COS = (
    0.9999992107823218,
    -19.738980355763992,
    64.92865742103312,
    -85.27162153429882,
    58.79049212013072,
    -21.07110562764302,
)
SIN = (
    6.283184916495431,
    -41.34158923268858,
    81.59994332978287,
    -76.61447253124996,
    41.342882354568324,
    -12.471243535026977,
)
PARAMS = pltpu.CompilerParams(vmem_limit_bytes=24 * 2**20)
PEAK = 1.15e15
F32, BF16, I32 = jnp.float32, jnp.bfloat16, jnp.int32


def whole():
    return pl.BlockSpec(memory_space=pltpu.VMEM)


def cost(microseconds):
    return pl.CostEstimate(
        flops=int(microseconds * 1e-6 * PEAK), bytes_accessed=0, transcendentals=0
    )


TOKEN = jax.ShapeDtypeStruct((8, 128), F32)


def token_spec():
    return pl.BlockSpec((8, 128), lambda *_: (0, 0))


def iota(shape, dim):
    return lax.broadcasted_iota(I32, shape, dim)


def ones_where(mask):
    return jnp.where(mask, jnp.ones((), F32), jnp.zeros((), F32)).astype(BF16)


def matmul(a, b):
    return jnp.dot(a, b, preferred_element_type=F32)


def matmul_nt(a, b):
    return lax.dot_general(a, b, (((1,), (1,)), ((), ())), preferred_element_type=F32)


class Layout:
    def __init__(self, n_row, n_col):
        self.core = 2 if n_row % 2 == 0 else 1
        self.x = n_row // self.core
        self.y = math.gcd(n_col, self.x)
        self.z = n_col // self.y
        self.devices = n_row * n_col
        self.plane = [(dx, dy) for dx in range(self.x) for dy in range(self.y)]

    def digits(self, index):
        y = index % self.y
        z = index // self.y % self.z
        core = index // (self.y * self.z) % self.core
        return index // (self.y * self.z * self.core), core, z, y

    def shift(self, value, dx=0, dc=0, dz=0, dy=0):
        pairs = []
        for i in range(self.devices):
            pairs.append((i, self.near(i, dx, dc, dz, dy)))
        return lax.ppermute(value, AXES, pairs)

    def along(self, value):
        return [value] + [self.shift(value, dz=-dz) for dz in range(1, self.z)]

    def swapped(self, values):
        pieces = []
        for value in values:
            pieces.append(value)
            pieces += [self.shift(value, dc=-dc) for dc in range(1, self.core)]
        return pieces

    def index(self, x, core, z, y):
        x, core, z, y = x % self.x, core % self.core, z % self.z, y % self.y
        return ((x * self.core + core) * self.z + z) * self.y + y

    def near(self, me, dx=0, dc=0, dz=0, dy=0):
        x, core, z, y = self.digits(me)
        return self.index(x + dx, core + dc, z + dz, y + dy)

    def spot(self, me, step):
        x, _, _, y = self.digits(me)
        return (x + step // self.y) % self.x * self.y + (y + step % self.y) % self.y

    def given(self, blocks):
        return [blocks[0]] + [
            self.shift(block, dx=dx, dy=dy)
            for block, (dx, dy) in zip(blocks[1:], self.plane[1:])
        ]

    def place(self, triangle, tri_dev, me):
        x, core, z, y = self.digits(triangle // tri_dev)
        mx, mcore, mz, my = self.digits(me)
        block = (z - mz) % self.z * self.core + (core - mcore) % self.core
        inside = (x == mx) & (y == my)
        return jnp.where(inside, block * tri_dev + triangle % tri_dev, -1)


class Letter:
    def __init__(self, edges, tri_dev, labels):
        self.edges, self.tri_dev, self.half = edges, tri_dev, -(-tri_dev // 2)
        sizes = [edges, tri_dev, self.half, labels]
        starts = [0]
        for size in sizes:
            starts.append(starts[-1] + -(-size // 128))
        self.starts, self.rows = starts[:4], -(-starts[4] // 8) * 8

    def take(self, letter, part, size):
        first = self.starts[part]
        parts = [letter[first + k : first + k + 1, :] for k in range(-(-size // 128))]
        return jnp.concatenate(parts, axis=1)[:, :size]

    def ends(self, letter):
        pair = self.take(letter, 0, self.edges)
        return pair & 0xFFFF, lax.shift_right_logical(pair, 16)

    def points(self, letter):
        first = self.take(letter, 1, self.tri_dev)
        third = self.take(letter, 2, self.half)
        third = jnp.concatenate([third & 0xFFFF, lax.shift_right_logical(third, 16)], axis=1)
        return jnp.concatenate(
            [first & 0xFFFF, lax.shift_right_logical(first, 16), third[:, : self.tri_dev]], axis=0
        )


def in_rows(row):
    size = row.shape[1]
    if size % 128:
        row = jnp.concatenate([row, jnp.zeros((1, -size % 128), I32)], axis=1)
    return [row[:, k : k + 128] for k in range(0, row.shape[1], 128)]


def letter_kernel(layout, form, slots, inc_ref, points_ref, letter_ref, slot_ref):
    edges, tri_dev, half = form.edges, form.tri_dev, form.half
    ends, devices = 2 * edges, layout.devices
    plus, minus = inc_ref[0:1, :], inc_ref[1:2, :]
    tri = jnp.concatenate([plus, minus], axis=1)
    other = jnp.concatenate([minus, plus], axis=1)
    owner = tri // tri_dev
    hits = iota((devices, ends), 0) == owner
    upper = ones_where(iota((ends, ends), 0) <= iota((ends, ends), 1))
    count = matmul(ones_where(hits), upper)
    rank = jnp.sum(jnp.where(hits, count, 0.0), axis=0, keepdims=True).astype(I32) - 1
    slot_ref[...] = owner * slots + rank
    order = ones_where(iota((slots, ends), 0) == rank)
    label = jnp.zeros((devices, slots), I32)
    digits = ((tri % tri_dev + 1, 1), (other & 255, 65536), (other >> 8, 65536 * 256))
    for digit, weight in digits:
        spread = jnp.where(hits, digit.astype(F32), 0.0).astype(BF16)
        label = label + matmul_nt(spread, order).astype(I32) * weight
    third = points_ref[2:3, :]
    if tri_dev % 2:
        third = jnp.concatenate([third, jnp.zeros((1, 1), I32)], axis=1)
    common = (
        in_rows(plus + (minus << 16))
        + in_rows(points_ref[0:1, :] + (points_ref[1:2, :] << 16))
        + in_rows(third[:, :half] + (third[:, half:] << 16))
    )
    places = [(x, y) for x in range(layout.x) for y in range(layout.y)]
    for core in range(layout.core):
        for z in range(layout.z):
            there = [layout.index(x, core, z, y) for x, y in places]
            mine = in_rows(jnp.concatenate([label[d : d + 1, :] for d in there], axis=1))
            blank = form.rows - len(common) - len(mine)
            rows = common + mine + [jnp.zeros((1, 128), I32)] * blank
            letter = jnp.concatenate(rows, axis=0)
            for d in there:
                letter_ref[d] = letter


def letters_of(layout, form, incidence, centroids, slots):
    return pl.pallas_call(
        functools.partial(letter_kernel, layout, form, slots),
        in_specs=[whole()] * 2,
        out_specs=[whole()] * 2,
        out_shape=[
            jax.ShapeDtypeStruct((layout.devices, form.rows, 128), I32),
            jax.ShapeDtypeStruct((1, 2 * form.edges), I32),
        ],
        compiler_params=PARAMS,
        cost_estimate=cost(1),
    )(incidence, centroids)


def route_kernel(slot_ref, cur_ref, *refs):
    out_ref, token_ref = refs[-2:]
    token_ref[...] = jnp.zeros_like(token_ref)
    edges, cells = cur_ref.shape[0], out_ref.shape[0]
    chunk = min(256, cells)
    slot = slot_ref[...]
    for base in range(0, cells, chunk):
        mask = jnp.where(iota((chunk, 2 * edges), 0) + base == slot, 1.0, 0.0).astype(F32)
        signed = (mask[:, :edges] - mask[:, edges:]).astype(BF16)
        out_ref[base : base + chunk, :] = matmul(signed, cur_ref[...]).astype(BF16)


def route(slot, currents, cells, after):
    return pl.pallas_call(
        route_kernel,
        in_specs=[whole()] * (2 + len(after)),
        out_specs=[whole()] * 2,
        out_shape=[jax.ShapeDtypeStruct((cells, currents.shape[1]), BF16), TOKEN],
        compiler_params=PARAMS,
        cost_estimate=cost(1),
    )(slot, currents, *after)


def features(points, scale, first):
    rows, count = points.shape
    square = jnp.sum(points * points, axis=0, keepdims=True)
    norms = [square & 255, square & 0xFF00, square & 0xFF0000]
    ones = [jnp.ones_like(square)] * 3
    zeros = [jnp.zeros((16 - rows - 7, count), I32)]
    if first:
        parts = [-2 * points] + norms + ones + [ones[0]] + zeros
    else:
        parts = [points] + ones + norms + [ones[0]] + zeros
    return (jnp.concatenate(parts, axis=0).astype(F32) * scale).astype(BF16)


def poly(coefs, scale, u):
    value = jnp.full_like(u, coefs[-1] * scale)
    for coef in coefs[-2::-1]:
        value = value * u + coef * scale
    return value


def tile_kernel(layout, form, block, me_ref, letter_ref, after_ref, *refs):
    real_ref, imag_ref, token_ref, col_ref = refs
    token_ref[...] = jnp.zeros_like(token_ref)
    me, step, size = me_ref[0], pl.program_id(0), form.tri_dev

    @pl.when(step == 0)
    def _():
        for k in range(layout.z * layout.core):
            letter = letter_ref[layout.near(me, dz=k // layout.core, dc=k % layout.core)]
            col_ref[:, k * size : (k + 1) * size] = features(form.points(letter), 1.0, False)

    letter = letter_ref[layout.near(me, dx=step // layout.y, dy=step % layout.y)]
    row = features(form.points(letter), 1.0 / (TURNS * TURNS), True)
    for base in range(0, col_ref.shape[1], block):
        cols = slice(base, base + block)
        square = lax.dot_general(
            row, col_ref[:, cols], (((0,), (0,)), ((), ())), preferred_element_type=F32
        )
        inverse = lax.rsqrt(square)
        turns = square * inverse
        frac = turns - ((turns + ROUND) - ROUND)
        u = frac * frac
        real_ref[:, cols] = (poly(COS, SPACING / TURNS, u) * inverse).astype(BF16)
        imag_ref[:, cols] = (poly(SIN, -SPACING / TURNS, u) * (frac * inverse)).astype(BF16)


def fixed(array):
    return pl.BlockSpec(array.shape, lambda j: (0,) * array.ndim)


def build(kernel, outs, rows, layout, cols, me, arrays, time, scratch=()):
    count = len(layout.plane)
    return pl.pallas_call(
        kernel,
        grid=(count,),
        in_specs=[pl.BlockSpec(memory_space=pltpu.SMEM)] + [fixed(array) for array in arrays],
        out_specs=[pl.BlockSpec((rows, cols), lambda j: (j, 0))] * outs + [token_spec()],
        out_shape=[pltpu.HBM((count * rows, cols), BF16)] * outs + [TOKEN],
        scratch_shapes=scratch,
        compiler_params=PARAMS,
        cost_estimate=cost(time),
    )(me, *arrays)


def pick(row, base, count):
    low = jnp.where((row >= base) & (row < base + count), row - base, -1)
    wanted = iota((count, row.shape[1]), 0).astype(F32).astype(BF16)
    same = wanted == low.astype(F32).astype(BF16)
    return jnp.where(same, jnp.ones((), BF16), jnp.zeros((), BF16))


def adjacency_kernel(layout, tri_dev, me_ref, label_ref, after_ref, out_ref, token_ref):
    token_ref[...] = jnp.zeros_like(token_ref)
    me = me_ref[0]
    rows, cols = out_ref.shape
    label = label_ref[layout.spot(me, pl.program_id(0))]
    mark = (label & 0xFFFF) - 1
    place = layout.place(lax.shift_right_logical(label, 16), tri_dev, me)
    place = jnp.where(mark >= 0, place, -1)
    low = pick(jnp.where(place >= 0, place % rows, -1), 0, rows)
    for base in range(0, cols, rows):
        inside = (place >= base) & (place < base + rows)
        here = pick(jnp.where(inside, mark, -1), 0, rows)
        out_ref[:, base : base + rows] = matmul_nt(here, low).astype(BF16)


def incidence_kernel(layout, form, me_ref, letter_ref, after_ref, out_ref, token_ref):
    token_ref[...] = jnp.zeros_like(token_ref)
    me, step = me_ref[0], pl.program_id(0)
    edges, cols = out_ref.shape
    size = form.tri_dev
    letter = letter_ref[layout.near(me, dx=step // layout.y, dy=step % layout.y)]
    plus, minus = [layout.place(end, size, me) for end in form.ends(letter)]
    eye = ones_where(iota((edges, edges), 0) == iota((edges, edges), 1))
    for base in range(0, cols, size):
        signed = pick(plus, base, size) - pick(minus, base, size)
        out_ref[:, base : base + size] = matmul_nt(eye, signed).astype(BF16)


def collect_kernel(layout, tri_dev, me_ref, label_ref, value_ref, *refs):
    charge_ref, rounded_ref, degree_ref = refs[-3:]
    here = pick((label_ref[layout.spot(me_ref[0], 0)] & 0xFFFF) - 1, 0, tri_dev)
    charge = matmul(here, value_ref[...])
    charge_ref[...] = charge
    rounded_ref[...] = charge.astype(BF16)
    degree_ref[...] = matmul(here, jnp.ones((here.shape[1], degree_ref.shape[1]), BF16))


def collect(layout, me, labels, values, tri_dev, after):
    width = values.shape[1]
    return pl.pallas_call(
        functools.partial(collect_kernel, layout, tri_dev),
        in_specs=[pl.BlockSpec(memory_space=pltpu.SMEM)] + [whole()] * (2 + len(after)),
        out_specs=[whole()] * 3,
        out_shape=[
            jax.ShapeDtypeStruct((tri_dev, width), F32),
            jax.ShapeDtypeStruct((tri_dev, width), BF16),
            jax.ShapeDtypeStruct((tri_dev, 128), F32),
        ],
        compiler_params=PARAMS,
        cost_estimate=cost(1),
    )(me, labels, values, *after)


def apply_kernel(mats, fed, count, *refs):
    matrices, pieces, outs = refs[:mats], refs[mats : mats + fed], refs[-count - 1 : -1]
    refs[-1][...] = jnp.zeros_like(refs[-1])
    block = pieces[0].shape[0]
    half = pieces[0].shape[1] // 2
    sums = []
    for matrix in matrices:
        total = None
        for k, piece in enumerate(pieces):
            term = matmul(matrix[:, k * block : (k + 1) * block], piece[...])
            total = term if total is None else total + term
        sums.append(total)
    value = sums[0]
    if mats == 2:
        real, imag = sums
        value = jnp.concatenate(
            [real[:, :half] - imag[:, half:], real[:, half:] + imag[:, :half]], axis=1
        )
    for k, out in enumerate(outs):

        @pl.when(pl.program_id(0) == k)
        def _(out=out):
            out[...] = value.astype(out.dtype)


def apply(matrices, pieces, count, after=()):
    rows, cols = matrices[0].shape
    block = rows // count
    size, width = pieces[0].shape
    return pl.pallas_call(
        functools.partial(apply_kernel, len(matrices), len(pieces), count),
        grid=(count,),
        in_specs=[pl.BlockSpec((block, cols), lambda j: (j, 0))] * len(matrices)
        + [pl.BlockSpec((size, width), lambda j: (0, 0))] * len(pieces)
        + [token_spec()] * len(after),
        out_specs=[pl.BlockSpec((block, width), lambda j: (0, 0))] * count + [token_spec()],
        out_shape=[
            jax.ShapeDtypeStruct((block, width), F32 if k == 0 else BF16) for k in range(count)
        ]
        + [TOKEN],
        compiler_params=PARAMS,
        cost_estimate=cost(2 * len(matrices)),
    )(*matrices, *pieces, *after)


def potential_kernel(count, own_ref, *refs):
    total = own_ref[...]
    for ref in refs[:count]:
        total = total + ref[...].astype(F32)
    refs[-1][...] = total.astype(BF16)


def potential_of(blocks, after):
    got = blocks[1:]
    return pl.pallas_call(
        functools.partial(potential_kernel, len(got)),
        in_specs=[whole()] * (len(blocks) + len(after)),
        out_specs=whole(),
        out_shape=jax.ShapeDtypeStruct(blocks[0].shape, BF16),
        compiler_params=PARAMS,
        cost_estimate=cost(1),
    )(*blocks, *after)


def charge_kernel(count, weight_ref, charge_ref, degree_ref, potential_ref, own_ref, *refs):
    around = own_ref[...]
    for ref in refs[:count]:
        around = around + ref[...].astype(F32)
    out_ref, rounded_ref = refs[-2:]
    change = degree_ref[:, 0:1] * potential_ref[...].astype(F32) - around
    value = charge_ref[...] - weight_ref[0] * change
    out_ref[...] = value
    rounded_ref[...] = value.astype(BF16)


def charge_of(weight, charge, degree, potential, blocks):
    return pl.pallas_call(
        functools.partial(charge_kernel, len(blocks) - 1),
        in_specs=[pl.BlockSpec(memory_space=pltpu.SMEM)] + [whole()] * (3 + len(blocks)),
        out_specs=[whole()] * 2,
        out_shape=[
            jax.ShapeDtypeStruct(charge.shape, F32),
            jax.ShapeDtypeStruct(charge.shape, BF16),
        ],
        compiler_params=PARAMS,
        cost_estimate=cost(1),
    )(weight, charge, degree, potential, *blocks)


def current_kernel(count, weight_ref, current_ref, own_ref, *refs):
    slope = own_ref[...]
    for ref in refs[:count]:
        slope = slope + ref[...].astype(F32)
    out_ref, token_ref = refs[-2:]
    out_ref[...] = (current_ref[...].astype(F32) - weight_ref[0] * slope).astype(BF16)
    token_ref[...] = jnp.zeros_like(token_ref)


def current_of(weight, current, blocks):
    return pl.pallas_call(
        functools.partial(current_kernel, len(blocks) - 1),
        in_specs=[pl.BlockSpec(memory_space=pltpu.SMEM)] + [whole()] * (1 + len(blocks)),
        out_specs=[whole()] * 2,
        out_shape=[jax.ShapeDtypeStruct(current.shape, BF16), TOKEN],
        compiler_params=PARAMS,
        cost_estimate=cost(1),
    )(weight, current, *blocks)


def per_device(currents, incidence, centroids, sweep_weights):
    layout = Layout(lax.axis_size("row"), lax.axis_size("col"))
    devices = layout.devices
    me = lax.axis_index(AXES)
    tri_dev = centroids.shape[1]
    edge_dev, width = currents.shape
    slots = 8 * tri_dev // devices
    cells = devices * slots
    sweeps = sweep_weights.shape[0]
    count = len(layout.plane)
    cols = layout.z * layout.core * tri_dev

    form = Letter(edge_dev, tri_dev, count * slots)
    letters, slot = letters_of(layout, form, incidence, centroids, slots)
    letters = lax.all_to_all(letters, AXES, split_axis=0, concat_axis=0, tiled=True)
    outgoing, token = route(slot, currents, cells, (letters,))
    arrived = lax.all_to_all(
        outgoing.reshape(devices, slots, width), AXES, split_axis=0, concat_axis=0, tiled=True
    ).reshape(cells, width)
    labels = letters[:, form.starts[3] :, :].reshape(devices, -1)[:, : count * slots]
    labels = labels.reshape(devices, count, slots).transpose(1, 0, 2).reshape(count, 1, cells)
    where = me.astype(I32).reshape(1)
    make = functools.partial(build, layout=layout, cols=cols, me=where)
    *tiles, token_1 = make(
        functools.partial(tile_kernel, layout, form, min(512, cols)),
        2,
        tri_dev,
        arrays=(letters, token),
        time=12,
        scratch=[pltpu.VMEM((16, cols), BF16)],
    )
    slopes_of, token_2 = make(
        functools.partial(incidence_kernel, layout, form),
        1,
        edge_dev,
        arrays=(letters, token),
        time=6,
    )
    neighbours, token_3 = make(
        functools.partial(adjacency_kernel, layout, tri_dev),
        1,
        tri_dev,
        arrays=(labels, token),
        time=10,
    )
    charge, rounded, degree = collect(
        layout, where, labels, arrived, tri_dev, (token_1, token_2, token_3)
    )
    current = currents
    potential = None
    slopes, after = None, ()
    for sweep in range(sweeps):
        weight = sweep_weights[sweep].reshape(1)
        pieces = layout.swapped(layout.along(rounded))
        *blocks, _ = apply(tiles, pieces, count, after)
        after = ()
        if slopes is not None:
            current, token = current_of(last_weight, current, layout.given(slopes))
            after = (token,)
        potential = potential_of(layout.given(blocks), after)
        pieces = layout.swapped(layout.along(potential))
        if sweep + 1 < sweeps:
            *blocks, _ = apply([neighbours], pieces, count)
            charge, rounded = charge_of(
                weight, charge, degree, potential, layout.given(blocks)
            )
        *slopes, token = apply([slopes_of], pieces, count)
        after, last_weight = (token,), weight
    current, _ = current_of(last_weight, current, layout.given(slopes))
    return current, potential


def solution(mesh):
    in_specs = (P(AXES, None), P(None, AXES), P(None, AXES), P())
    out_specs = (P(AXES, None), P(AXES, None))
    return jax.shard_map(
        per_device, mesh=mesh, in_specs=in_specs, out_specs=out_specs, check_vma=False
    )
```

```python
import functools
import math

import jax
import jax.numpy as jnp
from jax import lax
from jax.experimental import pallas as pl
from jax.experimental.pallas import tpu as pltpu
from jax.sharding import PartitionSpec as P

SPACING = 0.2
TURNS = 32.0
AXES = ("x", "core", "z", "y")
ROUND = 12582912.0
COS = (
    0.9999992107823218,
    -19.738980355763992,
    64.92865742103312,
    -85.27162153429882,
    58.79049212013072,
    -21.07110562764302,
)
SIN = (
    6.283184916495431,
    -41.34158923268858,
    81.59994332978287,
    -76.61447253124996,
    41.342882354568324,
    -12.471243535026977,
)
PARAMS = pltpu.CompilerParams(vmem_limit_bytes=24 * 2**20)
PEAK = 1.15e15
F32, BF16, I32 = jnp.float32, jnp.bfloat16, jnp.int32


def whole():
    return pl.BlockSpec(memory_space=pltpu.VMEM)


def cost(microseconds):
    return pl.CostEstimate(
        flops=int(microseconds * 1e-6 * PEAK), bytes_accessed=0, transcendentals=0
    )


TOKEN = jax.ShapeDtypeStruct((8, 128), F32)


def token_spec():
    return pl.BlockSpec((8, 128), lambda *_: (0, 0))


def iota(shape, dim):
    return lax.broadcasted_iota(I32, shape, dim)


def ones_where(mask):
    return jnp.where(mask, jnp.ones((), F32), jnp.zeros((), F32)).astype(BF16)


def matmul(a, b):
    return jnp.dot(a, b, preferred_element_type=F32)


def matmul_nt(a, b):
    return lax.dot_general(a, b, (((1,), (1,)), ((), ())), preferred_element_type=F32)


class Layout:
    def __init__(self, n_row, n_col):
        self.core = 2 if n_row % 2 == 0 else 1
        self.x = n_row // self.core
        self.y = math.gcd(n_col, self.x)
        self.z = n_col // self.y
        self.devices = n_row * n_col
        self.plane = self.x * self.y
        self.line = self.core * self.z

    def mesh(self, devices):
        return jax.sharding.Mesh(devices.reshape(self.x, self.core, self.z, self.y), AXES)

    def digits(self, index):
        y = index % self.y
        z = index // self.y % self.z
        core = index // (self.y * self.z) % self.core
        return index // (self.y * self.z * self.core), core, z, y

    def shift(self, value, dx=0, dc=0, dz=0, dy=0):
        pairs = []
        for i in range(self.devices):
            pairs.append((i, self.near(i, dx, dc, dz, dy)))
        return lax.ppermute(value, AXES, pairs)

    def gathered(self, value):
        along = lax.all_gather(value, "z", axis=0, tiled=True)
        return [along] + [self.shift(along, dc=-dc) for dc in range(1, self.core)]

    def index(self, x, core, z, y):
        x, core, z, y = x % self.x, core % self.core, z % self.z, y % self.y
        return ((x * self.core + core) * self.z + z) * self.y + y

    def near(self, me, dx=0, dc=0, dz=0, dy=0):
        x, core, z, y = self.digits(me)
        return self.index(x + dx, core + dc, z + dz, y + dy)

    def in_line(self, me, k):
        x, core, _, y = self.digits(me)
        return self.index(x, core + k // self.z, k % self.z, y)

    def in_plane(self, me, k):
        _, core, z, _ = self.digits(me)
        return self.index(k // self.y, core, z, k % self.y)

    def spot(self, me):
        x, _, _, y = self.digits(me)
        return x * self.y + y

    def place(self, triangle, tri_dev, me):
        x, core, z, y = self.digits(triangle // tri_dev)
        mx, mcore, _, my = self.digits(me)
        block = (core - mcore) % self.core * self.z + z
        inside = (x == mx) & (y == my)
        return jnp.where(inside, block * tri_dev + triangle % tri_dev, -1)


class Letter:
    def __init__(self, edges, tri_dev, labels):
        self.edges, self.tri_dev, self.half = edges, tri_dev, -(-tri_dev // 2)
        sizes = [edges, tri_dev, self.half, labels]
        starts = [0]
        for size in sizes:
            starts.append(starts[-1] + -(-size // 128))
        self.starts, self.rows = starts[:4], -(-starts[4] // 8) * 8

    def take(self, letter, part, size):
        first = self.starts[part]
        parts = [letter[first + k : first + k + 1, :] for k in range(-(-size // 128))]
        return jnp.concatenate(parts, axis=1)[:, :size]

    def ends(self, letter):
        pair = self.take(letter, 0, self.edges)
        return pair & 0xFFFF, lax.shift_right_logical(pair, 16)

    def points(self, letter):
        first = self.take(letter, 1, self.tri_dev)
        third = self.take(letter, 2, self.half)
        third = jnp.concatenate([third & 0xFFFF, lax.shift_right_logical(third, 16)], axis=1)
        return jnp.concatenate(
            [first & 0xFFFF, lax.shift_right_logical(first, 16), third[:, : self.tri_dev]], axis=0
        )


def in_rows(row):
    size = row.shape[1]
    if size % 128:
        row = jnp.concatenate([row, jnp.zeros((1, -size % 128), I32)], axis=1)
    return [row[:, k : k + 128] for k in range(0, row.shape[1], 128)]


def letter_kernel(layout, form, slots, inc_ref, points_ref, letter_ref, slot_ref):
    edges, tri_dev, half = form.edges, form.tri_dev, form.half
    ends, devices = 2 * edges, layout.devices
    plus, minus = inc_ref[0:1, :], inc_ref[1:2, :]
    tri = jnp.concatenate([plus, minus], axis=1)
    other = jnp.concatenate([minus, plus], axis=1)
    owner = tri // tri_dev
    hits = iota((devices, ends), 0) == owner
    upper = ones_where(iota((ends, ends), 0) <= iota((ends, ends), 1))
    count = matmul(ones_where(hits), upper)
    rank = jnp.sum(jnp.where(hits, count, 0.0), axis=0, keepdims=True).astype(I32) - 1
    slot_ref[...] = owner * slots + rank
    order = ones_where(iota((slots, ends), 0) == rank)
    label = jnp.zeros((devices, slots), I32)
    digits = ((tri % tri_dev + 1, 1), (other & 255, 65536), (other >> 8, 65536 * 256))
    for digit, weight in digits:
        spread = jnp.where(hits, digit.astype(F32), 0.0).astype(BF16)
        label = label + matmul_nt(spread, order).astype(I32) * weight
    third = points_ref[2:3, :]
    if tri_dev % 2:
        third = jnp.concatenate([third, jnp.zeros((1, 1), I32)], axis=1)
    common = (
        in_rows(plus + (minus << 16))
        + in_rows(points_ref[0:1, :] + (points_ref[1:2, :] << 16))
        + in_rows(third[:, :half] + (third[:, half:] << 16))
    )
    places = [(x, y) for x in range(layout.x) for y in range(layout.y)]
    for core in range(layout.core):
        for z in range(layout.z):
            there = [layout.index(x, core, z, y) for x, y in places]
            mine = in_rows(jnp.concatenate([label[d : d + 1, :] for d in there], axis=1))
            blank = form.rows - len(common) - len(mine)
            rows = common + mine + [jnp.zeros((1, 128), I32)] * blank
            letter = jnp.concatenate(rows, axis=0)
            for d in there:
                letter_ref[d] = letter


def letters_of(layout, form, incidence, centroids, slots):
    return pl.pallas_call(
        functools.partial(letter_kernel, layout, form, slots),
        in_specs=[whole()] * 2,
        out_specs=[whole()] * 2,
        out_shape=[
            jax.ShapeDtypeStruct((layout.devices, form.rows, 128), I32),
            jax.ShapeDtypeStruct((1, 2 * form.edges), I32),
        ],
        compiler_params=PARAMS,
        cost_estimate=cost(1),
    )(incidence, centroids)


def route_kernel(slot_ref, cur_ref, *refs):
    out_ref, token_ref = refs[-2:]
    token_ref[...] = jnp.zeros_like(token_ref)
    edges, cells = cur_ref.shape[0], out_ref.shape[0]
    chunk = min(256, cells)
    slot = slot_ref[...]
    for base in range(0, cells, chunk):
        mask = jnp.where(iota((chunk, 2 * edges), 0) + base == slot, 1.0, 0.0).astype(F32)
        signed = (mask[:, :edges] - mask[:, edges:]).astype(BF16)
        out_ref[base : base + chunk, :] = matmul(signed, cur_ref[...]).astype(BF16)


def route(slot, currents, cells, after):
    return pl.pallas_call(
        route_kernel,
        in_specs=[whole()] * (2 + len(after)),
        out_specs=[whole()] * 2,
        out_shape=[jax.ShapeDtypeStruct((cells, currents.shape[1]), BF16), TOKEN],
        compiler_params=PARAMS,
        cost_estimate=cost(1),
    )(slot, currents, *after)


def features(points, scale, first):
    rows, count = points.shape
    square = jnp.sum(points * points, axis=0, keepdims=True)
    norms = [square & 255, square & 0xFF00, square & 0xFF0000]
    ones = [jnp.ones_like(square)] * 3
    zeros = [jnp.zeros((16 - rows - 7, count), I32)]
    if first:
        parts = [-2 * points] + norms + ones + [ones[0]] + zeros
    else:
        parts = [points] + ones + norms + [ones[0]] + zeros
    return (jnp.concatenate(parts, axis=0).astype(F32) * scale).astype(BF16)


def poly(coefs, scale, u):
    value = jnp.full_like(u, coefs[-1] * scale)
    for coef in coefs[-2::-1]:
        value = value * u + coef * scale
    return value


def tile_kernel(layout, form, block, me_ref, letter_ref, after_ref, *refs):
    real_ref, imag_ref, token_ref, col_ref = refs
    token_ref[...] = jnp.zeros_like(token_ref)
    me, step, size = me_ref[0], pl.program_id(0), form.tri_dev

    @pl.when(step == 0)
    def _():
        for k in range(layout.line):
            letter = letter_ref[layout.in_line(me, k)]
            col_ref[:, k * size : (k + 1) * size] = features(form.points(letter), 1.0, False)

    letter = letter_ref[layout.in_plane(me, step)]
    row = features(form.points(letter), 1.0 / (TURNS * TURNS), True)
    for base in range(0, col_ref.shape[1], block):
        cols = slice(base, base + block)
        square = lax.dot_general(
            row, col_ref[:, cols], (((0,), (0,)), ((), ())), preferred_element_type=F32
        )
        inverse = lax.rsqrt(square)
        turns = square * inverse
        frac = turns - ((turns + ROUND) - ROUND)
        u = frac * frac
        real_ref[:, cols] = (poly(COS, SPACING / TURNS, u) * inverse).astype(BF16)
        imag_ref[:, cols] = (poly(SIN, -SPACING / TURNS, u) * (frac * inverse)).astype(BF16)


def fixed(array):
    return pl.BlockSpec(array.shape, lambda j: (0,) * array.ndim)


def build(kernel, outs, rows, layout, cols, me, arrays, time, scratch=()):
    count = layout.plane
    return pl.pallas_call(
        kernel,
        grid=(count,),
        in_specs=[pl.BlockSpec(memory_space=pltpu.SMEM)] + [fixed(array) for array in arrays],
        out_specs=[pl.BlockSpec((rows, cols), lambda j: (j, 0))] * outs + [token_spec()],
        out_shape=[pltpu.HBM((count * rows, cols), BF16)] * outs + [TOKEN],
        scratch_shapes=scratch,
        compiler_params=PARAMS,
        cost_estimate=cost(time),
    )(me, *arrays)


def pick(row, base, count):
    low = jnp.where((row >= base) & (row < base + count), row - base, -1)
    wanted = iota((count, row.shape[1]), 0).astype(F32).astype(BF16)
    same = wanted == low.astype(F32).astype(BF16)
    return jnp.where(same, jnp.ones((), BF16), jnp.zeros((), BF16))


def adjacency_kernel(layout, tri_dev, me_ref, label_ref, after_ref, out_ref, token_ref):
    token_ref[...] = jnp.zeros_like(token_ref)
    me = me_ref[0]
    rows, cols = out_ref.shape
    label = label_ref[pl.program_id(0)]
    mark = (label & 0xFFFF) - 1
    place = layout.place(lax.shift_right_logical(label, 16), tri_dev, me)
    place = jnp.where(mark >= 0, place, -1)
    low = pick(jnp.where(place >= 0, place % rows, -1), 0, rows)
    for base in range(0, cols, rows):
        inside = (place >= base) & (place < base + rows)
        here = pick(jnp.where(inside, mark, -1), 0, rows)
        out_ref[:, base : base + rows] = matmul_nt(here, low).astype(BF16)


def incidence_kernel(layout, form, me_ref, letter_ref, after_ref, out_ref, token_ref):
    token_ref[...] = jnp.zeros_like(token_ref)
    me, step = me_ref[0], pl.program_id(0)
    edges, cols = out_ref.shape
    size = form.tri_dev
    letter = letter_ref[layout.in_plane(me, step)]
    plus, minus = [layout.place(end, size, me) for end in form.ends(letter)]
    eye = ones_where(iota((edges, edges), 0) == iota((edges, edges), 1))
    for base in range(0, cols, size):
        signed = pick(plus, base, size) - pick(minus, base, size)
        out_ref[:, base : base + size] = matmul_nt(eye, signed).astype(BF16)


def collect_kernel(layout, tri_dev, me_ref, label_ref, value_ref, *refs):
    charge_ref, rounded_ref, degree_ref, token_ref = refs[-4:]
    token_ref[...] = jnp.zeros_like(token_ref)
    here = pick((label_ref[layout.spot(me_ref[0])] & 0xFFFF) - 1, 0, tri_dev)
    charge = matmul(here, value_ref[...])
    charge_ref[...] = charge
    rounded_ref[...] = charge.astype(BF16)
    degree_ref[...] = matmul(here, jnp.ones((here.shape[1], degree_ref.shape[1]), BF16))


def collect(layout, me, labels, values, tri_dev, after):
    width = values.shape[1]
    return pl.pallas_call(
        functools.partial(collect_kernel, layout, tri_dev),
        in_specs=[pl.BlockSpec(memory_space=pltpu.SMEM)] + [whole()] * (2 + len(after)),
        out_specs=[whole()] * 4,
        out_shape=[
            jax.ShapeDtypeStruct((tri_dev, width), F32),
            jax.ShapeDtypeStruct((tri_dev, width), BF16),
            jax.ShapeDtypeStruct((tri_dev, 128), F32),
            TOKEN,
        ],
        compiler_params=PARAMS,
        cost_estimate=cost(1),
    )(me, labels, values, *after)


def apply_kernel(mats, fed, *refs):
    matrices, pieces = refs[:mats], refs[mats : mats + fed]
    out_ref, token_ref = refs[-2:]
    token_ref[...] = jnp.zeros_like(token_ref)
    block, width = pieces[0].shape
    half = width // 2
    sums = []
    for matrix in matrices:
        total = None
        for k, piece in enumerate(pieces):
            term = matmul(matrix[:, k * block : (k + 1) * block], piece[...])
            total = term if total is None else total + term
        sums.append(total)
    value = sums[0]
    if mats == 2:
        real, imag = sums
        value = jnp.concatenate(
            [real[:, :half] - imag[:, half:], real[:, half:] + imag[:, :half]], axis=1
        )
    out_ref[0] = value.astype(BF16)


def apply(matrices, pieces, count, after=()):
    rows, cols = matrices[0].shape
    block = rows // count
    size, width = pieces[0].shape
    return pl.pallas_call(
        functools.partial(apply_kernel, len(matrices), len(pieces)),
        grid=(count,),
        in_specs=[pl.BlockSpec((block, cols), lambda j: (j, 0))] * len(matrices)
        + [pl.BlockSpec((size, width), lambda j: (0, 0))] * len(pieces)
        + [token_spec()] * len(after),
        out_specs=[pl.BlockSpec((1, block, width), lambda j: (j, 0, 0)), token_spec()],
        out_shape=[jax.ShapeDtypeStruct((count, block, width), BF16), TOKEN],
        compiler_params=PARAMS,
        cost_estimate=cost(2 * len(matrices)),
    )(*matrices, *pieces, *after)


def exchange(blocks):
    return lax.all_to_all(blocks, ("x", "y"), split_axis=0, concat_axis=0, tiled=True)


def added(ref):
    total = ref[0].astype(F32)
    for k in range(1, ref.shape[0]):
        total = total + ref[k].astype(F32)
    return total


def potential_kernel(parts_ref, *refs):
    refs[-1][...] = added(parts_ref).astype(BF16)


def potential_of(parts, after):
    return pl.pallas_call(
        potential_kernel,
        in_specs=[whole()] * (1 + len(after)),
        out_specs=whole(),
        out_shape=jax.ShapeDtypeStruct(parts.shape[1:], BF16),
        compiler_params=PARAMS,
        cost_estimate=cost(1),
    )(parts, *after)


def charge_kernel(weight_ref, charge_ref, degree_ref, potential_ref, parts_ref, *refs):
    out_ref, rounded_ref = refs
    change = degree_ref[:, 0:1] * potential_ref[...].astype(F32) - added(parts_ref)
    value = charge_ref[...] - weight_ref[0] * change
    out_ref[...] = value
    rounded_ref[...] = value.astype(BF16)


def charge_of(weight, charge, degree, potential, parts):
    return pl.pallas_call(
        charge_kernel,
        in_specs=[pl.BlockSpec(memory_space=pltpu.SMEM)] + [whole()] * 4,
        out_specs=[whole()] * 2,
        out_shape=[
            jax.ShapeDtypeStruct(charge.shape, F32),
            jax.ShapeDtypeStruct(charge.shape, BF16),
        ],
        compiler_params=PARAMS,
        cost_estimate=cost(1),
    )(weight, charge, degree, potential, parts)


def current_kernel(weight_ref, current_ref, parts_ref, out_ref, token_ref):
    change = weight_ref[0] * added(parts_ref)
    out_ref[...] = (current_ref[...].astype(F32) - change).astype(BF16)
    token_ref[...] = jnp.zeros_like(token_ref)


def current_of(weight, current, parts):
    return pl.pallas_call(
        current_kernel,
        in_specs=[pl.BlockSpec(memory_space=pltpu.SMEM)] + [whole()] * 2,
        out_specs=[whole()] * 2,
        out_shape=[jax.ShapeDtypeStruct(current.shape, BF16), TOKEN],
        compiler_params=PARAMS,
        cost_estimate=cost(1),
    )(weight, current, parts)


def per_device(layout, currents, incidence, centroids, sweep_weights):
    devices = layout.devices
    me = lax.axis_index(AXES)
    tri_dev = centroids.shape[1]
    edge_dev, width = currents.shape
    slots = 8 * tri_dev // devices
    cells = devices * slots
    sweeps = sweep_weights.shape[0]
    count = layout.plane
    cols = layout.line * tri_dev

    form = Letter(edge_dev, tri_dev, count * slots)
    letters, slot = letters_of(layout, form, incidence, centroids, slots)
    letters = lax.all_to_all(letters, AXES, split_axis=0, concat_axis=0, tiled=True)
    outgoing, token = route(slot, currents, cells, (letters,))
    arrived = lax.all_to_all(
        outgoing.reshape(devices, slots, width), AXES, split_axis=0, concat_axis=0, tiled=True
    ).reshape(cells, width)
    labels = letters[:, form.starts[3] :, :].reshape(devices, -1)[:, : count * slots]
    labels = labels.reshape(devices, count, slots).transpose(1, 0, 2).reshape(count, 1, cells)
    where = me.astype(I32).reshape(1)
    make = functools.partial(build, layout=layout, cols=cols, me=where)
    *tiles, token_1 = make(
        functools.partial(tile_kernel, layout, form, min(512, cols)),
        2,
        tri_dev,
        arrays=(letters, token),
        time=12,
        scratch=[pltpu.VMEM((16, cols), BF16)],
    )
    neighbours, token_3 = make(
        functools.partial(adjacency_kernel, layout, tri_dev),
        1,
        tri_dev,
        arrays=(labels, token),
        time=10,
    )
    charge, rounded, degree, done = collect(
        layout, where, labels, arrived, tri_dev, (token_1, token_3)
    )
    slopes_of, token = make(
        functools.partial(incidence_kernel, layout, form),
        1,
        edge_dev,
        arrays=(letters, done),
        time=6,
    )
    current = currents
    potential = None
    slopes, after = None, (token,)
    for sweep in range(sweeps):
        weight = sweep_weights[sweep].reshape(1)
        pieces = layout.gathered(rounded)
        blocks, _ = apply(tiles, pieces, count, after)
        after = ()
        if slopes is not None:
            current, token = current_of(last_weight, current, exchange(slopes))
            after = (token,)
        potential = potential_of(exchange(blocks), after)
        pieces = layout.gathered(potential)
        if sweep + 1 < sweeps:
            blocks, _ = apply([neighbours], pieces, count)
            charge, rounded = charge_of(weight, charge, degree, potential, exchange(blocks))
        slopes, token = apply([slopes_of], pieces, count)
        after, last_weight = (token,), weight
    current, _ = current_of(last_weight, current, exchange(slopes))
    return current, potential


def solution(mesh):
    layout = Layout(mesh.shape["row"], mesh.shape["col"])
    in_specs = (P(AXES, None), P(None, AXES), P(None, AXES), P())
    out_specs = (P(AXES, None), P(AXES, None))
    return jax.shard_map(
        functools.partial(per_device, layout),
        mesh=layout.mesh(mesh.devices),
        in_specs=in_specs,
        out_specs=out_specs,
        check_vma=False,
    )
```

```python
import functools
import math

import jax
import jax.numpy as jnp
from jax import lax
from jax.experimental import pallas as pl
from jax.experimental.pallas import tpu as pltpu
from jax.sharding import PartitionSpec as P

SPACING = 0.2
TURNS = 32.0
AXES = ("row", "col")
ROUND = 12582912.0
COS = (
    0.9999992107823218,
    -19.738980355763992,
    64.92865742103312,
    -85.27162153429882,
    58.79049212013072,
    -21.07110562764302,
)
SIN = (
    6.283184916495431,
    -41.34158923268858,
    81.59994332978287,
    -76.61447253124996,
    41.342882354568324,
    -12.471243535026977,
)
PARAMS = pltpu.CompilerParams(vmem_limit_bytes=24 * 2**20)
PEAK = 1.15e15
F32, BF16, I32 = jnp.float32, jnp.bfloat16, jnp.int32


def whole():
    return pl.BlockSpec(memory_space=pltpu.VMEM)


def fixed(array):
    return pl.BlockSpec(array.shape, lambda j: (0,) * len(array.shape))


def cost(microseconds):
    return pl.CostEstimate(
        flops=int(microseconds * 1e-6 * PEAK), bytes_accessed=0, transcendentals=0
    )


TOKEN = jax.ShapeDtypeStruct((8, 128), F32)


def token_spec():
    return pl.BlockSpec((8, 128), lambda *_: (0, 0))


def iota(shape, dim):
    return lax.broadcasted_iota(I32, shape, dim)


def ones_where(mask):
    return jnp.where(mask, jnp.ones((), F32), jnp.zeros((), F32)).astype(BF16)


def matmul(a, b):
    return jnp.dot(a, b, preferred_element_type=F32)


def matmul_nt(a, b):
    return lax.dot_general(a, b, (((1,), (1,)), ((), ())), preferred_element_type=F32)


class Layout:
    def __init__(self, n_row, n_col):
        self.core = 2 if n_row % 2 == 0 else 1
        self.x = n_row // self.core
        self.y = math.gcd(n_col, self.x)
        self.z = n_col // self.y
        self.devices = n_row * n_col
        self.plane = [(dx, dy) for dx in range(self.x) for dy in range(self.y)]

    def digits(self, index):
        y = index % self.y
        z = index // self.y % self.z
        core = index // (self.y * self.z) % self.core
        return index // (self.y * self.z * self.core), core, z, y

    def shift(self, value, dx=0, dc=0, dz=0, dy=0):
        pairs = []
        for i in range(self.devices):
            pairs.append((i, self.near(i, dx, dc, dz, dy)))
        return lax.ppermute(value, AXES, pairs)

    def gathered(self, value, after):
        cores = range(1, self.core)
        pieces = [value] + [self.shift(value, dc=-dc) for dc in cores]
        along = [self.shift(value, dz=-dz) for dz in range(1, self.z)]
        if along:
            along = pack(along, after)
            pieces += [along] + [self.shift(along, dc=-dc) for dc in cores]
        return pieces

    def index(self, x, core, z, y):
        x, core, z, y = x % self.x, core % self.core, z % self.z, y % self.y
        return ((x * self.core + core) * self.z + z) * self.y + y

    def near(self, me, dx=0, dc=0, dz=0, dy=0):
        x, core, z, y = self.digits(me)
        return self.index(x + dx, core + dc, z + dz, y + dy)

    def in_line(self, me, k):
        if k < self.core:
            return self.near(me, dc=k)
        rest = k - self.core
        return self.near(me, dc=rest // (self.z - 1), dz=1 + rest % (self.z - 1))

    def in_plane(self, me, step):
        return self.near(me, dx=step // self.y, dy=step % self.y)

    def spot(self, me, step):
        x, _, _, y = self.digits(me)
        return (x + step // self.y) % self.x * self.y + (y + step % self.y) % self.y

    def given(self, blocks):
        return [blocks[0]] + [
            self.shift(block, dx=dx, dy=dy)
            for block, (dx, dy) in zip(blocks[1:], self.plane[1:])
        ]

    def place(self, triangle, tri_dev, me):
        x, core, z, y = self.digits(triangle // tri_dev)
        mx, mcore, mz, my = self.digits(me)
        dz, dc = (z - mz) % self.z, (core - mcore) % self.core
        block = jnp.where(dz == 0, dc, self.core + dc * (self.z - 1) + dz - 1)
        inside = (x == mx) & (y == my)
        return jnp.where(inside, block * tri_dev + triangle % tri_dev, -1)


class Letter:
    def __init__(self, edges, tri_dev, labels):
        self.edges, self.tri_dev, self.half = edges, tri_dev, -(-tri_dev // 2)
        sizes = [edges, tri_dev, self.half, labels]
        starts = [0]
        for size in sizes:
            starts.append(starts[-1] + -(-size // 128))
        self.starts, self.rows = starts[:4], -(-starts[4] // 8) * 8

    def take(self, letter, part, size):
        first = self.starts[part]
        parts = [letter[first + k : first + k + 1, :] for k in range(-(-size // 128))]
        return jnp.concatenate(parts, axis=1)[:, :size]

    def ends(self, letter):
        pair = self.take(letter, 0, self.edges)
        return pair & 0xFFFF, lax.shift_right_logical(pair, 16)

    def points(self, letter):
        first = self.take(letter, 1, self.tri_dev)
        third = self.take(letter, 2, self.half)
        third = jnp.concatenate([third & 0xFFFF, lax.shift_right_logical(third, 16)], axis=1)
        return jnp.concatenate(
            [first & 0xFFFF, lax.shift_right_logical(first, 16), third[:, : self.tri_dev]], axis=0
        )


def in_rows(row):
    size = row.shape[1]
    if size % 128:
        row = jnp.concatenate([row, jnp.zeros((1, -size % 128), I32)], axis=1)
    return [row[:, k : k + 128] for k in range(0, row.shape[1], 128)]


def letter_kernel(layout, form, slots, inc_ref, points_ref, letter_ref):
    edges, tri_dev, half = form.edges, form.tri_dev, form.half
    ends, devices = 2 * edges, layout.devices
    plus, minus = inc_ref[0:1, :], inc_ref[1:2, :]
    tri = jnp.concatenate([plus, minus], axis=1)
    other = jnp.concatenate([minus, plus], axis=1)
    owner = tri // tri_dev
    hits = iota((devices, ends), 0) == owner
    upper = ones_where(iota((ends, ends), 0) <= iota((ends, ends), 1))
    count = matmul(ones_where(hits), upper)
    rank = jnp.sum(jnp.where(hits, count, 0.0), axis=0, keepdims=True).astype(I32) - 1
    order = ones_where(iota((slots, ends), 0) == rank)
    label = jnp.zeros((devices, slots), I32)
    digits = ((tri % tri_dev + 1, 1), (other & 255, 65536), (other >> 8, 65536 * 256))
    for digit, weight in digits:
        spread = jnp.where(hits, digit.astype(F32), 0.0).astype(BF16)
        label = label + matmul_nt(spread, order).astype(I32) * weight
    third = points_ref[2:3, :]
    if tri_dev % 2:
        third = jnp.concatenate([third, jnp.zeros((1, 1), I32)], axis=1)
    common = (
        in_rows(plus + (minus << 16))
        + in_rows(points_ref[0:1, :] + (points_ref[1:2, :] << 16))
        + in_rows(third[:, :half] + (third[:, half:] << 16))
    )
    places = [(x, y) for x in range(layout.x) for y in range(layout.y)]
    for core in range(layout.core):
        for z in range(layout.z):
            there = [layout.index(x, core, z, y) for x, y in places]
            mine = in_rows(jnp.concatenate([label[d : d + 1, :] for d in there], axis=1))
            blank = form.rows - len(common) - len(mine)
            rows = common + mine + [jnp.zeros((1, 128), I32)] * blank
            letter = jnp.concatenate(rows, axis=0)
            for d in there:
                letter_ref[d] = letter


def letters_of(layout, form, incidence, centroids, slots):
    return pl.pallas_call(
        functools.partial(letter_kernel, layout, form, slots),
        in_specs=[whole()] * 2,
        out_specs=whole(),
        out_shape=jax.ShapeDtypeStruct((layout.devices, form.rows, 128), I32),
        compiler_params=PARAMS,
        cost_estimate=cost(1),
    )(incidence, centroids)


def pack_kernel(count, *refs):
    out_ref = refs[-1]
    size = refs[0].shape[0]
    for k in range(count):
        out_ref[k * size : (k + 1) * size, :] = refs[k][...]


def pack(pieces, after):
    size, width = pieces[0].shape
    return pl.pallas_call(
        functools.partial(pack_kernel, len(pieces)),
        in_specs=[whole()] * (len(pieces) + len(after)),
        out_specs=whole(),
        out_shape=jax.ShapeDtypeStruct((len(pieces) * size, width), BF16),
        compiler_params=PARAMS,
        cost_estimate=cost(0.5),
    )(*pieces, *after)


def features(points, scale, first):
    rows, count = points.shape
    square = jnp.sum(points * points, axis=0, keepdims=True)
    norms = [square & 255, square & 0xFF00, square & 0xFF0000]
    ones = [jnp.ones_like(square)] * 3
    zeros = [jnp.zeros((16 - rows - 7, count), I32)]
    if first:
        parts = [-2 * points] + norms + ones + [ones[0]] + zeros
    else:
        parts = [points] + ones + norms + [ones[0]] + zeros
    return (jnp.concatenate(parts, axis=0).astype(F32) * scale).astype(BF16)


def poly(coefs, scale, u):
    value = jnp.full_like(u, coefs[-1] * scale)
    for coef in coefs[-2::-1]:
        value = value * u + coef * scale
    return value


def tile_kernel(layout, form, block, me_ref, letter_ref, *refs):
    real_ref, imag_ref, token_ref, col_ref = refs
    token_ref[...] = jnp.zeros_like(token_ref)
    me, step, size = me_ref[0], pl.program_id(0), form.tri_dev

    @pl.when(step == 0)
    def _():
        for k in range(layout.z * layout.core):
            letter = letter_ref[layout.in_line(me, k)]
            col_ref[:, k * size : (k + 1) * size] = features(form.points(letter), 1.0, False)

    letter = letter_ref[layout.in_plane(me, step)]
    row = features(form.points(letter), 1.0 / (TURNS * TURNS), True)
    for base in range(0, col_ref.shape[1], block):
        cols = slice(base, base + block)
        square = lax.dot_general(
            row, col_ref[:, cols], (((0,), (0,)), ((), ())), preferred_element_type=F32
        )
        inverse = lax.rsqrt(square)
        turns = square * inverse
        frac = turns - ((turns + ROUND) - ROUND)
        u = frac * frac
        real_ref[:, cols] = (poly(COS, SPACING / TURNS, u) * inverse).astype(BF16)
        imag_ref[:, cols] = (poly(SIN, -SPACING / TURNS, u) * (frac * inverse)).astype(BF16)


def build(kernel, outs, rows, span, cols, me, arrays, time, scratch=(), extra=()):
    return pl.pallas_call(
        kernel,
        grid=(len(span),),
        in_specs=[pl.BlockSpec(memory_space=pltpu.SMEM)] + [fixed(array) for array in arrays],
        out_specs=[pl.BlockSpec((rows, cols), lambda j: (j, 0))] * outs
        + [fixed(array) for array in extra]
        + [token_spec()],
        out_shape=[pltpu.HBM((len(span) * rows, cols), BF16)] * outs + list(extra) + [TOKEN],
        scratch_shapes=scratch,
        compiler_params=PARAMS,
        cost_estimate=cost(time),
    )(me, *arrays)


def pick(row, base, count):
    low = jnp.where((row >= base) & (row < base + count), row - base, -1)
    wanted = iota((count, row.shape[1]), 0).astype(F32).astype(BF16)
    same = wanted == low.astype(F32).astype(BF16)
    return jnp.where(same, jnp.ones((), BF16), jnp.zeros((), BF16))


def adjacency_kernel(layout, tri_dev, first, me_ref, label_ref, after_ref, out_ref, *refs):
    refs[-1][...] = jnp.zeros_like(refs[-1])
    me, step = me_ref[0], pl.program_id(0)
    rows, cols = out_ref.shape
    label = label_ref[layout.spot(me, first + step)]
    mark = (label & 0xFFFF) - 1
    place = layout.place(lax.shift_right_logical(label, 16), tri_dev, me)
    place = jnp.where(mark >= 0, place, -1)
    low = pick(jnp.where(place >= 0, place % rows, -1), 0, rows)
    for base in range(0, cols, rows):
        inside = (place >= base) & (place < base + rows)
        here = pick(jnp.where(inside, mark, -1), 0, rows)
        out_ref[:, base : base + rows] = matmul_nt(here, low).astype(BF16)
    if first == 0:

        @pl.when(step == 0)
        def _():
            every = pick(mark, 0, rows)
            refs[0][...] = matmul(every, jnp.ones((every.shape[1], 128), BF16))


def incidence_kernel(layout, form, me_ref, letter_ref, after_ref, out_ref, token_ref):
    token_ref[...] = jnp.zeros_like(token_ref)
    me, step = me_ref[0], pl.program_id(0)
    edges, cols = out_ref.shape
    size = form.tri_dev
    letter = letter_ref[layout.in_plane(me, step)]
    plus, minus = [layout.place(end, size, me) for end in form.ends(letter)]
    eye = ones_where(iota((edges, edges), 0) == iota((edges, edges), 1))
    for base in range(0, cols, size):
        signed = pick(plus, base, size) - pick(minus, base, size)
        out_ref[:, base : base + size] = matmul_nt(eye, signed).astype(BF16)


def set_blocks(value, outs):
    for k, out in enumerate(outs):

        @pl.when(pl.program_id(0) == k)
        def _(out=out):
            out[...] = value.astype(out.dtype)


def blocks_like(count, rows, width, exact):
    return [
        jax.ShapeDtypeStruct((rows, width), F32 if exact and k == 0 else BF16)
        for k in range(count)
    ]


def first_kernel(layout, form, me_ref, letter_ref, *refs):
    count = len(layout.plane)
    pieces, outs, token_ref = refs[: -count - 1], refs[-count - 1 : -1], refs[-1]
    token_ref[...] = jnp.zeros_like(token_ref)
    me, size, edges = me_ref[0], form.tri_dev, form.edges
    base = layout.in_plane(me, pl.program_id(0)) * size
    total, k = None, 0
    for piece in pieces:
        for row in range(0, piece.shape[0], edges):
            plus, minus = form.ends(letter_ref[layout.in_line(me, k)])
            signed = pick(plus, base, size) - pick(minus, base, size)
            term = matmul(signed, piece[row : row + edges, :])
            total = term if total is None else total + term
            k += 1
    set_blocks(total, outs)


def first_charges(layout, form, me, letters, pieces):
    count, width = len(layout.plane), pieces[0].shape[1]
    shapes = blocks_like(count, form.tri_dev, width, True) + [TOKEN]
    return pl.pallas_call(
        functools.partial(first_kernel, layout, form),
        grid=(count,),
        in_specs=[pl.BlockSpec(memory_space=pltpu.SMEM), fixed(letters)]
        + [fixed(piece) for piece in pieces],
        out_specs=[fixed(shape) for shape in shapes],
        out_shape=shapes,
        compiler_params=PARAMS,
        cost_estimate=cost(4),
    )(me, letters, *pieces)


def apply_kernel(mats, fed, count, *refs):
    matrices, pieces = refs[:mats], refs[mats : mats + fed]
    outs, token_ref = refs[-count - 3 : -3], refs[-3]
    slots, sems = refs[-2:]
    token_ref[...] = jnp.zeros_like(token_ref)
    step = pl.program_id(0)
    rows = slots.shape[2]
    half = pieces[0].shape[1] // 2

    def copy(m, block):
        start = pl.multiple_of(block * rows, rows)
        slot = block % 2
        return pltpu.make_async_copy(
            matrices[m].at[pl.ds(start, rows), :], slots.at[slot, m], sems.at[slot, m]
        )

    @pl.when(step == 0)
    def _():
        for m in range(mats):
            copy(m, step).start()

    @pl.when(step + 1 < count)
    def _():
        for m in range(mats):
            copy(m, step + 1).start()

    sums = []
    for m in range(mats):
        copy(m, step).wait()
        matrix = slots.at[step % 2, m]
        total, col = None, 0
        for piece in pieces:
            size = piece.shape[0]
            term = matmul(matrix[:, col : col + size], piece[...])
            total = term if total is None else total + term
            col += size
        sums.append(total)
    value = sums[0]
    if mats == 2:
        real, imag = sums
        value = jnp.concatenate(
            [real[:, :half] - imag[:, half:], real[:, half:] + imag[:, :half]], axis=1
        )
    set_blocks(value, outs)


def apply(matrices, pieces, block, after=(), exact=True):
    rows, cols = matrices[0].shape
    count, mats = rows // block, len(matrices)
    shapes = blocks_like(count, block, pieces[0].shape[1], exact) + [TOKEN]
    return pl.pallas_call(
        functools.partial(apply_kernel, mats, len(pieces), count),
        grid=(count,),
        in_specs=[pl.BlockSpec(memory_space=pltpu.HBM)] * mats
        + [fixed(piece) for piece in pieces]
        + [token_spec()] * len(after),
        out_specs=[fixed(shape) for shape in shapes],
        out_shape=shapes,
        scratch_shapes=[
            pltpu.VMEM((2, mats, block, cols), BF16),
            pltpu.SemaphoreType.DMA((2, mats)),
        ],
        compiler_params=PARAMS,
        cost_estimate=cost(2 * mats),
    )(*matrices, *pieces, *after)


def sum_kernel(count, own_ref, *refs):
    total = own_ref[...]
    for ref in refs[:count]:
        total = total + ref[...].astype(F32)
    out_ref, rounded_ref, token_ref = refs[-3:]
    out_ref[...] = total
    rounded_ref[...] = total.astype(BF16)
    token_ref[...] = jnp.zeros_like(token_ref)


def sum_of(blocks, after):
    shape = blocks[0].shape
    return pl.pallas_call(
        functools.partial(sum_kernel, len(blocks) - 1),
        in_specs=[whole()] * (len(blocks) + len(after)),
        out_specs=[whole()] * 3,
        out_shape=[
            jax.ShapeDtypeStruct(shape, F32),
            jax.ShapeDtypeStruct(shape, BF16),
            TOKEN,
        ],
        compiler_params=PARAMS,
        cost_estimate=cost(1),
    )(*blocks, *after)


def potential_kernel(count, own_ref, *refs):
    total = own_ref[...]
    for ref in refs[:count]:
        total = total + ref[...].astype(F32)
    refs[-1][...] = total.astype(BF16)


def potential_of(blocks, after):
    got = blocks[1:]
    return pl.pallas_call(
        functools.partial(potential_kernel, len(got)),
        in_specs=[whole()] * (len(blocks) + len(after)),
        out_specs=whole(),
        out_shape=jax.ShapeDtypeStruct(blocks[0].shape, BF16),
        compiler_params=PARAMS,
        cost_estimate=cost(1),
    )(*blocks, *after)


def charge_kernel(count, weight_ref, charge_ref, degree_ref, potential_ref, own_ref, *refs):
    around = own_ref[...]
    for ref in refs[:count]:
        around = around + ref[...].astype(F32)
    out_ref, rounded_ref = refs[-2:]
    change = degree_ref[:, 0:1] * potential_ref[...].astype(F32) - around
    value = charge_ref[...] - weight_ref[0] * change
    out_ref[...] = value
    rounded_ref[...] = value.astype(BF16)


def charge_of(weight, charge, degree, potential, blocks):
    return pl.pallas_call(
        functools.partial(charge_kernel, len(blocks) - 1),
        in_specs=[pl.BlockSpec(memory_space=pltpu.SMEM)] + [whole()] * (3 + len(blocks)),
        out_specs=[whole()] * 2,
        out_shape=[
            jax.ShapeDtypeStruct(charge.shape, F32),
            jax.ShapeDtypeStruct(charge.shape, BF16),
        ],
        compiler_params=PARAMS,
        cost_estimate=cost(1),
    )(weight, charge, degree, potential, *blocks)


def current_kernel(count, weight_ref, current_ref, own_ref, *refs):
    slope = own_ref[...]
    for ref in refs[:count]:
        slope = slope + ref[...].astype(F32)
    out_ref, token_ref = refs[-2:]
    out_ref[...] = (current_ref[...].astype(F32) - weight_ref[0] * slope).astype(BF16)
    token_ref[...] = jnp.zeros_like(token_ref)


def current_of(weight, current, blocks):
    return pl.pallas_call(
        functools.partial(current_kernel, len(blocks) - 1),
        in_specs=[pl.BlockSpec(memory_space=pltpu.SMEM)] + [whole()] * (1 + len(blocks)),
        out_specs=[whole()] * 2,
        out_shape=[jax.ShapeDtypeStruct(current.shape, BF16), TOKEN],
        compiler_params=PARAMS,
        cost_estimate=cost(1),
    )(weight, current, *blocks)


def per_device(layout, currents, incidence, centroids, sweep_weights):
    me = lax.axis_index(AXES).astype(I32).reshape(1)
    tri_dev = centroids.shape[1]
    edge_dev = currents.shape[0]
    devices, count = layout.devices, len(layout.plane)
    slots = 8 * tri_dev // devices
    sweeps = sweep_weights.shape[0]
    cols = layout.z * layout.core * tri_dev

    form = Letter(edge_dev, tri_dev, count * slots)
    letters = letters_of(layout, form, incidence, centroids, slots)
    letters = lax.all_to_all(letters, AXES, split_axis=0, concat_axis=0, tiled=True)
    labels = letters[:, form.starts[3] :, :].reshape(devices, -1)[:, : count * slots]
    labels = labels.reshape(devices, count, slots).transpose(1, 0, 2)
    labels = labels.reshape(count, 1, devices * slots)

    make = functools.partial(build, cols=cols, me=me)
    plane = range(count)
    *tiles, token = make(
        functools.partial(tile_kernel, layout, form, min(512, cols)),
        2,
        tri_dev,
        plane,
        arrays=(letters,),
        time=12,
        scratch=[pltpu.VMEM((16, cols), BF16)],
    )
    pieces = layout.gathered(currents, (token,))
    *blocks, token = first_charges(layout, form, me, letters, pieces)
    slopes_of, token = make(
        functools.partial(incidence_kernel, layout, form),
        1,
        edge_dev,
        plane,
        arrays=(letters, token),
        time=6,
    )
    charge, rounded, token = sum_of(layout.given(blocks), (token,))

    cut = (count + 1) // 2

    def adjacency(span, token):
        *parts, token = make(
            functools.partial(adjacency_kernel, layout, tri_dev, span[0]),
            1,
            tri_dev,
            span,
            arrays=(labels, token),
            time=5,
            extra=() if span[0] else (jax.ShapeDtypeStruct((tri_dev, 128), F32),),
        )
        return parts, token

    (near, degree), token = adjacency(plane[:cut], token)
    neighbours = [near]
    current = currents
    potential = None
    slopes, after = None, (token,)
    for sweep in range(sweeps):
        weight = sweep_weights[sweep].reshape(1)
        pieces = layout.gathered(rounded, after)
        *blocks, token = apply(tiles, pieces, tri_dev)
        if slopes is not None:
            current, token = current_of(last_weight, current, layout.given(slopes))
        elif cut < count:
            (far,), token = adjacency(plane[cut:], token)
            neighbours.append(far)
        potential = potential_of(layout.given(blocks), (token,))
        pieces = layout.gathered(potential, ())
        if sweep + 1 < sweeps:
            blocks = []
            for part in neighbours:
                *more, _ = apply([part], pieces, tri_dev, (), not blocks)
                blocks += more
            charge, rounded = charge_of(
                weight, charge, degree, potential, layout.given(blocks)
            )
        *slopes, token = apply([slopes_of], pieces, edge_dev)
        after, last_weight = (token,), weight
    current, _ = current_of(last_weight, current, layout.given(slopes))
    return current, potential


def solution(mesh):
    layout = Layout(mesh.shape["row"], mesh.shape["col"])
    in_specs = (P(AXES, None), P(None, AXES), P(None, AXES), P())
    out_specs = (P(AXES, None), P(AXES, None))
    return jax.shard_map(
        functools.partial(per_device, layout),
        mesh=mesh,
        in_specs=in_specs,
        out_specs=out_specs,
        check_vma=False,
    )
```

```python
import functools
import math

import jax
import jax.numpy as jnp
from jax import lax
from jax.experimental import pallas as pl
from jax.experimental.pallas import tpu as pltpu
from jax.sharding import PartitionSpec as P

SPACING = 0.2
TURNS = 32.0
AXES = ("row", "col")
ROUND = 12582912.0
COS = (
    0.9999992107823218,
    -19.738980355763992,
    64.92865742103312,
    -85.27162153429882,
    58.79049212013072,
    -21.07110562764302,
)
SIN = (
    6.283184916495431,
    -41.34158923268858,
    81.59994332978287,
    -76.61447253124996,
    41.342882354568324,
    -12.471243535026977,
)
PARAMS = pltpu.CompilerParams(vmem_limit_bytes=24 * 2**20)
PEAK = 1.15e15
F32, BF16, I32 = jnp.float32, jnp.bfloat16, jnp.int32


def whole():
    return pl.BlockSpec(memory_space=pltpu.VMEM)


def fixed(array):
    return pl.BlockSpec(array.shape, lambda j: (0,) * len(array.shape))


def cost(microseconds):
    return pl.CostEstimate(
        flops=int(microseconds * 1e-6 * PEAK), bytes_accessed=0, transcendentals=0
    )


TOKEN = jax.ShapeDtypeStruct((8, 128), F32)


def token_spec():
    return pl.BlockSpec((8, 128), lambda *_: (0, 0))


def iota(shape, dim):
    return lax.broadcasted_iota(I32, shape, dim)


def ones_where(mask):
    return jnp.where(mask, jnp.ones((), F32), jnp.zeros((), F32)).astype(BF16)


def matmul(a, b):
    return jnp.dot(a, b, preferred_element_type=F32)


def matmul_nt(a, b):
    return lax.dot_general(a, b, (((1,), (1,)), ((), ())), preferred_element_type=F32)


class Layout:
    def __init__(self, n_row, n_col):
        self.core = 2 if n_row % 2 == 0 else 1
        self.x = n_row // self.core
        self.y = math.gcd(n_col, self.x)
        self.z = n_col // self.y
        self.devices = n_row * n_col
        self.plane = [(dx, dy) for dx in range(self.x) for dy in range(self.y)]

    def digits(self, index):
        y = index % self.y
        z = index // self.y % self.z
        core = index // (self.y * self.z) % self.core
        return index // (self.y * self.z * self.core), core, z, y

    def shift(self, value, dx=0, dc=0, dz=0, dy=0):
        pairs = []
        for i in range(self.devices):
            pairs.append((i, self.near(i, dx, dc, dz, dy)))
        return lax.ppermute(value, AXES, pairs)

    def by_core(self, value):
        return [value] + [self.shift(value, dc=-dc) for dc in range(1, self.core)]

    def gathered(self, value, after, own=None):
        pieces = own or self.by_core(value)
        along = [self.shift(value, dz=-dz) for dz in range(1, self.z)]
        return pieces + (self.by_core(pack(along, after)) if along else [])

    def index(self, x, core, z, y):
        x, core, z, y = x % self.x, core % self.core, z % self.z, y % self.y
        return ((x * self.core + core) * self.z + z) * self.y + y

    def near(self, me, dx=0, dc=0, dz=0, dy=0):
        x, core, z, y = self.digits(me)
        return self.index(x + dx, core + dc, z + dz, y + dy)

    def in_line(self, me, k):
        if k < self.core:
            return self.near(me, dc=k)
        rest = k - self.core
        return self.near(me, dc=rest // (self.z - 1), dz=1 + rest % (self.z - 1))

    def in_plane(self, me, step):
        return self.near(me, dx=step // self.y, dy=step % self.y)

    def spot(self, me, step):
        x, _, _, y = self.digits(me)
        return (x + step // self.y) % self.x * self.y + (y + step % self.y) % self.y

    def given(self, blocks):
        return [blocks[0]] + [
            self.shift(block, dx=dx, dy=dy)
            for block, (dx, dy) in zip(blocks[1:], self.plane[1:])
        ]

    def place(self, triangle, tri_dev, me):
        x, core, z, y = self.digits(triangle // tri_dev)
        mx, mcore, mz, my = self.digits(me)
        dz, dc = (z - mz) % self.z, (core - mcore) % self.core
        block = jnp.where(dz == 0, dc, self.core + dc * (self.z - 1) + dz - 1)
        inside = (x == mx) & (y == my)
        return jnp.where(inside, block * tri_dev + triangle % tri_dev, -1)


class Letter:
    def __init__(self, edges, tri_dev, labels):
        self.edges, self.tri_dev, self.half = edges, tri_dev, -(-tri_dev // 2)
        sizes = [edges, tri_dev, self.half, labels]
        starts = [0]
        for size in sizes:
            starts.append(starts[-1] + -(-size // 128))
        self.starts, self.rows = starts[:4], -(-starts[4] // 8) * 8

    def take(self, letter, part, size):
        first = self.starts[part]
        parts = [letter[first + k : first + k + 1, :] for k in range(-(-size // 128))]
        return jnp.concatenate(parts, axis=1)[:, :size]

    def ends(self, letter):
        pair = self.take(letter, 0, self.edges)
        return pair & 0xFFFF, lax.shift_right_logical(pair, 16)

    def points(self, letter):
        first = self.take(letter, 1, self.tri_dev)
        third = self.take(letter, 2, self.half)
        third = jnp.concatenate([third & 0xFFFF, lax.shift_right_logical(third, 16)], axis=1)
        return jnp.concatenate(
            [first & 0xFFFF, lax.shift_right_logical(first, 16), third[:, : self.tri_dev]], axis=0
        )


def in_rows(row):
    size = row.shape[1]
    if size % 128:
        row = jnp.concatenate([row, jnp.zeros((1, -size % 128), I32)], axis=1)
    return [row[:, k : k + 128] for k in range(0, row.shape[1], 128)]


def letter_kernel(layout, form, slots, inc_ref, points_ref, *refs):
    letter_ref = refs[-1]
    edges, tri_dev, half = form.edges, form.tri_dev, form.half
    ends, devices = 2 * edges, layout.devices
    plus, minus = inc_ref[0:1, :], inc_ref[1:2, :]
    tri = jnp.concatenate([plus, minus], axis=1)
    other = jnp.concatenate([minus, plus], axis=1)
    owner = tri // tri_dev
    hits = iota((devices, ends), 0) == owner
    upper = ones_where(iota((ends, ends), 0) <= iota((ends, ends), 1))
    count = matmul(ones_where(hits), upper)
    rank = jnp.sum(jnp.where(hits, count, 0.0), axis=0, keepdims=True).astype(I32) - 1
    order = ones_where(iota((slots, ends), 0) == rank)
    label = jnp.zeros((devices, slots), I32)
    digits = ((tri % tri_dev + 1, 1), (other & 255, 65536), (other >> 8, 65536 * 256))
    for digit, weight in digits:
        spread = jnp.where(hits, digit.astype(F32), 0.0).astype(BF16)
        label = label + matmul_nt(spread, order).astype(I32) * weight
    third = points_ref[2:3, :]
    if tri_dev % 2:
        third = jnp.concatenate([third, jnp.zeros((1, 1), I32)], axis=1)
    common = (
        in_rows(plus + (minus << 16))
        + in_rows(points_ref[0:1, :] + (points_ref[1:2, :] << 16))
        + in_rows(third[:, :half] + (third[:, half:] << 16))
    )
    places = [(x, y) for x in range(layout.x) for y in range(layout.y)]
    for core in range(layout.core):
        for z in range(layout.z):
            there = [layout.index(x, core, z, y) for x, y in places]
            mine = in_rows(jnp.concatenate([label[d : d + 1, :] for d in there], axis=1))
            blank = form.rows - len(common) - len(mine)
            rows = common + mine + [jnp.zeros((1, 128), I32)] * blank
            letter = jnp.concatenate(rows, axis=0)
            for d in there:
                letter_ref[d] = letter


def letters_of(layout, form, incidence, centroids, slots, after):
    return pl.pallas_call(
        functools.partial(letter_kernel, layout, form, slots),
        in_specs=[whole()] * (2 + len(after)),
        out_specs=whole(),
        out_shape=jax.ShapeDtypeStruct((layout.devices, form.rows, 128), I32),
        compiler_params=PARAMS,
        cost_estimate=cost(1),
    )(incidence, centroids, *after)


def pack_kernel(count, *refs):
    out_ref = refs[-1]
    size = refs[0].shape[0]
    for k in range(count):
        out_ref[k * size : (k + 1) * size, :] = refs[k][...]


def pack(pieces, after):
    size, width = pieces[0].shape
    return pl.pallas_call(
        functools.partial(pack_kernel, len(pieces)),
        in_specs=[whole()] * (len(pieces) + len(after)),
        out_specs=whole(),
        out_shape=jax.ShapeDtypeStruct((len(pieces) * size, width), BF16),
        compiler_params=PARAMS,
        cost_estimate=cost(0.5),
    )(*pieces, *after)


def features(points, scale, first):
    rows, count = points.shape
    square = jnp.sum(points * points, axis=0, keepdims=True)
    norms = [square & 255, square & 0xFF00, square & 0xFF0000]
    ones = [jnp.ones_like(square)] * 3
    zeros = [jnp.zeros((16 - rows - 7, count), I32)]
    if first:
        parts = [-2 * points] + norms + ones + [ones[0]] + zeros
    else:
        parts = [points] + ones + norms + [ones[0]] + zeros
    return (jnp.concatenate(parts, axis=0).astype(F32) * scale).astype(BF16)


def poly(coefs, scale, u):
    value = jnp.full_like(u, coefs[-1] * scale)
    for coef in coefs[-2::-1]:
        value = value * u + coef * scale
    return value


def rows_at(ref, step, rows):
    if ref.shape[0] == rows:
        return ref
    return ref.at[pl.ds(pl.multiple_of(step * rows, rows), rows), :]


def tile_kernel(layout, form, block, first, me_ref, letter_ref, after_ref, *refs):
    real_ref, imag_ref, token_ref, col_ref = refs
    token_ref[...] = jnp.zeros_like(token_ref)
    me, step, size = me_ref[0], pl.program_id(0), form.tri_dev

    @pl.when(step == 0)
    def _():
        for k in range(layout.z * layout.core):
            letter = letter_ref[layout.in_line(me, k)]
            col_ref[:, k * size : (k + 1) * size] = features(form.points(letter), 1.0, False)

    real_ref, imag_ref = [rows_at(ref, step, size) for ref in (real_ref, imag_ref)]
    letter = letter_ref[layout.in_plane(me, first + step)]
    row = features(form.points(letter), 1.0 / (TURNS * TURNS), True)
    for base in range(0, col_ref.shape[1], block):
        cols = slice(base, base + block)
        square = lax.dot_general(
            row, col_ref[:, cols], (((0,), (0,)), ((), ())), preferred_element_type=F32
        )
        inverse = lax.rsqrt(square)
        turns = square * inverse
        frac = turns - ((turns + ROUND) - ROUND)
        u = frac * frac
        real_ref[:, cols] = (poly(COS, SPACING / TURNS, u) * inverse).astype(BF16)
        imag_ref[:, cols] = (poly(SIN, -SPACING / TURNS, u) * (frac * inverse)).astype(BF16)


def build(kernel, outs, rows, span, arrays, time, cols, me, resident, scratch=(), extra=()):
    space = pltpu.VMEM if resident else pltpu.HBM
    block = whole() if resident else pl.BlockSpec((rows, cols), lambda j: (j, 0))
    return pl.pallas_call(
        kernel,
        grid=(len(span),),
        in_specs=[pl.BlockSpec(memory_space=pltpu.SMEM)] + [fixed(array) for array in arrays],
        out_specs=[block] * outs + [fixed(array) for array in extra] + [token_spec()],
        out_shape=[space((len(span) * rows, cols), BF16)] * outs + list(extra) + [TOKEN],
        scratch_shapes=scratch,
        compiler_params=PARAMS,
        cost_estimate=cost(time),
    )(me, *arrays)


def pick(row, base, count):
    low = jnp.where((row >= base) & (row < base + count), row - base, -1)
    wanted = iota((count, row.shape[1]), 0).astype(F32).astype(BF16)
    same = wanted == low.astype(F32).astype(BF16)
    return jnp.where(same, jnp.ones((), BF16), jnp.zeros((), BF16))


def adjacency_kernel(layout, tri_dev, first, me_ref, label_ref, after_ref, out_ref, *refs):
    refs[-1][...] = jnp.zeros_like(refs[-1])
    me, step = me_ref[0], pl.program_id(0)
    rows, cols = tri_dev, out_ref.shape[1]
    out_ref = rows_at(out_ref, step, rows)
    label = label_ref[layout.spot(me, first + step)]
    mark = (label & 0xFFFF) - 1
    place = layout.place(lax.shift_right_logical(label, 16), tri_dev, me)
    place = jnp.where(mark >= 0, place, -1)
    low = pick(jnp.where(place >= 0, place % rows, -1), 0, rows)
    for base in range(0, cols, rows):
        inside = (place >= base) & (place < base + rows)
        here = pick(jnp.where(inside, mark, -1), 0, rows)
        out_ref[:, base : base + rows] = matmul_nt(here, low).astype(BF16)
    if first == 0:

        @pl.when(step == 0)
        def _():
            every = pick(mark, 0, rows)
            refs[0][...] = matmul(every, jnp.ones((every.shape[1], 128), BF16))


def incidence_kernel(layout, form, me_ref, letter_ref, after_ref, out_ref, token_ref):
    token_ref[...] = jnp.zeros_like(token_ref)
    me, step = me_ref[0], pl.program_id(0)
    edges, cols = form.edges, out_ref.shape[1]
    out_ref = rows_at(out_ref, step, edges)
    size = form.tri_dev
    letter = letter_ref[layout.in_plane(me, step)]
    plus, minus = [layout.place(end, size, me) for end in form.ends(letter)]
    eye = ones_where(iota((edges, edges), 0) == iota((edges, edges), 1))
    for base in range(0, cols, size):
        signed = pick(plus, base, size) - pick(minus, base, size)
        out_ref[:, base : base + size] = matmul_nt(eye, signed).astype(BF16)


def set_blocks(value, outs):
    for k, out in enumerate(outs):

        @pl.when(pl.program_id(0) == k)
        def _(out=out):
            out[...] = value.astype(out.dtype)


def blocks_like(count, rows, width, exact):
    return [
        jax.ShapeDtypeStruct((rows, width), F32 if exact and k == 0 else BF16)
        for k in range(count)
    ]


def first_kernel(layout, form, me_ref, letter_ref, *refs):
    count = len(layout.plane)
    pieces, outs, token_ref = refs[: -count - 1], refs[-count - 1 : -1], refs[-1]
    token_ref[...] = jnp.zeros_like(token_ref)
    me, size, edges = me_ref[0], form.tri_dev, form.edges
    base = layout.in_plane(me, pl.program_id(0)) * size
    total, k = None, 0
    for piece in pieces:
        for row in range(0, piece.shape[0], edges):
            plus, minus = form.ends(letter_ref[layout.in_line(me, k)])
            signed = pick(plus, base, size) - pick(minus, base, size)
            term = matmul(signed, piece[row : row + edges, :])
            total = term if total is None else total + term
            k += 1
    set_blocks(total, outs)


def first_charges(layout, form, me, letters, pieces):
    count, width = len(layout.plane), pieces[0].shape[1]
    shapes = blocks_like(count, form.tri_dev, width, True) + [TOKEN]
    return pl.pallas_call(
        functools.partial(first_kernel, layout, form),
        grid=(count,),
        in_specs=[pl.BlockSpec(memory_space=pltpu.SMEM), fixed(letters)]
        + [fixed(piece) for piece in pieces],
        out_specs=[fixed(shape) for shape in shapes],
        out_shape=shapes,
        compiler_params=PARAMS,
        cost_estimate=cost(4),
    )(me, letters, *pieces)


def apply_kernel(mats, fed, block, *refs):
    matrices, pieces, outs = refs[:mats], refs[mats : mats + fed], refs[mats + fed : -1]
    refs[-1][...] = jnp.zeros_like(refs[-1])
    half = pieces[0].shape[1] // 2
    sums = []
    for matrix in matrices:
        matrix = rows_at(matrix, pl.program_id(0), block)
        total, col = None, 0
        for piece in pieces:
            size = piece.shape[0]
            term = matmul(matrix[:, col : col + size], piece[...])
            total = term if total is None else total + term
            col += size
        sums.append(total)
    value = sums[0]
    if mats == 2:
        real, imag = sums
        value = jnp.concatenate(
            [real[:, :half] - imag[:, half:], real[:, half:] + imag[:, :half]], axis=1
        )
    set_blocks(value, outs)


def apply(matrices, pieces, block, resident, exact, after):
    rows, cols = matrices[0].shape
    count, mats = rows // block, len(matrices)
    shapes = blocks_like(count, block, pieces[0].shape[1], exact) + [TOKEN]
    spec = whole() if resident else pl.BlockSpec((block, cols), lambda j: (j, 0))

    def kernel(*refs):
        fed = len(refs) - len(shapes) - len(after)
        apply_kernel(mats, fed - mats, block, *refs[:fed], *refs[fed + len(after) :])

    return pl.pallas_call(
        kernel,
        grid=(count,),
        in_specs=[spec] * mats
        + [fixed(piece) for piece in pieces]
        + [token_spec()] * len(after),
        out_specs=[fixed(shape) for shape in shapes],
        out_shape=shapes,
        compiler_params=PARAMS,
        cost_estimate=cost(count * mats / 2),
    )(*matrices, *pieces, *after)


def multiply(parts, pieces, block, resident, after=()):
    blocks, token = [], None
    for part in parts:
        *more, token = apply(part, pieces, block, resident, not blocks, after)
        blocks += more
    return blocks, token


def sum_kernel(count, own_ref, *refs):
    total = own_ref[...]
    for ref in refs[:count]:
        total = total + ref[...].astype(F32)
    out_ref, rounded_ref, token_ref = refs[-3:]
    out_ref[...] = total
    rounded_ref[...] = total.astype(BF16)
    token_ref[...] = jnp.zeros_like(token_ref)


def sum_of(blocks, after):
    shape = blocks[0].shape
    return pl.pallas_call(
        functools.partial(sum_kernel, len(blocks) - 1),
        in_specs=[whole()] * (len(blocks) + len(after)),
        out_specs=[whole()] * 3,
        out_shape=[
            jax.ShapeDtypeStruct(shape, F32),
            jax.ShapeDtypeStruct(shape, BF16),
            TOKEN,
        ],
        compiler_params=PARAMS,
        cost_estimate=cost(1),
    )(*blocks, *after)


def potential_kernel(count, own_ref, *refs):
    total = own_ref[...]
    for ref in refs[:count]:
        total = total + ref[...].astype(F32)
    refs[-2][...] = total.astype(BF16)
    refs[-1][...] = jnp.zeros_like(refs[-1])


def potential_of(blocks, after):
    got = blocks[1:]
    return pl.pallas_call(
        functools.partial(potential_kernel, len(got)),
        in_specs=[whole()] * (len(blocks) + len(after)),
        out_specs=[whole()] * 2,
        out_shape=[jax.ShapeDtypeStruct(blocks[0].shape, BF16), TOKEN],
        compiler_params=PARAMS,
        cost_estimate=cost(1),
    )(*blocks, *after)


def charge_kernel(count, weight_ref, charge_ref, degree_ref, potential_ref, own_ref, *refs):
    around = own_ref[...]
    for ref in refs[:count]:
        around = around + ref[...].astype(F32)
    out_ref, rounded_ref, token_ref = refs[-3:]
    token_ref[...] = jnp.zeros_like(token_ref)
    change = degree_ref[:, 0:1] * potential_ref[...].astype(F32) - around
    value = charge_ref[...] - weight_ref[0] * change
    out_ref[...] = value
    rounded_ref[...] = value.astype(BF16)


def charge_of(weight, charge, degree, potential, blocks, after):
    return pl.pallas_call(
        functools.partial(charge_kernel, len(blocks) - 1),
        in_specs=[pl.BlockSpec(memory_space=pltpu.SMEM)] + [whole()] * (3 + len(blocks) + len(after)),
        out_specs=[whole()] * 3,
        out_shape=[
            jax.ShapeDtypeStruct(charge.shape, F32),
            jax.ShapeDtypeStruct(charge.shape, BF16),
            TOKEN,
        ],
        compiler_params=PARAMS,
        cost_estimate=cost(1),
    )(weight, charge, degree, potential, *blocks, *after)


def current_kernel(count, weight_ref, current_ref, own_ref, *refs):
    slope = own_ref[...]
    for ref in refs[:count]:
        slope = slope + ref[...].astype(F32)
    out_ref, token_ref = refs[-2:]
    out_ref[...] = (current_ref[...].astype(F32) - weight_ref[0] * slope).astype(BF16)
    token_ref[...] = jnp.zeros_like(token_ref)


def current_of(weight, current, blocks):
    return pl.pallas_call(
        functools.partial(current_kernel, len(blocks) - 1),
        in_specs=[pl.BlockSpec(memory_space=pltpu.SMEM)] + [whole()] * (1 + len(blocks)),
        out_specs=[whole()] * 2,
        out_shape=[jax.ShapeDtypeStruct(current.shape, BF16), TOKEN],
        compiler_params=PARAMS,
        cost_estimate=cost(1),
    )(weight, current, *blocks)


def per_device(layout, currents, incidence, centroids, sweep_weights):
    me = lax.axis_index(AXES).astype(I32).reshape(1)
    tri_dev = centroids.shape[1]
    edge_dev = currents.shape[0]
    devices, count = layout.devices, len(layout.plane)
    slots = 8 * tri_dev // devices
    sweeps = sweep_weights.shape[0]
    cols = layout.z * layout.core * tri_dev

    resident = count * (3 * tri_dev + edge_dev) * cols * 2 <= 24 * 2**20

    own = layout.by_core(currents)
    form = Letter(edge_dev, tri_dev, count * slots)
    letters = letters_of(
        layout, form, incidence, centroids, slots, own[1:]
    )
    letters = lax.all_to_all(letters, AXES, split_axis=0, concat_axis=0, tiled=True)
    labels = letters[:, form.starts[3] :, :].reshape(devices, -1)[:, : count * slots]
    labels = labels.reshape(devices, count, slots).transpose(1, 0, 2)
    labels = labels.reshape(count, 1, devices * slots)

    make = functools.partial(build, cols=cols, me=me, resident=resident)
    cut = (count + 1) // 2
    spans = [span for span in (range(cut), range(cut, count)) if span]

    def tile_part(span, token):
        *part, token = make(
            functools.partial(tile_kernel, layout, form, min(512, cols), span[0]),
            2,
            tri_dev,
            span,
            (letters, token),
            6,
            scratch=[pltpu.VMEM((16, cols), BF16)],
        )
        return part, token

    def adjacency_part(span, token):
        extra = () if span[0] else (jax.ShapeDtypeStruct((tri_dev, 128), F32),)
        *part, token = make(
            functools.partial(adjacency_kernel, layout, tri_dev, span[0]),
            1,
            tri_dev,
            span,
            (labels, token),
            6,
            extra=extra,
        )
        return part, token

    pieces = layout.gathered(currents, (letters,), own)
    *blocks, token = first_charges(layout, form, me, letters, pieces)
    part, token = tile_part(spans[0], token)
    tiles = [part]
    charge, rounded, token = sum_of(layout.given(blocks), (token,))
    for span in spans[1:]:
        part, token = tile_part(span, token)
        tiles.append(part)

    near, slopes_of = [], []
    degree, slopes = None, None
    current, potential = currents, None
    for sweep in range(sweeps):
        weight = sweep_weights[sweep].reshape(1)
        pieces = layout.gathered(rounded, (token,))
        blocks, token = multiply(tiles, pieces, tri_dev, resident)
        if slopes is not None:
            current, token = current_of(last_weight, current, layout.given(slopes))
        else:
            (part, degree), token = adjacency_part(spans[0], token)
            near.append([part])
        potential, token = potential_of(layout.given(blocks), (token,))
        if slopes is None:
            for span in spans[1:]:
                part, token = adjacency_part(span, token)
                near.append(part)
        pieces = layout.gathered(potential, (token,))
        if sweep + 1 < sweeps:
            blocks, token = multiply(near, pieces, tri_dev, resident)
        if slopes is None:
            *part, token = make(
                functools.partial(incidence_kernel, layout, form),
                1,
                edge_dev,
                range(count),
                (letters, token),
                6,
            )
            slopes_of.append(part)
        if sweep + 1 < sweeps:
            charge, rounded, token = charge_of(
                weight, charge, degree, potential, layout.given(blocks), (token,)
            )
        slopes, token = multiply(slopes_of, pieces, edge_dev, resident, (token,))
        last_weight = weight
    current, _ = current_of(last_weight, current, layout.given(slopes))
    return current, potential


def solution(mesh):
    layout = Layout(mesh.shape["row"], mesh.shape["col"])
    in_specs = (P(AXES, None), P(None, AXES), P(None, AXES), P())
    out_specs = (P(AXES, None), P(AXES, None))
    return jax.shard_map(
        functools.partial(per_device, layout),
        mesh=mesh,
        in_specs=in_specs,
        out_specs=out_specs,
        check_vma=False,
    )
```

```python
import functools
import math

import jax
import jax.numpy as jnp
from jax import lax
from jax.experimental import pallas as pl
from jax.experimental.pallas import tpu as pltpu
from jax.sharding import PartitionSpec as P

SPACING = 0.2
TURNS = 32.0
AXES = ("row", "col")
ROUND = 12582912.0
COS = (
    0.9999992107823218,
    -19.738980355763992,
    64.92865742103312,
    -85.27162153429882,
    58.79049212013072,
    -21.07110562764302,
)
SIN = (
    6.283184916495431,
    -41.34158923268858,
    81.59994332978287,
    -76.61447253124996,
    41.342882354568324,
    -12.471243535026977,
)
SMALL, LARGE = 10 * 2**20, 24 * 2**20
PARAMS = pltpu.CompilerParams(vmem_limit_bytes=SMALL)
PEAK = 1.15e15
F32, BF16, I32 = jnp.float32, jnp.bfloat16, jnp.int32


def whole():
    return pl.BlockSpec(memory_space=pltpu.VMEM)


def fixed(array):
    return pl.BlockSpec(array.shape, lambda j: (0,) * len(array.shape))


def params(resident):
    return pltpu.CompilerParams(vmem_limit_bytes=SMALL if resident else LARGE)


def cost(microseconds):
    return pl.CostEstimate(
        flops=int(microseconds * 1e-6 * PEAK), bytes_accessed=0, transcendentals=0
    )


TOKEN = jax.ShapeDtypeStruct((8, 128), F32)


def token_spec():
    return pl.BlockSpec((8, 128), lambda *_: (0, 0))


def iota(shape, dim):
    return lax.broadcasted_iota(I32, shape, dim)


def ones_where(mask):
    return jnp.where(mask, jnp.ones((), F32), jnp.zeros((), F32)).astype(BF16)


def matmul(a, b):
    return jnp.dot(a, b, preferred_element_type=F32)


def matmul_nt(a, b):
    return lax.dot_general(a, b, (((1,), (1,)), ((), ())), preferred_element_type=F32)


class Layout:
    def __init__(self, n_row, n_col):
        self.core = 2 if n_row % 2 == 0 else 1
        self.x = n_row // self.core
        self.y = math.gcd(n_col, self.x)
        self.z = n_col // self.y
        self.devices = n_row * n_col
        self.plane = [(dx, dy) for dx in range(self.x) for dy in range(self.y)]

    def digits(self, index):
        y = index % self.y
        z = index // self.y % self.z
        core = index // (self.y * self.z) % self.core
        return index // (self.y * self.z * self.core), core, z, y

    def shift(self, value, dx=0, dc=0, dz=0, dy=0):
        pairs = []
        for i in range(self.devices):
            pairs.append((i, self.near(i, dx, dc, dz, dy)))
        return lax.ppermute(value, AXES, pairs)

    def by_core(self, value):
        return [value] + [self.shift(value, dc=-dc) for dc in range(1, self.core)]

    def gathered(self, value, after, own=None):
        pieces = own or self.by_core(value)
        along = [self.shift(value, dz=-dz) for dz in range(1, self.z)]
        return pieces + (self.by_core(pack(along, after)) if along else [])

    def index(self, x, core, z, y):
        x, core, z, y = x % self.x, core % self.core, z % self.z, y % self.y
        return ((x * self.core + core) * self.z + z) * self.y + y

    def near(self, me, dx=0, dc=0, dz=0, dy=0):
        x, core, z, y = self.digits(me)
        return self.index(x + dx, core + dc, z + dz, y + dy)

    def in_line(self, me, k):
        if k < self.core:
            return self.near(me, dc=k)
        rest = k - self.core
        return self.near(me, dc=rest // (self.z - 1), dz=1 + rest % (self.z - 1))

    def in_plane(self, me, step):
        return self.near(me, dx=step // self.y, dy=step % self.y)

    def spot(self, me, step):
        x, _, _, y = self.digits(me)
        return (x + step // self.y) % self.x * self.y + (y + step % self.y) % self.y

    def given(self, blocks):
        return [blocks[0]] + [
            self.shift(block, dx=dx, dy=dy)
            for block, (dx, dy) in zip(blocks[1:], self.plane[1:])
        ]

    def place(self, triangle, tri_dev, me):
        x, core, z, y = self.digits(triangle // tri_dev)
        mx, mcore, mz, my = self.digits(me)
        dz, dc = (z - mz) % self.z, (core - mcore) % self.core
        block = jnp.where(dz == 0, dc, self.core + dc * (self.z - 1) + dz - 1)
        inside = (x == mx) & (y == my)
        return jnp.where(inside, block * tri_dev + triangle % tri_dev, -1)


class Letter:
    def __init__(self, edges, tri_dev, labels):
        self.edges, self.tri_dev, self.half = edges, tri_dev, -(-tri_dev // 2)
        sizes = [edges, tri_dev, self.half, labels]
        starts = [0]
        for size in sizes:
            starts.append(starts[-1] + -(-size // 128))
        self.starts, self.rows = starts[:4], -(-starts[4] // 8) * 8

    def take(self, letter, part, size):
        first = self.starts[part]
        parts = [letter[first + k : first + k + 1, :] for k in range(-(-size // 128))]
        return jnp.concatenate(parts, axis=1)[:, :size]

    def ends(self, letter):
        pair = self.take(letter, 0, self.edges)
        return pair & 0xFFFF, lax.shift_right_logical(pair, 16)

    def points(self, letter):
        first = self.take(letter, 1, self.tri_dev)
        third = self.take(letter, 2, self.half)
        third = jnp.concatenate([third & 0xFFFF, lax.shift_right_logical(third, 16)], axis=1)
        return jnp.concatenate(
            [first & 0xFFFF, lax.shift_right_logical(first, 16), third[:, : self.tri_dev]], axis=0
        )


def in_rows(row):
    size = row.shape[1]
    if size % 128:
        row = jnp.concatenate([row, jnp.zeros((1, -size % 128), I32)], axis=1)
    return [row[:, k : k + 128] for k in range(0, row.shape[1], 128)]


def letter_kernel(layout, form, slots, inc_ref, points_ref, *refs):
    letter_ref = refs[-1]
    edges, tri_dev, half = form.edges, form.tri_dev, form.half
    ends, devices = 2 * edges, layout.devices
    plus, minus = inc_ref[0:1, :], inc_ref[1:2, :]
    tri = jnp.concatenate([plus, minus], axis=1)
    other = jnp.concatenate([minus, plus], axis=1)
    owner = tri // tri_dev
    hits = iota((devices, ends), 0) == owner
    upper = ones_where(iota((ends, ends), 0) <= iota((ends, ends), 1))
    count = matmul(ones_where(hits), upper)
    rank = jnp.sum(jnp.where(hits, count, 0.0), axis=0, keepdims=True).astype(I32) - 1
    order = ones_where(iota((slots, ends), 0) == rank)
    label = jnp.zeros((devices, slots), I32)
    digits = ((tri % tri_dev + 1, 1), (other & 255, 65536), (other >> 8, 65536 * 256))
    for digit, weight in digits:
        spread = jnp.where(hits, digit.astype(F32), 0.0).astype(BF16)
        label = label + matmul_nt(spread, order).astype(I32) * weight
    third = points_ref[2:3, :]
    if tri_dev % 2:
        third = jnp.concatenate([third, jnp.zeros((1, 1), I32)], axis=1)
    common = (
        in_rows(plus + (minus << 16))
        + in_rows(points_ref[0:1, :] + (points_ref[1:2, :] << 16))
        + in_rows(third[:, :half] + (third[:, half:] << 16))
    )
    places = [(x, y) for x in range(layout.x) for y in range(layout.y)]
    for core in range(layout.core):
        for z in range(layout.z):
            there = [layout.index(x, core, z, y) for x, y in places]
            mine = in_rows(jnp.concatenate([label[d : d + 1, :] for d in there], axis=1))
            blank = form.rows - len(common) - len(mine)
            rows = common + mine + [jnp.zeros((1, 128), I32)] * blank
            letter = jnp.concatenate(rows, axis=0)
            for d in there:
                letter_ref[d] = letter


def letters_of(layout, form, incidence, centroids, slots, after):
    return pl.pallas_call(
        functools.partial(letter_kernel, layout, form, slots),
        in_specs=[whole()] * (2 + len(after)),
        out_specs=whole(),
        out_shape=jax.ShapeDtypeStruct((layout.devices, form.rows, 128), I32),
        compiler_params=PARAMS,
        cost_estimate=cost(1),
    )(incidence, centroids, *after)


def pack_kernel(count, *refs):
    out_ref = refs[-1]
    size = refs[0].shape[0]
    for k in range(count):
        out_ref[k * size : (k + 1) * size, :] = refs[k][...]


def pack(pieces, after):
    size, width = pieces[0].shape
    return pl.pallas_call(
        functools.partial(pack_kernel, len(pieces)),
        in_specs=[whole()] * (len(pieces) + len(after)),
        out_specs=whole(),
        out_shape=jax.ShapeDtypeStruct((len(pieces) * size, width), BF16),
        compiler_params=PARAMS,
        cost_estimate=cost(0.5),
    )(*pieces, *after)


def features(points, scale, first):
    rows, count = points.shape
    square = jnp.sum(points * points, axis=0, keepdims=True)
    norms = [square & 255, square & 0xFF00, square & 0xFF0000]
    ones = [jnp.ones_like(square)] * 3
    zeros = [jnp.zeros((16 - rows - 7, count), I32)]
    if first:
        parts = [-2 * points] + norms + ones + [ones[0]] + zeros
    else:
        parts = [points] + ones + norms + [ones[0]] + zeros
    return (jnp.concatenate(parts, axis=0).astype(F32) * scale).astype(BF16)


def poly(coefs, scale, u):
    value = jnp.full_like(u, coefs[-1] * scale)
    for coef in coefs[-2::-1]:
        value = value * u + coef * scale
    return value


def rows_at(ref, step, rows):
    if ref.shape[0] == rows:
        return ref
    return ref.at[pl.ds(pl.multiple_of(step * rows, rows), rows), :]


def tile_kernel(layout, form, block, first, me_ref, letter_ref, after_ref, *refs):
    real_ref, imag_ref, token_ref, col_ref = refs
    token_ref[...] = jnp.zeros_like(token_ref)
    me, step, size = me_ref[0], pl.program_id(0), form.tri_dev

    @pl.when(step == 0)
    def _():
        for k in range(layout.z * layout.core):
            letter = letter_ref[layout.in_line(me, k)]
            col_ref[:, k * size : (k + 1) * size] = features(form.points(letter), 1.0, False)

    real_ref, imag_ref = [rows_at(ref, step, size) for ref in (real_ref, imag_ref)]
    letter = letter_ref[layout.in_plane(me, first + step)]
    row = features(form.points(letter), 1.0 / (TURNS * TURNS), True)
    for base in range(0, col_ref.shape[1], block):
        cols = slice(base, base + block)
        square = lax.dot_general(
            row, col_ref[:, cols], (((0,), (0,)), ((), ())), preferred_element_type=F32
        )
        inverse = lax.rsqrt(square)
        turns = square * inverse
        frac = turns - ((turns + ROUND) - ROUND)
        u = frac * frac
        real_ref[:, cols] = (poly(COS, SPACING / TURNS, u) * inverse).astype(BF16)
        imag_ref[:, cols] = (poly(SIN, -SPACING / TURNS, u) * (frac * inverse)).astype(BF16)


def build(kernel, outs, rows, span, arrays, time, cols, me, resident, scratch=(), extra=()):
    space = pltpu.VMEM if resident else pltpu.HBM
    block = whole() if resident else pl.BlockSpec((rows, cols), lambda j: (j, 0))
    return pl.pallas_call(
        kernel,
        grid=(len(span),),
        in_specs=[pl.BlockSpec(memory_space=pltpu.SMEM)] + [fixed(array) for array in arrays],
        out_specs=[block] * outs + [fixed(array) for array in extra] + [token_spec()],
        out_shape=[space((len(span) * rows, cols), BF16)] * outs + list(extra) + [TOKEN],
        scratch_shapes=scratch,
        compiler_params=params(resident),
        cost_estimate=cost(time),
    )(me, *arrays)


def pick(row, base, count):
    low = jnp.where((row >= base) & (row < base + count), row - base, -1)
    wanted = iota((count, row.shape[1]), 0).astype(F32).astype(BF16)
    same = wanted == low.astype(F32).astype(BF16)
    return jnp.where(same, jnp.ones((), BF16), jnp.zeros((), BF16))


def adjacency_kernel(layout, tri_dev, first, me_ref, label_ref, after_ref, out_ref, *refs):
    refs[-1][...] = jnp.zeros_like(refs[-1])
    me, step = me_ref[0], pl.program_id(0)
    rows, cols = tri_dev, out_ref.shape[1]
    out_ref = rows_at(out_ref, step, rows)
    label = label_ref[layout.spot(me, first + step)]
    mark = (label & 0xFFFF) - 1
    place = layout.place(lax.shift_right_logical(label, 16), tri_dev, me)
    place = jnp.where(mark >= 0, place, -1)
    low = pick(jnp.where(place >= 0, place % rows, -1), 0, rows)
    for base in range(0, cols, rows):
        inside = (place >= base) & (place < base + rows)
        here = pick(jnp.where(inside, mark, -1), 0, rows)
        out_ref[:, base : base + rows] = matmul_nt(here, low).astype(BF16)
    if first == 0:

        @pl.when(step == 0)
        def _():
            every = pick(mark, 0, rows)
            refs[0][...] = matmul(every, jnp.ones((every.shape[1], 128), BF16))


def incidence_kernel(layout, form, me_ref, letter_ref, after_ref, out_ref, token_ref):
    token_ref[...] = jnp.zeros_like(token_ref)
    me, step = me_ref[0], pl.program_id(0)
    edges, cols = form.edges, out_ref.shape[1]
    out_ref = rows_at(out_ref, step, edges)
    size = form.tri_dev
    letter = letter_ref[layout.in_plane(me, step)]
    plus, minus = [layout.place(end, size, me) for end in form.ends(letter)]
    eye = ones_where(iota((edges, edges), 0) == iota((edges, edges), 1))
    for base in range(0, cols, size):
        signed = pick(plus, base, size) - pick(minus, base, size)
        out_ref[:, base : base + size] = matmul_nt(eye, signed).astype(BF16)


def set_blocks(value, outs):
    for k, out in enumerate(outs):

        @pl.when(pl.program_id(0) == k)
        def _(out=out):
            out[...] = value.astype(out.dtype)


def blocks_like(count, rows, width, exact):
    return [
        jax.ShapeDtypeStruct((rows, width), F32 if exact and k == 0 else BF16)
        for k in range(count)
    ]


def first_kernel(layout, form, me_ref, letter_ref, *refs):
    count = len(layout.plane)
    pieces, outs, token_ref = refs[: -count - 1], refs[-count - 1 : -1], refs[-1]
    token_ref[...] = jnp.zeros_like(token_ref)
    me, size, edges = me_ref[0], form.tri_dev, form.edges
    base = layout.in_plane(me, pl.program_id(0)) * size
    total, k = None, 0
    for piece in pieces:
        for row in range(0, piece.shape[0], edges):
            plus, minus = form.ends(letter_ref[layout.in_line(me, k)])
            signed = pick(plus, base, size) - pick(minus, base, size)
            term = matmul(signed, piece[row : row + edges, :])
            total = term if total is None else total + term
            k += 1
    set_blocks(total, outs)


def first_charges(layout, form, me, letters, pieces, resident):
    count, width = len(layout.plane), pieces[0].shape[1]
    shapes = blocks_like(count, form.tri_dev, width, True) + [TOKEN]
    return pl.pallas_call(
        functools.partial(first_kernel, layout, form),
        grid=(count,),
        in_specs=[pl.BlockSpec(memory_space=pltpu.SMEM), fixed(letters)]
        + [fixed(piece) for piece in pieces],
        out_specs=[fixed(shape) for shape in shapes],
        out_shape=shapes,
        compiler_params=params(resident),
        cost_estimate=cost(4),
    )(me, letters, *pieces)


def apply_kernel(mats, fed, block, *refs):
    matrices, pieces, outs = refs[:mats], refs[mats : mats + fed], refs[mats + fed : -1]
    refs[-1][...] = jnp.zeros_like(refs[-1])
    half = pieces[0].shape[1] // 2
    sums = []
    for matrix in matrices:
        matrix = rows_at(matrix, pl.program_id(0), block)
        total, col = None, 0
        for piece in pieces:
            size = piece.shape[0]
            term = matmul(matrix[:, col : col + size], piece[...])
            total = term if total is None else total + term
            col += size
        sums.append(total)
    value = sums[0]
    if mats == 2:
        real, imag = sums
        value = jnp.concatenate(
            [real[:, :half] - imag[:, half:], real[:, half:] + imag[:, :half]], axis=1
        )
    set_blocks(value, outs)


def apply(matrices, pieces, block, resident, exact, after):
    rows, cols = matrices[0].shape
    count, mats = rows // block, len(matrices)
    shapes = blocks_like(count, block, pieces[0].shape[1], exact) + [TOKEN]
    spec = whole() if resident else pl.BlockSpec((block, cols), lambda j: (j, 0))

    def kernel(*refs):
        fed = len(refs) - len(shapes) - len(after)
        apply_kernel(mats, fed - mats, block, *refs[:fed], *refs[fed + len(after) :])

    return pl.pallas_call(
        kernel,
        grid=(count,),
        in_specs=[spec] * mats
        + [fixed(piece) for piece in pieces]
        + [token_spec()] * len(after),
        out_specs=[fixed(shape) for shape in shapes],
        out_shape=shapes,
        compiler_params=params(resident),
        cost_estimate=cost(count * mats / 2),
    )(*matrices, *pieces, *after)


def multiply(parts, pieces, block, resident, after=()):
    blocks, token = [], None
    for part in parts:
        *more, token = apply(part, pieces, block, resident, not blocks, after)
        blocks += more
    return blocks, token


def sum_kernel(count, own_ref, *refs):
    total = own_ref[...]
    for ref in refs[:count]:
        total = total + ref[...].astype(F32)
    out_ref, rounded_ref, token_ref = refs[-3:]
    out_ref[...] = total
    rounded_ref[...] = total.astype(BF16)
    token_ref[...] = jnp.zeros_like(token_ref)


def sum_of(blocks, after):
    shape = blocks[0].shape
    return pl.pallas_call(
        functools.partial(sum_kernel, len(blocks) - 1),
        in_specs=[whole()] * (len(blocks) + len(after)),
        out_specs=[whole()] * 3,
        out_shape=[
            jax.ShapeDtypeStruct(shape, F32),
            jax.ShapeDtypeStruct(shape, BF16),
            TOKEN,
        ],
        compiler_params=PARAMS,
        cost_estimate=cost(1),
    )(*blocks, *after)


def potential_kernel(count, summed, weight_ref, own_ref, *refs):
    total = own_ref[...]
    for ref in refs[:count]:
        total = total + ref[...].astype(F32)
    out_ref, sum_ref, rounded_ref, token_ref = refs[-4:]
    potential = total.astype(BF16)
    out_ref[...] = potential
    value = weight_ref[0] * potential.astype(F32)
    if summed:
        value = value + refs[count][...]
    sum_ref[...] = value
    rounded_ref[...] = value.astype(BF16)
    token_ref[...] = jnp.zeros_like(token_ref)


def potential_of(weight, blocks, summed, after):
    shape = blocks[0].shape
    return pl.pallas_call(
        functools.partial(potential_kernel, len(blocks) - 1, len(summed)),
        in_specs=[pl.BlockSpec(memory_space=pltpu.SMEM)]
        + [whole()] * (len(blocks) + len(summed) + len(after)),
        out_specs=[whole()] * 4,
        out_shape=[
            jax.ShapeDtypeStruct(shape, BF16),
            jax.ShapeDtypeStruct(shape, F32),
            jax.ShapeDtypeStruct(shape, BF16),
            TOKEN,
        ],
        compiler_params=PARAMS,
        cost_estimate=cost(1),
    )(weight, *blocks, *summed, *after)


def charge_kernel(count, weight_ref, charge_ref, degree_ref, potential_ref, own_ref, *refs):
    around = own_ref[...]
    for ref in refs[:count]:
        around = around + ref[...].astype(F32)
    out_ref, rounded_ref, token_ref = refs[-3:]
    token_ref[...] = jnp.zeros_like(token_ref)
    change = degree_ref[:, 0:1] * potential_ref[...].astype(F32) - around
    value = charge_ref[...] - weight_ref[0] * change
    out_ref[...] = value
    rounded_ref[...] = value.astype(BF16)


def charge_of(weight, charge, degree, potential, blocks, after):
    return pl.pallas_call(
        functools.partial(charge_kernel, len(blocks) - 1),
        in_specs=[pl.BlockSpec(memory_space=pltpu.SMEM)] + [whole()] * (3 + len(blocks) + len(after)),
        out_specs=[whole()] * 3,
        out_shape=[
            jax.ShapeDtypeStruct(charge.shape, F32),
            jax.ShapeDtypeStruct(charge.shape, BF16),
            TOKEN,
        ],
        compiler_params=PARAMS,
        cost_estimate=cost(1),
    )(weight, charge, degree, potential, *blocks, *after)


def current_kernel(count, current_ref, own_ref, *refs):
    change = own_ref[...]
    for ref in refs[:count]:
        change = change + ref[...].astype(F32)
    refs[-1][...] = (current_ref[...].astype(F32) - change).astype(BF16)


def current_of(current, blocks):
    return pl.pallas_call(
        functools.partial(current_kernel, len(blocks) - 1),
        in_specs=[whole()] * (1 + len(blocks)),
        out_specs=whole(),
        out_shape=jax.ShapeDtypeStruct(current.shape, BF16),
        compiler_params=PARAMS,
        cost_estimate=cost(1),
    )(current, *blocks)


def per_device(layout, currents, incidence, centroids, sweep_weights):
    me = lax.axis_index(AXES).astype(I32).reshape(1)
    tri_dev = centroids.shape[1]
    edge_dev = currents.shape[0]
    devices, count = layout.devices, len(layout.plane)
    slots = 8 * tri_dev // devices
    sweeps = sweep_weights.shape[0]
    cols = layout.z * layout.core * tri_dev

    resident = count * (3 * tri_dev + edge_dev) * cols * 2 <= 24 * 2**20

    own = layout.by_core(currents)
    form = Letter(edge_dev, tri_dev, count * slots)
    letters = letters_of(
        layout, form, incidence, centroids, slots, ()
    )
    letters = lax.all_to_all(letters, AXES, split_axis=0, concat_axis=0, tiled=True)
    labels = letters[:, form.starts[3] :, :].reshape(devices, -1)[:, : count * slots]
    labels = labels.reshape(devices, count, slots).transpose(1, 0, 2)
    labels = labels.reshape(count, 1, devices * slots)

    make = functools.partial(build, cols=cols, me=me, resident=resident)
    cut = (count + 1) // 2
    spans = [span for span in (range(cut), range(cut, count)) if span]

    def tile_part(span, token):
        *part, token = make(
            functools.partial(tile_kernel, layout, form, min(512, cols), span[0]),
            2,
            tri_dev,
            span,
            (letters, token),
            6,
            scratch=[pltpu.VMEM((16, cols), BF16)],
        )
        return part, token

    def adjacency_part(span, token):
        extra = () if span[0] else (jax.ShapeDtypeStruct((tri_dev, 128), F32),)
        *part, token = make(
            functools.partial(adjacency_kernel, layout, tri_dev, span[0]),
            1,
            tri_dev,
            span,
            (labels, token),
            6,
            extra=extra,
        )
        return part, token

    pieces = layout.gathered(currents, (), own)
    *blocks, token = first_charges(layout, form, me, letters, pieces, resident)
    part, token = tile_part(spans[0], token)
    tiles = [part]
    charge, rounded, token = sum_of(layout.given(blocks), (token,))
    for span in spans[1:]:
        part, token = tile_part(span, token)
        tiles.append(part)

    def incidence_part(token):
        *part, token = make(
            functools.partial(incidence_kernel, layout, form),
            1,
            edge_dev,
            range(count),
            (letters, token),
            6,
        )
        return part, token

    near, ends = [], None
    summed, potential = (), None
    for sweep in range(sweeps):
        weight = sweep_weights[sweep].reshape(1)
        pieces = layout.gathered(rounded, (token,))
        blocks, token = multiply(tiles, pieces, tri_dev, resident)
        last = sweep + 1 == sweeps
        if not near and not last:
            (part, degree), token = adjacency_part(spans[0], token)
            near.append([part])
        potential, *summed, weighted, token = potential_of(
            weight, layout.given(blocks), summed, (token,)
        )
        if last:
            break
        for span in spans[len(near) :]:
            part, token = adjacency_part(span, token)
            near.append(part)
        pieces = layout.gathered(potential, (token,))
        blocks, token = multiply(near, pieces, tri_dev, resident)
        if ends is None:
            ends, token = incidence_part(token)
        charge, rounded, token = charge_of(
            weight, charge, degree, potential, layout.given(blocks), (token,)
        )
    if ends is None:
        ends, token = incidence_part(token)
    pieces = layout.gathered(weighted, (token,))
    blocks, _ = multiply([ends], pieces, edge_dev, resident)
    return current_of(currents, layout.given(blocks)), potential


def solution(mesh):
    layout = Layout(mesh.shape["row"], mesh.shape["col"])
    in_specs = (P(AXES, None), P(None, AXES), P(None, AXES), P())
    out_specs = (P(AXES, None), P(AXES, None))
    return jax.shard_map(
        functools.partial(per_device, layout),
        mesh=mesh,
        in_specs=in_specs,
        out_specs=out_specs,
        check_vma=False,
    )
```

```python
import functools
import math

import jax
import jax.numpy as jnp
from jax import lax
from jax.experimental import pallas as pl
from jax.experimental.pallas import tpu as pltpu
from jax.sharding import PartitionSpec as P

SPACING = 0.2
TURNS = 32.0
AXES = ("row", "col")
ROUND = 12582912.0
COS = (
    0.9999992107823218,
    -19.738980355763992,
    64.92865742103312,
    -85.27162153429882,
    58.79049212013072,
    -21.07110562764302,
)
SIN = (
    6.283184916495431,
    -41.34158923268858,
    81.59994332978287,
    -76.61447253124996,
    41.342882354568324,
    -12.471243535026977,
)
SMALL, LARGE = 10 * 2**20, 24 * 2**20
PARAMS = pltpu.CompilerParams(vmem_limit_bytes=SMALL)
PEAK = 1.15e15
F32, BF16, I32 = jnp.float32, jnp.bfloat16, jnp.int32


def whole():
    return pl.BlockSpec(memory_space=pltpu.VMEM)


def fixed(array):
    return pl.BlockSpec(array.shape, lambda j: (0,) * len(array.shape))


def params(resident):
    return pltpu.CompilerParams(vmem_limit_bytes=SMALL if resident else LARGE)


def cost(microseconds):
    return pl.CostEstimate(
        flops=int(microseconds * 1e-6 * PEAK), bytes_accessed=0, transcendentals=0
    )


TOKEN = jax.ShapeDtypeStruct((8, 128), F32)


def token_spec():
    return pl.BlockSpec((8, 128), lambda *_: (0, 0))


def iota(shape, dim):
    return lax.broadcasted_iota(I32, shape, dim)


def ones_where(mask):
    return jnp.where(mask, jnp.ones((), F32), jnp.zeros((), F32)).astype(BF16)


def matmul(a, b):
    return jnp.dot(a, b, preferred_element_type=F32)


def matmul_nt(a, b):
    return lax.dot_general(a, b, (((1,), (1,)), ((), ())), preferred_element_type=F32)


class Layout:
    def __init__(self, n_row, n_col):
        self.core = 2 if n_row % 2 == 0 else 1
        self.x = n_row // self.core
        self.y = math.gcd(n_col, self.x)
        self.z = n_col // self.y
        self.devices = n_row * n_col
        self.plane = [(dx, dy) for dx in range(self.x) for dy in range(self.y)]

    def digits(self, index):
        y = index % self.y
        z = index // self.y % self.z
        core = index // (self.y * self.z) % self.core
        return index // (self.y * self.z * self.core), core, z, y

    def shift(self, value, dx=0, dc=0, dz=0, dy=0):
        pairs = []
        for i in range(self.devices):
            pairs.append((i, self.near(i, dx, dc, dz, dy)))
        return lax.ppermute(value, AXES, pairs)

    def by_core(self, value):
        return [value] + [self.shift(value, dc=-dc) for dc in range(1, self.core)]

    def along(self, value):
        return [self.shift(value, dz=-dz) for dz in range(1, self.z)]

    def gathered(self, value, after, along=None):
        along = self.along(value) if along is None else along
        return self.by_core(value) + (self.by_core(pack(along, after)) if along else [])

    def index(self, x, core, z, y):
        x, core, z, y = x % self.x, core % self.core, z % self.z, y % self.y
        return ((x * self.core + core) * self.z + z) * self.y + y

    def near(self, me, dx=0, dc=0, dz=0, dy=0):
        x, core, z, y = self.digits(me)
        return self.index(x + dx, core + dc, z + dz, y + dy)

    def in_line(self, me, k):
        if k < self.core:
            return self.near(me, dc=k)
        rest = k - self.core
        return self.near(me, dc=rest // (self.z - 1), dz=1 + rest % (self.z - 1))

    def in_plane(self, me, step):
        return self.near(me, dx=step // self.y, dy=step % self.y)

    def spot(self, me, step):
        x, _, _, y = self.digits(me)
        return (x + step // self.y) % self.x * self.y + (y + step % self.y) % self.y

    def given(self, blocks):
        return [blocks[0]] + [
            self.shift(block, dx=dx, dy=dy)
            for block, (dx, dy) in zip(blocks[1:], self.plane[1:])
        ]

    def place(self, triangle, tri_dev, me):
        x, core, z, y = self.digits(triangle // tri_dev)
        mx, mcore, mz, my = self.digits(me)
        dz, dc = (z - mz) % self.z, (core - mcore) % self.core
        block = jnp.where(dz == 0, dc, self.core + dc * (self.z - 1) + dz - 1)
        inside = (x == mx) & (y == my)
        return jnp.where(inside, block * tri_dev + triangle % tri_dev, -1)


class Letter:
    def __init__(self, edges, tri_dev, labels):
        self.edges, self.tri_dev, self.half = edges, tri_dev, -(-tri_dev // 2)
        sizes = [edges, tri_dev, self.half, labels]
        starts = [0]
        for size in sizes:
            starts.append(starts[-1] + -(-size // 128))
        self.starts, self.rows = starts[:4], -(-starts[4] // 8) * 8

    def take(self, letter, part, size):
        first = self.starts[part]
        parts = [letter[first + k : first + k + 1, :] for k in range(-(-size // 128))]
        return jnp.concatenate(parts, axis=1)[:, :size]

    def ends(self, letter):
        pair = self.take(letter, 0, self.edges)
        return pair & 0xFFFF, lax.shift_right_logical(pair, 16)

    def points(self, letter):
        first = self.take(letter, 1, self.tri_dev)
        third = self.take(letter, 2, self.half)
        third = jnp.concatenate([third & 0xFFFF, lax.shift_right_logical(third, 16)], axis=1)
        return jnp.concatenate(
            [first & 0xFFFF, lax.shift_right_logical(first, 16), third[:, : self.tri_dev]], axis=0
        )


def in_rows(row):
    size = row.shape[1]
    if size % 128:
        row = jnp.concatenate([row, jnp.zeros((1, -size % 128), I32)], axis=1)
    return [row[:, k : k + 128] for k in range(0, row.shape[1], 128)]


def letter_kernel(layout, form, slots, inc_ref, points_ref, *refs):
    letter_ref = refs[-1]
    edges, tri_dev, half = form.edges, form.tri_dev, form.half
    ends, devices = 2 * edges, layout.devices
    plus, minus = inc_ref[0:1, :], inc_ref[1:2, :]
    tri = jnp.concatenate([plus, minus], axis=1)
    other = jnp.concatenate([minus, plus], axis=1)
    owner = tri // tri_dev
    hits = iota((devices, ends), 0) == owner
    upper = ones_where(iota((ends, ends), 0) <= iota((ends, ends), 1))
    count = matmul(ones_where(hits), upper)
    rank = jnp.sum(jnp.where(hits, count, 0.0), axis=0, keepdims=True).astype(I32) - 1
    order = ones_where(iota((slots, ends), 0) == rank)
    label = jnp.zeros((devices, slots), I32)
    digits = ((tri % tri_dev + 1, 1), (other & 255, 65536), (other >> 8, 65536 * 256))
    for digit, weight in digits:
        spread = jnp.where(hits, digit.astype(F32), 0.0).astype(BF16)
        label = label + matmul_nt(spread, order).astype(I32) * weight
    third = points_ref[2:3, :]
    if tri_dev % 2:
        third = jnp.concatenate([third, jnp.zeros((1, 1), I32)], axis=1)
    common = (
        in_rows(plus + (minus << 16))
        + in_rows(points_ref[0:1, :] + (points_ref[1:2, :] << 16))
        + in_rows(third[:, :half] + (third[:, half:] << 16))
    )
    places = [(x, y) for x in range(layout.x) for y in range(layout.y)]
    for core in range(layout.core):
        for z in range(layout.z):
            there = [layout.index(x, core, z, y) for x, y in places]
            mine = in_rows(jnp.concatenate([label[d : d + 1, :] for d in there], axis=1))
            blank = form.rows - len(common) - len(mine)
            rows = common + mine + [jnp.zeros((1, 128), I32)] * blank
            letter = jnp.concatenate(rows, axis=0)
            for d in there:
                letter_ref[d] = letter


def letters_of(layout, form, incidence, centroids, slots, after):
    return pl.pallas_call(
        functools.partial(letter_kernel, layout, form, slots),
        in_specs=[whole()] * (2 + len(after)),
        out_specs=whole(),
        out_shape=jax.ShapeDtypeStruct((layout.devices, form.rows, 128), I32),
        compiler_params=PARAMS,
        cost_estimate=cost(1),
    )(incidence, centroids, *after)


def pack_kernel(count, *refs):
    out_ref = refs[-1]
    size = refs[0].shape[0]
    for k in range(count):
        out_ref[k * size : (k + 1) * size, :] = refs[k][...]


def pack(pieces, after):
    size, width = pieces[0].shape
    return pl.pallas_call(
        functools.partial(pack_kernel, len(pieces)),
        in_specs=[whole()] * (len(pieces) + len(after)),
        out_specs=whole(),
        out_shape=jax.ShapeDtypeStruct((len(pieces) * size, width), BF16),
        compiler_params=PARAMS,
        cost_estimate=cost(0.5),
    )(*pieces, *after)


def features(points, scale, first):
    rows, count = points.shape
    square = jnp.sum(points * points, axis=0, keepdims=True)
    norms = [square & 255, square & 0xFF00, square & 0xFF0000]
    ones = [jnp.ones_like(square)] * 3
    zeros = [jnp.zeros((16 - rows - 7, count), I32)]
    if first:
        parts = [-2 * points] + norms + ones + [ones[0]] + zeros
    else:
        parts = [points] + ones + norms + [ones[0]] + zeros
    return (jnp.concatenate(parts, axis=0).astype(F32) * scale).astype(BF16)


def poly(coefs, scale, u):
    value = jnp.full_like(u, coefs[-1] * scale)
    for coef in coefs[-2::-1]:
        value = value * u + coef * scale
    return value


def rows_at(ref, step, rows):
    if ref.shape[0] == rows:
        return ref
    return ref.at[pl.ds(pl.multiple_of(step * rows, rows), rows), :]


def tile_kernel(layout, form, block, first, me_ref, letter_ref, after_ref, *refs):
    real_ref, imag_ref, token_ref, col_ref = refs
    token_ref[...] = jnp.zeros_like(token_ref)
    me, step, size = me_ref[0], pl.program_id(0), form.tri_dev

    @pl.when(step == 0)
    def _():
        for k in range(layout.z * layout.core):
            letter = letter_ref[layout.in_line(me, k)]
            col_ref[:, k * size : (k + 1) * size] = features(form.points(letter), 1.0, False)

    real_ref, imag_ref = [rows_at(ref, step, size) for ref in (real_ref, imag_ref)]
    letter = letter_ref[layout.in_plane(me, first + step)]
    row = features(form.points(letter), 1.0 / (TURNS * TURNS), True)
    for base in range(0, col_ref.shape[1], block):
        cols = slice(base, base + block)
        square = lax.dot_general(
            row, col_ref[:, cols], (((0,), (0,)), ((), ())), preferred_element_type=F32
        )
        inverse = lax.rsqrt(square)
        turns = square * inverse
        frac = turns - ((turns + ROUND) - ROUND)
        u = frac * frac
        real_ref[:, cols] = (poly(COS, SPACING / TURNS, u) * inverse).astype(BF16)
        imag_ref[:, cols] = (poly(SIN, -SPACING / TURNS, u) * (frac * inverse)).astype(BF16)


def build(
    kernel, outs, rows, span, arrays, time, cols, me, resident=False, scratch=(), extra=()
):
    space = pltpu.VMEM if resident else pltpu.HBM
    block = whole() if resident else pl.BlockSpec((rows, cols), lambda j: (j, 0))
    return pl.pallas_call(
        kernel,
        grid=(len(span),),
        in_specs=[pl.BlockSpec(memory_space=pltpu.SMEM)] + [fixed(array) for array in arrays],
        out_specs=[block] * outs + [fixed(array) for array in extra] + [token_spec()],
        out_shape=[space((len(span) * rows, cols), BF16)] * outs + list(extra) + [TOKEN],
        scratch_shapes=scratch,
        compiler_params=params(resident),
        cost_estimate=cost(time),
    )(me, *arrays)


def pick(row, base, count):
    low = jnp.where((row >= base) & (row < base + count), row - base, -1)
    wanted = iota((count, row.shape[1]), 0).astype(F32).astype(BF16)
    same = wanted == low.astype(F32).astype(BF16)
    return jnp.where(same, jnp.ones((), BF16), jnp.zeros((), BF16))


def adjacency_kernel(layout, tri_dev, first, me_ref, label_ref, after_ref, out_ref, *refs):
    refs[-1][...] = jnp.zeros_like(refs[-1])
    me, step = me_ref[0], pl.program_id(0)
    rows, cols = tri_dev, out_ref.shape[1]
    out_ref = rows_at(out_ref, step, rows)
    label = label_ref[layout.spot(me, first + step)]
    mark = (label & 0xFFFF) - 1
    place = layout.place(lax.shift_right_logical(label, 16), tri_dev, me)
    place = jnp.where(mark >= 0, place, -1)
    low = pick(jnp.where(place >= 0, place % rows, -1), 0, rows)
    for base in range(0, cols, rows):
        inside = (place >= base) & (place < base + rows)
        here = pick(jnp.where(inside, mark, -1), 0, rows)
        out_ref[:, base : base + rows] = matmul_nt(here, low).astype(BF16)
    if first == 0:

        @pl.when(step == 0)
        def _():
            every = pick(mark, 0, rows)
            refs[0][...] = matmul(every, jnp.ones((every.shape[1], 128), BF16))


def incidence_kernel(layout, form, first, me_ref, letter_ref, after_ref, out_ref, token_ref):
    token_ref[...] = jnp.zeros_like(token_ref)
    me, step = me_ref[0], pl.program_id(0)
    edges, cols = form.edges, out_ref.shape[1]
    out_ref = rows_at(out_ref, step, edges)
    size = form.tri_dev
    letter = letter_ref[layout.in_plane(me, first + step)]
    plus, minus = [layout.place(end, size, me) for end in form.ends(letter)]
    eye = ones_where(iota((edges, edges), 0) == iota((edges, edges), 1))
    for base in range(0, cols, size):
        signed = pick(plus, base, size) - pick(minus, base, size)
        out_ref[:, base : base + size] = matmul_nt(eye, signed).astype(BF16)


def set_blocks(value, outs):
    for k, out in enumerate(outs):

        @pl.when(pl.program_id(0) == k)
        def _(out=out):
            out[...] = value.astype(out.dtype)


def blocks_like(count, rows, width, exact):
    return [
        jax.ShapeDtypeStruct((rows, width), F32 if exact and k == 0 else BF16)
        for k in range(count)
    ]


def first_kernel(layout, form, me_ref, letter_ref, *refs):
    count = len(layout.plane)
    pieces, outs, token_ref = refs[: -count - 1], refs[-count - 1 : -1], refs[-1]
    token_ref[...] = jnp.zeros_like(token_ref)
    me, size, edges = me_ref[0], form.tri_dev, form.edges
    base = layout.in_plane(me, pl.program_id(0)) * size
    total, k = None, 0
    for piece in pieces:
        for row in range(0, piece.shape[0], edges):
            plus, minus = form.ends(letter_ref[layout.in_line(me, k)])
            signed = pick(plus, base, size) - pick(minus, base, size)
            term = matmul(signed, piece[row : row + edges, :])
            total = term if total is None else total + term
            k += 1
    set_blocks(total, outs)


def first_charges(layout, form, me, letters, pieces, resident):
    count, width = len(layout.plane), pieces[0].shape[1]
    shapes = blocks_like(count, form.tri_dev, width, True) + [TOKEN]
    return pl.pallas_call(
        functools.partial(first_kernel, layout, form),
        grid=(count,),
        in_specs=[pl.BlockSpec(memory_space=pltpu.SMEM)] + [whole()] * (1 + len(pieces)),
        out_specs=[whole()] * len(shapes),
        out_shape=shapes,
        compiler_params=params(resident),
        cost_estimate=cost(4),
    )(me, letters, *pieces)


def apply_kernel(mats, fed, block, row, *refs):
    matrices, pieces, outs = refs[:mats], refs[mats : mats + fed], refs[mats + fed : -1]
    refs[-1][...] = jnp.zeros_like(refs[-1])
    half = pieces[0].shape[1] // 2
    sums = []
    for matrix in matrices:
        total, col = None, 0
        for piece in pieces:
            size = piece.shape[0]
            term = matmul(matrix[row : row + block, col : col + size], piece[...])
            total = term if total is None else total + term
            col += size
        sums.append(total)
    value = sums[0]
    if mats == 2:
        real, imag = sums
        value = jnp.concatenate(
            [real[:, :half] - imag[:, half:], real[:, half:] + imag[:, :half]], axis=1
        )
    set_blocks(value, outs)


def apply(matrices, pieces, block, exact, row=None):
    rows, cols = matrices[0].shape
    count, mats = rows // block if row is None else 1, len(matrices)
    spec = pl.BlockSpec((block, cols), lambda j: (j, 0)) if row is None else whole()
    shapes = blocks_like(count, block, pieces[0].shape[1], exact) + [TOKEN]
    return pl.pallas_call(
        functools.partial(apply_kernel, mats, len(pieces), block, row or 0),
        grid=(count,),
        in_specs=[spec] * mats + [whole()] * len(pieces),
        out_specs=[whole()] * len(shapes),
        out_shape=shapes,
        compiler_params=params(row is not None),
        cost_estimate=cost(count * mats / 2),
    )(*matrices, *pieces)


def multiply(parts, pieces, block, resident=False):
    blocks, token = [], None
    for part in parts:
        for row in range(0, part[0].shape[0], block) if resident else [None]:
            *more, token = apply(part, pieces, block, not blocks, row)
            blocks += more
    return blocks, token


def sum_kernel(count, own_ref, *refs):
    total = own_ref[...]
    for ref in refs[:count]:
        total = total + ref[...].astype(F32)
    out_ref, rounded_ref, token_ref = refs[-3:]
    out_ref[...] = total
    rounded_ref[...] = total.astype(BF16)
    token_ref[...] = jnp.zeros_like(token_ref)


def sum_of(blocks, after):
    shape = blocks[0].shape
    return pl.pallas_call(
        functools.partial(sum_kernel, len(blocks) - 1),
        in_specs=[whole()] * (len(blocks) + len(after)),
        out_specs=[whole()] * 3,
        out_shape=[
            jax.ShapeDtypeStruct(shape, F32),
            jax.ShapeDtypeStruct(shape, BF16),
            TOKEN,
        ],
        compiler_params=PARAMS,
        cost_estimate=cost(1),
    )(*blocks, *after)


def potential_kernel(count, summed, weight_ref, own_ref, *refs):
    total = own_ref[...]
    for ref in refs[:count]:
        total = total + ref[...].astype(F32)
    out_ref, sum_ref, rounded_ref, token_ref = refs[-4:]
    potential = total.astype(BF16)
    out_ref[...] = potential
    value = weight_ref[0] * potential.astype(F32)
    if summed:
        value = value + refs[count][...]
    sum_ref[...] = value
    rounded_ref[...] = value.astype(BF16)
    token_ref[...] = jnp.zeros_like(token_ref)


def potential_of(weight, blocks, summed, after):
    shape = blocks[0].shape
    return pl.pallas_call(
        functools.partial(potential_kernel, len(blocks) - 1, len(summed)),
        in_specs=[pl.BlockSpec(memory_space=pltpu.SMEM)]
        + [whole()] * (len(blocks) + len(summed) + len(after)),
        out_specs=[whole()] * 4,
        out_shape=[
            jax.ShapeDtypeStruct(shape, BF16),
            jax.ShapeDtypeStruct(shape, F32),
            jax.ShapeDtypeStruct(shape, BF16),
            TOKEN,
        ],
        compiler_params=PARAMS,
        cost_estimate=cost(1),
    )(weight, *blocks, *summed, *after)


def charge_kernel(count, weight_ref, charge_ref, degree_ref, potential_ref, own_ref, *refs):
    around = own_ref[...]
    for ref in refs[:count]:
        around = around + ref[...].astype(F32)
    out_ref, rounded_ref, token_ref = refs[-3:]
    token_ref[...] = jnp.zeros_like(token_ref)
    change = degree_ref[:, 0:1] * potential_ref[...].astype(F32) - around
    value = charge_ref[...] - weight_ref[0] * change
    out_ref[...] = value
    rounded_ref[...] = value.astype(BF16)


def charge_of(weight, charge, degree, potential, blocks, after):
    return pl.pallas_call(
        functools.partial(charge_kernel, len(blocks) - 1),
        in_specs=[pl.BlockSpec(memory_space=pltpu.SMEM)] + [whole()] * (3 + len(blocks) + len(after)),
        out_specs=[whole()] * 3,
        out_shape=[
            jax.ShapeDtypeStruct(charge.shape, F32),
            jax.ShapeDtypeStruct(charge.shape, BF16),
            TOKEN,
        ],
        compiler_params=PARAMS,
        cost_estimate=cost(1),
    )(weight, charge, degree, potential, *blocks, *after)


def current_kernel(count, current_ref, own_ref, *refs):
    change = own_ref[...]
    for ref in refs[:count]:
        change = change + ref[...].astype(F32)
    refs[-1][...] = (current_ref[...].astype(F32) - change).astype(BF16)


def current_of(current, blocks):
    return pl.pallas_call(
        functools.partial(current_kernel, len(blocks) - 1),
        in_specs=[whole()] * (1 + len(blocks)),
        out_specs=whole(),
        out_shape=jax.ShapeDtypeStruct(current.shape, BF16),
        compiler_params=PARAMS,
        cost_estimate=cost(1),
    )(current, *blocks)


def per_device(layout, currents, incidence, centroids, sweep_weights):
    me = lax.axis_index(AXES).astype(I32).reshape(1)
    tri_dev = centroids.shape[1]
    edge_dev = currents.shape[0]
    devices, count = layout.devices, len(layout.plane)
    slots = 8 * tri_dev // devices
    sweeps = sweep_weights.shape[0]
    cols = layout.z * layout.core * tri_dev

    resident = count * 2 * tri_dev * cols * 2 <= 16 * 2**20

    along = layout.along(currents)
    form = Letter(edge_dev, tri_dev, count * slots)
    letters = letters_of(
        layout, form, incidence, centroids, slots, along[-1:]
    )
    letters = lax.all_to_all(letters, AXES, split_axis=0, concat_axis=0, tiled=True)
    labels = letters[:, form.starts[3] :, :].reshape(devices, -1)[:, : count * slots]
    labels = labels.reshape(devices, count, slots).transpose(1, 0, 2)
    labels = labels.reshape(count, 1, devices * slots)

    make = functools.partial(build, cols=cols, me=me)
    cut = (count + 1) // 2
    spans = [span for span in (range(cut), range(cut, count)) if span]

    def tile_part(span, token):
        *part, token = make(
            functools.partial(tile_kernel, layout, form, min(512, cols), span[0]),
            2,
            tri_dev,
            span,
            (letters, token),
            6,
            resident=resident,
            scratch=[pltpu.VMEM((16, cols), BF16)],
        )
        return part, token

    def adjacency_part(span, token):
        extra = () if span[0] else (jax.ShapeDtypeStruct((tri_dev, 128), F32),)
        *part, token = make(
            functools.partial(adjacency_kernel, layout, tri_dev, span[0]),
            1,
            tri_dev,
            span,
            (labels, token),
            6,
            extra=extra,
        )
        return part, token

    pieces = layout.gathered(currents, (letters,), along)
    *blocks, token = first_charges(layout, form, me, letters, pieces, resident)
    part, token = tile_part(spans[0], token)
    tiles = [part]
    charge, rounded, token = sum_of(layout.given(blocks), (token,))
    for span in spans[1:]:
        part, token = tile_part(span, token)
        tiles.append(part)

    def incidence_parts(token):
        parts = []
        for span in spans:
            *part, token = make(
                functools.partial(incidence_kernel, layout, form, span[0]),
                1,
                edge_dev,
                span,
                (letters, token),
                3,
            )
            parts.append(part)
        return parts, token

    near, ends = [], None
    summed, potential = (), None
    for sweep in range(sweeps):
        weight = sweep_weights[sweep].reshape(1)
        pieces = layout.gathered(rounded, (token,))
        blocks, token = multiply(tiles, pieces, tri_dev, resident)
        last = sweep + 1 == sweeps
        if not near and not last:
            (part, degree), token = adjacency_part(spans[0], token)
            near.append([part])
        potential, *summed, weighted, token = potential_of(
            weight, layout.given(blocks), summed, (token,)
        )
        if last:
            break
        for span in spans[len(near) :]:
            part, token = adjacency_part(span, token)
            near.append(part)
        pieces = layout.gathered(potential, (token,))
        blocks, token = multiply(near, pieces, tri_dev)
        if ends is None:
            ends, token = incidence_parts(token)
        charge, rounded, token = charge_of(
            weight, charge, degree, potential, layout.given(blocks), (token,)
        )
    if ends is None:
        ends, token = incidence_parts(token)
    pieces = layout.gathered(weighted, (token,))
    blocks, _ = multiply(ends, pieces, edge_dev)
    return current_of(currents, layout.given(blocks)), potential


def solution(mesh):
    layout = Layout(mesh.shape["row"], mesh.shape["col"])
    in_specs = (P(AXES, None), P(None, AXES), P(None, AXES), P())
    out_specs = (P(AXES, None), P(AXES, None))
    return jax.shard_map(
        functools.partial(per_device, layout),
        mesh=mesh,
        in_specs=in_specs,
        out_specs=out_specs,
        check_vma=False,
    )
```

```python
import functools
import math

import jax
import jax.numpy as jnp
from jax import lax
from jax.experimental import pallas as pl
from jax.experimental.pallas import tpu as pltpu
from jax.sharding import PartitionSpec as P

SPACING = 0.2
TURNS = 32.0
AXES = ("row", "col")
ROUND = 12582912.0
COS = (
    0.9999992107823218,
    -19.738980355763992,
    64.92865742103312,
    -85.27162153429882,
    58.79049212013072,
    -21.07110562764302,
)
SIN = (
    6.283184916495431,
    -41.34158923268858,
    81.59994332978287,
    -76.61447253124996,
    41.342882354568324,
    -12.471243535026977,
)
SMALL, LARGE = 10 * 2**20, 24 * 2**20
PARAMS = pltpu.CompilerParams(vmem_limit_bytes=SMALL)
PEAK = 1.15e15
F32, BF16, I32 = jnp.float32, jnp.bfloat16, jnp.int32


def whole():
    return pl.BlockSpec(memory_space=pltpu.VMEM)


def fixed(array):
    return pl.BlockSpec(array.shape, lambda j: (0,) * len(array.shape))


def params(resident):
    return pltpu.CompilerParams(vmem_limit_bytes=SMALL if resident else LARGE)


def cost(microseconds):
    return pl.CostEstimate(
        flops=int(microseconds * 1e-6 * PEAK), bytes_accessed=0, transcendentals=0
    )


TOKEN = jax.ShapeDtypeStruct((8, 128), F32)


def token_spec():
    return pl.BlockSpec((8, 128), lambda *_: (0, 0))


def iota(shape, dim):
    return lax.broadcasted_iota(I32, shape, dim)


def ones_where(mask):
    return jnp.where(mask, jnp.ones((), F32), jnp.zeros((), F32)).astype(BF16)


def matmul(a, b):
    return jnp.dot(a, b, preferred_element_type=F32)


def matmul_nt(a, b):
    return lax.dot_general(a, b, (((1,), (1,)), ((), ())), preferred_element_type=F32)


class Layout:
    def __init__(self, n_row, n_col):
        self.core = 2 if n_row % 2 == 0 else 1
        self.x = n_row // self.core
        self.y = math.gcd(n_col, self.x)
        self.z = n_col // self.y
        self.devices = n_row * n_col
        self.plane = [(dx, dy) for dx in range(self.x) for dy in range(self.y)]

    def digits(self, index):
        y = index % self.y
        z = index // self.y % self.z
        core = index // (self.y * self.z) % self.core
        return index // (self.y * self.z * self.core), core, z, y

    def shift(self, value, dx=0, dc=0, dz=0, dy=0):
        pairs = []
        for i in range(self.devices):
            pairs.append((i, self.near(i, dx, dc, dz, dy)))
        return lax.ppermute(value, AXES, pairs)

    def by_core(self, value):
        return [value] + [self.shift(value, dc=-dc) for dc in range(1, self.core)]

    def along(self, value):
        return [self.shift(value, dz=-dz) for dz in range(1, self.z)]

    def across(self, value):
        return [self.shift(value, dx=-dx, dy=-dy) for dx, dy in self.plane[1:]]

    def gathered(self, value, others, after):
        return self.by_core(value) + (self.by_core(pack(others, after)) if others else [])

    def index(self, x, core, z, y):
        x, core, z, y = x % self.x, core % self.core, z % self.z, y % self.y
        return ((x * self.core + core) * self.z + z) * self.y + y

    def near(self, me, dx=0, dc=0, dz=0, dy=0):
        x, core, z, y = self.digits(me)
        return self.index(x + dx, core + dc, z + dz, y + dy)

    def in_line(self, me, k):
        if k < self.core:
            return self.near(me, dc=k)
        rest = k - self.core
        return self.near(me, dc=rest // (self.z - 1), dz=1 + rest % (self.z - 1))

    def in_plane(self, me, step):
        return self.near(me, dx=step // self.y, dy=step % self.y)

    def in_planes(self, me, k):
        if k < self.core:
            return self.near(me, dc=k)
        rest, others = k - self.core, len(self.plane) - 1
        dx, dy = self.plane[1 + rest % others]
        return self.near(me, dx=dx, dy=dy, dc=rest // others)

    def given_along(self, blocks):
        return [blocks[0]] + [
            self.shift(block, dz=1 + dz) for dz, block in enumerate(blocks[1:])
        ]

    def spot(self, me, step):
        x, _, _, y = self.digits(me)
        return (x + step // self.y) % self.x * self.y + (y + step % self.y) % self.y

    def given(self, blocks):
        return [blocks[0]] + [
            self.shift(block, dx=dx, dy=dy)
            for block, (dx, dy) in zip(blocks[1:], self.plane[1:])
        ]

    def place(self, triangle, tri_dev, me):
        x, core, z, y = self.digits(triangle // tri_dev)
        mx, mcore, mz, my = self.digits(me)
        dz, dc = (z - mz) % self.z, (core - mcore) % self.core
        block = jnp.where(dz == 0, dc, self.core + dc * (self.z - 1) + dz - 1)
        inside = (x == mx) & (y == my)
        return jnp.where(inside, block * tri_dev + triangle % tri_dev, -1)


class Letter:
    def __init__(self, edges, tri_dev, labels):
        self.edges, self.tri_dev, self.half = edges, tri_dev, -(-tri_dev // 2)
        sizes = [edges, tri_dev, self.half, labels]
        starts = [0]
        for size in sizes:
            starts.append(starts[-1] + -(-size // 128))
        self.starts, self.rows = starts[:4], -(-starts[4] // 8) * 8

    def take(self, letter, part, size):
        first = self.starts[part]
        parts = [letter[first + k : first + k + 1, :] for k in range(-(-size // 128))]
        return jnp.concatenate(parts, axis=1)[:, :size]

    def ends(self, letter):
        pair = self.take(letter, 0, self.edges)
        return pair & 0xFFFF, lax.shift_right_logical(pair, 16)

    def points(self, letter):
        first = self.take(letter, 1, self.tri_dev)
        third = self.take(letter, 2, self.half)
        third = jnp.concatenate([third & 0xFFFF, lax.shift_right_logical(third, 16)], axis=1)
        return jnp.concatenate(
            [first & 0xFFFF, lax.shift_right_logical(first, 16), third[:, : self.tri_dev]], axis=0
        )


def in_rows(row):
    size = row.shape[1]
    if size % 128:
        row = jnp.concatenate([row, jnp.zeros((1, -size % 128), I32)], axis=1)
    return [row[:, k : k + 128] for k in range(0, row.shape[1], 128)]


def letter_kernel(layout, form, slots, inc_ref, points_ref, *refs):
    letter_ref = refs[-1]
    edges, tri_dev, half = form.edges, form.tri_dev, form.half
    ends, devices = 2 * edges, layout.devices
    plus, minus = inc_ref[0:1, :], inc_ref[1:2, :]
    tri = jnp.concatenate([plus, minus], axis=1)
    other = jnp.concatenate([minus, plus], axis=1)
    owner = tri // tri_dev
    hits = iota((devices, ends), 0) == owner
    upper = ones_where(iota((ends, ends), 0) <= iota((ends, ends), 1))
    count = matmul(ones_where(hits), upper)
    rank = jnp.sum(jnp.where(hits, count, 0.0), axis=0, keepdims=True).astype(I32) - 1
    order = ones_where(iota((slots, ends), 0) == rank)
    label = jnp.zeros((devices, slots), I32)
    digits = ((tri % tri_dev + 1, 1), (other & 255, 65536), (other >> 8, 65536 * 256))
    for digit, weight in digits:
        spread = jnp.where(hits, digit.astype(F32), 0.0).astype(BF16)
        label = label + matmul_nt(spread, order).astype(I32) * weight
    third = points_ref[2:3, :]
    if tri_dev % 2:
        third = jnp.concatenate([third, jnp.zeros((1, 1), I32)], axis=1)
    common = (
        in_rows(plus + (minus << 16))
        + in_rows(points_ref[0:1, :] + (points_ref[1:2, :] << 16))
        + in_rows(third[:, :half] + (third[:, half:] << 16))
    )
    places = [(x, y) for x in range(layout.x) for y in range(layout.y)]
    for core in range(layout.core):
        for z in range(layout.z):
            there = [layout.index(x, core, z, y) for x, y in places]
            mine = in_rows(jnp.concatenate([label[d : d + 1, :] for d in there], axis=1))
            blank = form.rows - len(common) - len(mine)
            rows = common + mine + [jnp.zeros((1, 128), I32)] * blank
            letter = jnp.concatenate(rows, axis=0)
            for d in there:
                letter_ref[d] = letter


def letters_of(layout, form, incidence, centroids, slots, after):
    return pl.pallas_call(
        functools.partial(letter_kernel, layout, form, slots),
        in_specs=[whole()] * (2 + len(after)),
        out_specs=whole(),
        out_shape=jax.ShapeDtypeStruct((layout.devices, form.rows, 128), I32),
        compiler_params=PARAMS,
        cost_estimate=cost(1),
    )(incidence, centroids, *after)


def pack_kernel(count, *refs):
    out_ref = refs[-1]
    size = refs[0].shape[0]
    for k in range(count):
        out_ref[k * size : (k + 1) * size, :] = refs[k][...]


def pack(pieces, after):
    size, width = pieces[0].shape
    return pl.pallas_call(
        functools.partial(pack_kernel, len(pieces)),
        in_specs=[whole()] * (len(pieces) + len(after)),
        out_specs=whole(),
        out_shape=jax.ShapeDtypeStruct((len(pieces) * size, width), BF16),
        compiler_params=PARAMS,
        cost_estimate=cost(0.5),
    )(*pieces, *after)


def features(points, scale, first):
    rows, count = points.shape
    square = jnp.sum(points * points, axis=0, keepdims=True)
    norms = [square & 255, square & 0xFF00, square & 0xFF0000]
    ones = [jnp.ones_like(square)] * 3
    zeros = [jnp.zeros((16 - rows - 7, count), I32)]
    if first:
        parts = [-2 * points] + norms + ones + [ones[0]] + zeros
    else:
        parts = [points] + ones + norms + [ones[0]] + zeros
    return (jnp.concatenate(parts, axis=0).astype(F32) * scale).astype(BF16)


def poly(coefs, scale, u):
    value = jnp.full_like(u, coefs[-1] * scale)
    for coef in coefs[-2::-1]:
        value = value * u + coef * scale
    return value


def rows_at(ref, step, rows):
    if ref.shape[0] == rows:
        return ref
    return ref.at[pl.ds(pl.multiple_of(step * rows, rows), rows), :]


def tile_kernel(layout, form, block, first, me_ref, letter_ref, after_ref, *refs):
    real_ref, imag_ref, token_ref, col_ref = refs
    token_ref[...] = jnp.zeros_like(token_ref)
    me, step, size = me_ref[0], pl.program_id(0), form.tri_dev

    @pl.when(step == 0)
    def _():
        for k in range(layout.z * layout.core):
            letter = letter_ref[layout.in_line(me, k)]
            col_ref[:, k * size : (k + 1) * size] = features(form.points(letter), 1.0, False)

    real_ref, imag_ref = [rows_at(ref, step, size) for ref in (real_ref, imag_ref)]
    letter = letter_ref[layout.in_plane(me, first + step)]
    row = features(form.points(letter), 1.0 / (TURNS * TURNS), True)
    for base in range(0, col_ref.shape[1], block):
        cols = slice(base, base + block)
        square = lax.dot_general(
            row, col_ref[:, cols], (((0,), (0,)), ((), ())), preferred_element_type=F32
        )
        inverse = lax.rsqrt(square)
        turns = square * inverse
        frac = turns - ((turns + ROUND) - ROUND)
        u = frac * frac
        real_ref[:, cols] = (poly(COS, SPACING / TURNS, u) * inverse).astype(BF16)
        imag_ref[:, cols] = (poly(SIN, -SPACING / TURNS, u) * (frac * inverse)).astype(BF16)


def build(
    kernel, outs, rows, span, arrays, time, cols, me, resident=False, scratch=(), extra=()
):
    space = pltpu.VMEM if resident else pltpu.HBM
    block = whole() if resident else pl.BlockSpec((rows, cols), lambda j: (j, 0))
    return pl.pallas_call(
        kernel,
        grid=(len(span),),
        in_specs=[pl.BlockSpec(memory_space=pltpu.SMEM)] + [fixed(array) for array in arrays],
        out_specs=[block] * outs + [fixed(array) for array in extra] + [token_spec()],
        out_shape=[space((len(span) * rows, cols), BF16)] * outs + list(extra) + [TOKEN],
        scratch_shapes=scratch,
        compiler_params=params(resident),
        cost_estimate=cost(time),
    )(me, *arrays)


def pick(row, base, count):
    low = jnp.where((row >= base) & (row < base + count), row - base, -1)
    wanted = iota((count, row.shape[1]), 0).astype(F32).astype(BF16)
    same = wanted == low.astype(F32).astype(BF16)
    return jnp.where(same, jnp.ones((), BF16), jnp.zeros((), BF16))


def adjacency_kernel(layout, tri_dev, first, me_ref, label_ref, after_ref, out_ref, *refs):
    refs[-1][...] = jnp.zeros_like(refs[-1])
    me, step = me_ref[0], pl.program_id(0)
    rows, cols = tri_dev, out_ref.shape[1]
    out_ref = rows_at(out_ref, step, rows)
    label = label_ref[layout.spot(me, first + step)]
    mark = (label & 0xFFFF) - 1
    place = layout.place(lax.shift_right_logical(label, 16), tri_dev, me)
    place = jnp.where(mark >= 0, place, -1)
    low = pick(jnp.where(place >= 0, place % rows, -1), 0, rows)
    for base in range(0, cols, rows):
        inside = (place >= base) & (place < base + rows)
        here = pick(jnp.where(inside, mark, -1), 0, rows)
        out_ref[:, base : base + rows] = matmul_nt(here, low).astype(BF16)
    if first == 0:

        @pl.when(step == 0)
        def _():
            every = pick(mark, 0, rows)
            refs[0][...] = matmul(every, jnp.ones((every.shape[1], 128), BF16))


def incidence_kernel(layout, form, first, me_ref, letter_ref, after_ref, out_ref, token_ref):
    token_ref[...] = jnp.zeros_like(token_ref)
    me, step = me_ref[0], pl.program_id(0)
    edges, cols = form.edges, out_ref.shape[1]
    out_ref = rows_at(out_ref, step, edges)
    size = form.tri_dev
    letter = letter_ref[layout.in_plane(me, first + step)]
    plus, minus = [layout.place(end, size, me) for end in form.ends(letter)]
    eye = ones_where(iota((edges, edges), 0) == iota((edges, edges), 1))
    for base in range(0, cols, size):
        signed = pick(plus, base, size) - pick(minus, base, size)
        out_ref[:, base : base + size] = matmul_nt(eye, signed).astype(BF16)


def set_blocks(value, outs):
    for k, out in enumerate(outs):

        @pl.when(pl.program_id(0) == k)
        def _(out=out):
            out[...] = value.astype(out.dtype)


def blocks_like(count, rows, width, exact):
    return [
        jax.ShapeDtypeStruct((rows, width), F32 if exact and k == 0 else BF16)
        for k in range(count)
    ]


def first_kernel(layout, form, me_ref, letter_ref, after_ref, *refs):
    count = layout.z
    pieces, outs, token_ref = refs[: -count - 1], refs[-count - 1 : -1], refs[-1]
    token_ref[...] = jnp.zeros_like(token_ref)
    me, size, edges = me_ref[0], form.tri_dev, form.edges
    base = layout.near(me, dz=pl.program_id(0)) * size
    total, k = None, 0
    for piece in pieces:
        for row in range(0, piece.shape[0], edges):
            plus, minus = form.ends(letter_ref[layout.in_planes(me, k)])
            signed = pick(plus, base, size) - pick(minus, base, size)
            term = matmul(signed, piece[row : row + edges, :])
            total = term if total is None else total + term
            k += 1
    set_blocks(total, outs)


def first_charges(layout, form, me, letters, labels, pieces, resident):
    count, width = layout.z, pieces[0].shape[1]
    shapes = blocks_like(count, form.tri_dev, width, True) + [TOKEN]
    return pl.pallas_call(
        functools.partial(first_kernel, layout, form),
        grid=(count,),
        in_specs=[pl.BlockSpec(memory_space=pltpu.SMEM)] + [whole()] * (2 + len(pieces)),
        out_specs=[whole()] * len(shapes),
        out_shape=shapes,
        compiler_params=params(resident),
        cost_estimate=cost(4),
    )(me, letters, labels, *pieces)


def apply_kernel(mats, fed, block, row, *refs):
    matrices, pieces, outs = refs[:mats], refs[mats : mats + fed], refs[mats + fed : -1]
    refs[-1][...] = jnp.zeros_like(refs[-1])
    half = pieces[0].shape[1] // 2
    sums = []
    for matrix in matrices:
        total, col = None, 0
        for piece in pieces:
            size = piece.shape[0]
            term = matmul(matrix[row : row + block, col : col + size], piece[...])
            total = term if total is None else total + term
            col += size
        sums.append(total)
    value = sums[0]
    if mats == 2:
        real, imag = sums
        value = jnp.concatenate(
            [real[:, :half] - imag[:, half:], real[:, half:] + imag[:, :half]], axis=1
        )
    set_blocks(value, outs)


def apply(matrices, pieces, block, exact, row=None):
    rows, cols = matrices[0].shape
    count, mats = rows // block if row is None else 1, len(matrices)
    spec = pl.BlockSpec((block, cols), lambda j: (j, 0)) if row is None else whole()
    shapes = blocks_like(count, block, pieces[0].shape[1], exact) + [TOKEN]
    return pl.pallas_call(
        functools.partial(apply_kernel, mats, len(pieces), block, row or 0),
        grid=(count,),
        in_specs=[spec] * mats + [whole()] * len(pieces),
        out_specs=[whole()] * len(shapes),
        out_shape=shapes,
        compiler_params=params(row is not None),
        cost_estimate=cost(count * mats / 2),
    )(*matrices, *pieces)


def multiply(parts, pieces, block, resident=False):
    blocks, token = [], None
    for part in parts:
        for row in range(0, part[0].shape[0], block) if resident else [None]:
            *more, token = apply(part, pieces, block, not blocks, row)
            blocks += more
    return blocks, token


def sum_kernel(count, own_ref, *refs):
    total = own_ref[...]
    for ref in refs[:count]:
        total = total + ref[...].astype(F32)
    out_ref, rounded_ref, token_ref = refs[-3:]
    out_ref[...] = total
    rounded_ref[...] = total.astype(BF16)
    token_ref[...] = jnp.zeros_like(token_ref)


def sum_of(blocks, after):
    shape = blocks[0].shape
    return pl.pallas_call(
        functools.partial(sum_kernel, len(blocks) - 1),
        in_specs=[whole()] * (len(blocks) + len(after)),
        out_specs=[whole()] * 3,
        out_shape=[
            jax.ShapeDtypeStruct(shape, F32),
            jax.ShapeDtypeStruct(shape, BF16),
            TOKEN,
        ],
        compiler_params=PARAMS,
        cost_estimate=cost(1),
    )(*blocks, *after)


def potential_kernel(count, summed, weight_ref, own_ref, *refs):
    total = own_ref[...]
    for ref in refs[:count]:
        total = total + ref[...].astype(F32)
    out_ref, sum_ref, rounded_ref, token_ref = refs[-4:]
    potential = total.astype(BF16)
    out_ref[...] = potential
    value = weight_ref[0] * potential.astype(F32)
    if summed:
        value = value + refs[count][...]
    sum_ref[...] = value
    rounded_ref[...] = value.astype(BF16)
    token_ref[...] = jnp.zeros_like(token_ref)


def potential_of(weight, blocks, summed, after):
    shape = blocks[0].shape
    return pl.pallas_call(
        functools.partial(potential_kernel, len(blocks) - 1, len(summed)),
        in_specs=[pl.BlockSpec(memory_space=pltpu.SMEM)]
        + [whole()] * (len(blocks) + len(summed) + len(after)),
        out_specs=[whole()] * 4,
        out_shape=[
            jax.ShapeDtypeStruct(shape, BF16),
            jax.ShapeDtypeStruct(shape, F32),
            jax.ShapeDtypeStruct(shape, BF16),
            TOKEN,
        ],
        compiler_params=PARAMS,
        cost_estimate=cost(1),
    )(weight, *blocks, *summed, *after)


def charge_kernel(count, weight_ref, charge_ref, degree_ref, potential_ref, own_ref, *refs):
    around = own_ref[...]
    for ref in refs[:count]:
        around = around + ref[...].astype(F32)
    out_ref, rounded_ref, token_ref = refs[-3:]
    token_ref[...] = jnp.zeros_like(token_ref)
    change = degree_ref[:, 0:1] * potential_ref[...].astype(F32) - around
    value = charge_ref[...] - weight_ref[0] * change
    out_ref[...] = value
    rounded_ref[...] = value.astype(BF16)


def charge_of(weight, charge, degree, potential, blocks, after):
    return pl.pallas_call(
        functools.partial(charge_kernel, len(blocks) - 1),
        in_specs=[pl.BlockSpec(memory_space=pltpu.SMEM)] + [whole()] * (3 + len(blocks) + len(after)),
        out_specs=[whole()] * 3,
        out_shape=[
            jax.ShapeDtypeStruct(charge.shape, F32),
            jax.ShapeDtypeStruct(charge.shape, BF16),
            TOKEN,
        ],
        compiler_params=PARAMS,
        cost_estimate=cost(1),
    )(weight, charge, degree, potential, *blocks, *after)


def current_kernel(count, current_ref, own_ref, *refs):
    change = own_ref[...]
    for ref in refs[:count]:
        change = change + ref[...].astype(F32)
    refs[-1][...] = (current_ref[...].astype(F32) - change).astype(BF16)


def current_of(current, blocks):
    return pl.pallas_call(
        functools.partial(current_kernel, len(blocks) - 1),
        in_specs=[whole()] * (1 + len(blocks)),
        out_specs=whole(),
        out_shape=jax.ShapeDtypeStruct(current.shape, BF16),
        compiler_params=PARAMS,
        cost_estimate=cost(1),
    )(current, *blocks)


def per_device(layout, currents, incidence, centroids, sweep_weights):
    me = lax.axis_index(AXES).astype(I32).reshape(1)
    tri_dev = centroids.shape[1]
    edge_dev = currents.shape[0]
    devices, count = layout.devices, len(layout.plane)
    slots = 8 * tri_dev // devices
    sweeps = sweep_weights.shape[0]
    cols = layout.z * layout.core * tri_dev

    resident = count * 2 * tri_dev * cols * 2 <= 16 * 2**20

    across = layout.across(currents)
    form = Letter(edge_dev, tri_dev, count * slots)
    letters = letters_of(
        layout, form, incidence, centroids, slots, ()
    )
    letters = lax.all_to_all(letters, AXES, split_axis=0, concat_axis=0, tiled=True)
    labels = letters[:, form.starts[3] :, :].reshape(devices, -1)[:, : count * slots]
    labels = labels.reshape(devices, count, slots).transpose(1, 0, 2)
    labels = labels.reshape(count, 1, devices * slots)

    make = functools.partial(build, cols=cols, me=me)
    cut = (count + 1) // 2
    spans = [span for span in (range(cut), range(cut, count)) if span]

    def tile_part(span, token):
        *part, token = make(
            functools.partial(tile_kernel, layout, form, min(512, cols), span[0]),
            2,
            tri_dev,
            span,
            (letters, token),
            6,
            resident=resident,
            scratch=[pltpu.VMEM((16, cols), BF16)],
        )
        return part, token

    def adjacency_part(span, token):
        extra = () if span[0] else (jax.ShapeDtypeStruct((tri_dev, 128), F32),)
        *part, token = make(
            functools.partial(adjacency_kernel, layout, tri_dev, span[0]),
            1,
            tri_dev,
            span,
            (labels, token),
            6,
            extra=extra,
        )
        return part, token

    pieces = layout.gathered(currents, across, (letters,))
    *blocks, token = first_charges(layout, form, me, letters, labels, pieces, resident)
    tiles = []
    for span in spans:
        part, token = tile_part(span, token)
        tiles.append(part)
    charge, rounded, token = sum_of(layout.given_along(blocks), (token,))

    def incidence_parts(token):
        parts = []
        for span in spans:
            *part, token = make(
                functools.partial(incidence_kernel, layout, form, span[0]),
                1,
                edge_dev,
                span,
                (letters, token),
                3,
            )
            parts.append(part)
        return parts, token

    near, ends = [], None
    summed, potential = (), None
    for sweep in range(sweeps):
        weight = sweep_weights[sweep].reshape(1)
        last = sweep + 1 == sweeps
        build_now = not near and not last
        if build_now:
            (part, degree), token = adjacency_part(spans[0], token)
            near.append([part])
        pieces = layout.gathered(rounded, layout.along(rounded), (token,))
        blocks, token = multiply(tiles, pieces, tri_dev, resident)
        if build_now:
            for span in spans[1:]:
                part, token = adjacency_part(span, token)
                near.append(part)
        potential, *summed, weighted, token = potential_of(
            weight, layout.given(blocks), summed, (token,)
        )
        if last:
            break
        if build_now:
            ends, token = incidence_parts(token)
        pieces = layout.gathered(potential, layout.along(potential), (token,))
        blocks, token = multiply(near, pieces, tri_dev)
        charge, rounded, token = charge_of(
            weight, charge, degree, potential, layout.given(blocks), (token,)
        )
    if ends is None:
        ends, token = incidence_parts(token)
    pieces = layout.gathered(weighted, layout.along(weighted), (token,))
    blocks, _ = multiply(ends, pieces, edge_dev)
    return current_of(currents, layout.given(blocks)), potential


def solution(mesh):
    layout = Layout(mesh.shape["row"], mesh.shape["col"])
    in_specs = (P(AXES, None), P(None, AXES), P(None, AXES), P())
    out_specs = (P(AXES, None), P(AXES, None))
    return jax.shard_map(
        functools.partial(per_device, layout),
        mesh=mesh,
        in_specs=in_specs,
        out_specs=out_specs,
        check_vma=False,
    )
```

```python
import functools
import math

import jax
import jax.numpy as jnp
from jax import lax
from jax.experimental import pallas as pl
from jax.experimental.pallas import tpu as pltpu
from jax.sharding import PartitionSpec as P

SPACING = 0.2
TURNS = 32.0
AXES = ("row", "col")
ROUND = 12582912.0
COS = (
    0.9999992107823218,
    -19.738980355763992,
    64.92865742103312,
    -85.27162153429882,
    58.79049212013072,
    -21.07110562764302,
)
SIN = (
    6.283184916495431,
    -41.34158923268858,
    81.59994332978287,
    -76.61447253124996,
    41.342882354568324,
    -12.471243535026977,
)
SMALL, LARGE = 10 * 2**20, 24 * 2**20
PARAMS = pltpu.CompilerParams(vmem_limit_bytes=SMALL)
PEAK = 1.15e15
F32, BF16, I32 = jnp.float32, jnp.bfloat16, jnp.int32


def whole():
    return pl.BlockSpec(memory_space=pltpu.VMEM)


def fixed(array):
    return pl.BlockSpec(array.shape, lambda j: (0,) * len(array.shape))


def params(resident):
    return pltpu.CompilerParams(vmem_limit_bytes=SMALL if resident else LARGE)


def cost(microseconds):
    return pl.CostEstimate(
        flops=int(microseconds * 1e-6 * PEAK), bytes_accessed=0, transcendentals=0
    )


TOKEN = jax.ShapeDtypeStruct((8, 128), F32)


def token_spec():
    return pl.BlockSpec((8, 128), lambda *_: (0, 0))


def iota(shape, dim):
    return lax.broadcasted_iota(I32, shape, dim)


def ones_where(mask):
    return jnp.where(mask, jnp.ones((), F32), jnp.zeros((), F32)).astype(BF16)


def matmul(a, b):
    return jnp.dot(a, b, preferred_element_type=F32)


def matmul_nt(a, b):
    return lax.dot_general(a, b, (((1,), (1,)), ((), ())), preferred_element_type=F32)


class Layout:
    def __init__(self, n_row, n_col):
        self.core = 2 if n_row % 2 == 0 else 1
        self.x = n_row // self.core
        self.y = math.gcd(n_col, self.x)
        self.z = n_col // self.y
        self.devices = n_row * n_col
        self.plane = [(dx, dy) for dx in range(self.x) for dy in range(self.y)]

    def digits(self, index):
        y = index % self.y
        z = index // self.y % self.z
        core = index // (self.y * self.z) % self.core
        return index // (self.y * self.z * self.core), core, z, y

    def shift(self, value, dx=0, dc=0, dz=0, dy=0):
        pairs = []
        for i in range(self.devices):
            pairs.append((i, self.near(i, dx, dc, dz, dy)))
        return lax.ppermute(value, AXES, pairs)

    def by_core(self, value):
        return [value] + [self.shift(value, dc=-dc) for dc in range(1, self.core)]

    def along(self, value):
        return [self.shift(value, dz=-dz) for dz in range(1, self.z)]

    def across(self, value):
        return [self.shift(value, dx=-dx, dy=-dy) for dx, dy in self.plane[1:]]

    def gathered(self, value, others, after):
        return self.by_core(value) + (self.by_core(pack(others, after)) if others else [])

    def index(self, x, core, z, y):
        x, core, z, y = x % self.x, core % self.core, z % self.z, y % self.y
        return ((x * self.core + core) * self.z + z) * self.y + y

    def near(self, me, dx=0, dc=0, dz=0, dy=0):
        x, core, z, y = self.digits(me)
        return self.index(x + dx, core + dc, z + dz, y + dy)

    def in_line(self, me, k):
        if k < self.core:
            return self.near(me, dc=k)
        rest = k - self.core
        return self.near(me, dc=rest // (self.z - 1), dz=1 + rest % (self.z - 1))

    def in_plane(self, me, step):
        return self.near(me, dx=step // self.y, dy=step % self.y)

    def in_planes(self, me, k):
        if k < self.core:
            return self.near(me, dc=k)
        rest, others = k - self.core, len(self.plane) - 1
        dx, dy = self.plane[1 + rest % others]
        return self.near(me, dx=dx, dy=dy, dc=rest // others)

    def given_along(self, blocks):
        return [blocks[0]] + [
            self.shift(block, dz=1 + dz) for dz, block in enumerate(blocks[1:])
        ]

    def spot(self, me, step):
        x, _, _, y = self.digits(me)
        return (x + step // self.y) % self.x * self.y + (y + step % self.y) % self.y

    def given(self, blocks):
        return [blocks[0]] + [
            self.shift(block, dx=dx, dy=dy)
            for block, (dx, dy) in zip(blocks[1:], self.plane[1:])
        ]

    def place(self, triangle, tri_dev, me):
        x, core, z, y = self.digits(triangle // tri_dev)
        mx, mcore, mz, my = self.digits(me)
        dz, dc = (z - mz) % self.z, (core - mcore) % self.core
        block = jnp.where(dz == 0, dc, self.core + dc * (self.z - 1) + dz - 1)
        inside = (x == mx) & (y == my)
        return jnp.where(inside, block * tri_dev + triangle % tri_dev, -1)


class Letter:
    def __init__(self, edges, tri_dev, labels):
        self.edges, self.tri_dev, self.half = edges, tri_dev, -(-tri_dev // 2)
        sizes = [edges, tri_dev, self.half, labels]
        starts = [0]
        for size in sizes:
            starts.append(starts[-1] + -(-size // 128))
        self.starts, self.rows = starts[:4], -(-starts[4] // 8) * 8

    def take(self, letter, part, size):
        first = self.starts[part]
        parts = [letter[first + k : first + k + 1, :] for k in range(-(-size // 128))]
        return jnp.concatenate(parts, axis=1)[:, :size]

    def ends(self, letter):
        pair = self.take(letter, 0, self.edges)
        return pair & 0xFFFF, lax.shift_right_logical(pair, 16)

    def points(self, letter):
        first = self.take(letter, 1, self.tri_dev)
        third = self.take(letter, 2, self.half)
        third = jnp.concatenate([third & 0xFFFF, lax.shift_right_logical(third, 16)], axis=1)
        return jnp.concatenate(
            [first & 0xFFFF, lax.shift_right_logical(first, 16), third[:, : self.tri_dev]], axis=0
        )


def in_rows(row):
    size = row.shape[1]
    if size % 128:
        row = jnp.concatenate([row, jnp.zeros((1, -size % 128), I32)], axis=1)
    return [row[:, k : k + 128] for k in range(0, row.shape[1], 128)]


def letter_kernel(layout, form, slots, inc_ref, points_ref, *refs):
    letter_ref = refs[-1]
    edges, tri_dev, half = form.edges, form.tri_dev, form.half
    ends, devices = 2 * edges, layout.devices
    plus, minus = inc_ref[0:1, :], inc_ref[1:2, :]
    tri = jnp.concatenate([plus, minus], axis=1)
    other = jnp.concatenate([minus, plus], axis=1)
    owner = tri // tri_dev
    hits = iota((devices, ends), 0) == owner
    upper = ones_where(iota((ends, ends), 0) <= iota((ends, ends), 1))
    count = matmul(ones_where(hits), upper)
    rank = jnp.sum(jnp.where(hits, count, 0.0), axis=0, keepdims=True).astype(I32) - 1
    order = ones_where(iota((slots, ends), 0) == rank)
    label = jnp.zeros((devices, slots), I32)
    digits = ((tri % tri_dev + 1, 1), (other & 255, 65536), (other >> 8, 65536 * 256))
    for digit, weight in digits:
        spread = jnp.where(hits, digit.astype(F32), 0.0).astype(BF16)
        label = label + matmul_nt(spread, order).astype(I32) * weight
    third = points_ref[2:3, :]
    if tri_dev % 2:
        third = jnp.concatenate([third, jnp.zeros((1, 1), I32)], axis=1)
    common = (
        in_rows(plus + (minus << 16))
        + in_rows(points_ref[0:1, :] + (points_ref[1:2, :] << 16))
        + in_rows(third[:, :half] + (third[:, half:] << 16))
    )
    places = [(x, y) for x in range(layout.x) for y in range(layout.y)]
    for core in range(layout.core):
        for z in range(layout.z):
            there = [layout.index(x, core, z, y) for x, y in places]
            mine = in_rows(jnp.concatenate([label[d : d + 1, :] for d in there], axis=1))
            blank = form.rows - len(common) - len(mine)
            rows = common + mine + [jnp.zeros((1, 128), I32)] * blank
            letter = jnp.concatenate(rows, axis=0)
            for d in there:
                letter_ref[d] = letter


def letters_of(layout, form, incidence, centroids, slots, after):
    return pl.pallas_call(
        functools.partial(letter_kernel, layout, form, slots),
        in_specs=[whole()] * (2 + len(after)),
        out_specs=whole(),
        out_shape=jax.ShapeDtypeStruct((layout.devices, form.rows, 128), I32),
        compiler_params=PARAMS,
        cost_estimate=cost(1),
    )(incidence, centroids, *after)


def pack_kernel(count, *refs):
    out_ref = refs[-1]
    size = refs[0].shape[0]
    for k in range(count):
        out_ref[k * size : (k + 1) * size, :] = refs[k][...]


def pack(pieces, after):
    size, width = pieces[0].shape
    return pl.pallas_call(
        functools.partial(pack_kernel, len(pieces)),
        in_specs=[whole()] * (len(pieces) + len(after)),
        out_specs=whole(),
        out_shape=jax.ShapeDtypeStruct((len(pieces) * size, width), BF16),
        compiler_params=PARAMS,
        cost_estimate=cost(0.5),
    )(*pieces, *after)


def features(points, scale, first):
    rows, count = points.shape
    square = jnp.sum(points * points, axis=0, keepdims=True)
    norms = [square & 255, square & 0xFF00, square & 0xFF0000]
    ones = [jnp.ones_like(square)] * 3
    zeros = [jnp.zeros((16 - rows - 7, count), I32)]
    if first:
        parts = [-2 * points] + norms + ones + [ones[0]] + zeros
    else:
        parts = [points] + ones + norms + [ones[0]] + zeros
    return (jnp.concatenate(parts, axis=0).astype(F32) * scale).astype(BF16)


def poly(coefs, scale, u):
    value = jnp.full_like(u, coefs[-1] * scale)
    for coef in coefs[-2::-1]:
        value = value * u + coef * scale
    return value


def rows_at(ref, step, rows):
    if ref.shape[0] == rows:
        return ref
    return ref.at[pl.ds(pl.multiple_of(step * rows, rows), rows), :]


def tile_kernel(layout, form, block, first, me_ref, letter_ref, after_ref, *refs):
    real_ref, imag_ref, token_ref, col_ref = refs
    token_ref[...] = jnp.zeros_like(token_ref)
    me, step, size = me_ref[0], pl.program_id(0), form.tri_dev

    @pl.when(step == 0)
    def _():
        for k in range(layout.z * layout.core):
            letter = letter_ref[layout.in_line(me, k)]
            col_ref[:, k * size : (k + 1) * size] = features(form.points(letter), 1.0, False)

    real_ref, imag_ref = [rows_at(ref, step, size) for ref in (real_ref, imag_ref)]
    letter = letter_ref[layout.in_plane(me, first + step)]
    row = features(form.points(letter), 1.0 / (TURNS * TURNS), True)
    for base in range(0, col_ref.shape[1], block):
        cols = slice(base, base + block)
        square = lax.dot_general(
            row, col_ref[:, cols], (((0,), (0,)), ((), ())), preferred_element_type=F32
        )
        inverse = lax.rsqrt(square)
        turns = square * inverse
        frac = turns - ((turns + ROUND) - ROUND)
        u = frac * frac
        real_ref[:, cols] = (poly(COS, SPACING / TURNS, u) * inverse).astype(BF16)
        imag_ref[:, cols] = (poly(SIN, -SPACING / TURNS, u) * (frac * inverse)).astype(BF16)


def build(
    kernel, outs, rows, span, arrays, time, cols, me, resident=False, scratch=(), extra=()
):
    space = pltpu.VMEM if resident else pltpu.HBM
    block = whole() if resident else pl.BlockSpec((rows, cols), lambda j: (j, 0))
    return pl.pallas_call(
        kernel,
        grid=(len(span),),
        in_specs=[pl.BlockSpec(memory_space=pltpu.SMEM)] + [fixed(array) for array in arrays],
        out_specs=[block] * outs + [fixed(array) for array in extra] + [token_spec()],
        out_shape=[space((len(span) * rows, cols), BF16)] * outs + list(extra) + [TOKEN],
        scratch_shapes=scratch,
        compiler_params=params(resident),
        cost_estimate=cost(time),
    )(me, *arrays)


def pick(row, base, count):
    low = jnp.where((row >= base) & (row < base + count), row - base, -1)
    wanted = iota((count, row.shape[1]), 0).astype(F32).astype(BF16)
    same = wanted == low.astype(F32).astype(BF16)
    return jnp.where(same, jnp.ones((), BF16), jnp.zeros((), BF16))


def adjacency_kernel(layout, tri_dev, first, me_ref, label_ref, after_ref, out_ref, *refs):
    refs[-1][...] = jnp.zeros_like(refs[-1])
    me, step = me_ref[0], pl.program_id(0)
    rows, cols = tri_dev, out_ref.shape[1]
    out_ref = rows_at(out_ref, step, rows)
    label = label_ref[layout.spot(me, first + step)]
    mark = (label & 0xFFFF) - 1
    place = layout.place(lax.shift_right_logical(label, 16), tri_dev, me)
    place = jnp.where(mark >= 0, place, -1)
    low = pick(jnp.where(place >= 0, place % rows, -1), 0, rows)
    for base in range(0, cols, rows):
        inside = (place >= base) & (place < base + rows)
        here = pick(jnp.where(inside, mark, -1), 0, rows)
        out_ref[:, base : base + rows] = matmul_nt(here, low).astype(BF16)
    if first == 0:

        @pl.when(step == 0)
        def _():
            every = pick(mark, 0, rows)
            refs[0][...] = matmul(every, jnp.ones((every.shape[1], 128), BF16))


def incidence_kernel(layout, form, first, me_ref, letter_ref, after_ref, out_ref, token_ref):
    token_ref[...] = jnp.zeros_like(token_ref)
    me, step = me_ref[0], pl.program_id(0)
    edges, cols = form.edges, out_ref.shape[1]
    out_ref = rows_at(out_ref, step, edges)
    size = form.tri_dev
    letter = letter_ref[layout.in_plane(me, first + step)]
    plus, minus = [layout.place(end, size, me) for end in form.ends(letter)]
    eye = ones_where(iota((edges, edges), 0) == iota((edges, edges), 1))
    for base in range(0, cols, size):
        signed = pick(plus, base, size) - pick(minus, base, size)
        out_ref[:, base : base + size] = matmul_nt(eye, signed).astype(BF16)


def set_blocks(value, outs):
    for k, out in enumerate(outs):

        @pl.when(pl.program_id(0) == k)
        def _(out=out):
            out[...] = value.astype(out.dtype)


def blocks_like(count, rows, width, exact):
    return [
        jax.ShapeDtypeStruct((rows, width), F32 if exact and k == 0 else BF16)
        for k in range(count)
    ]


def first_kernel(layout, form, me_ref, letter_ref, after_ref, out_ref, token_ref):
    token_ref[...] = jnp.zeros_like(token_ref)
    me, step = me_ref[0], pl.program_id(0)
    size, edges = form.tri_dev, form.edges
    out_ref = rows_at(out_ref, step, size)
    base = layout.near(me, dz=step) * size
    for k in range(out_ref.shape[1] // edges):
        plus, minus = form.ends(letter_ref[layout.in_planes(me, k)])
        signed = pick(plus, base, size) - pick(minus, base, size)
        out_ref[:, k * edges : (k + 1) * edges] = signed


def apply_kernel(mats, fed, block, row, *refs):
    matrices, pieces, outs = refs[:mats], refs[mats : mats + fed], refs[mats + fed : -1]
    refs[-1][...] = jnp.zeros_like(refs[-1])
    half = pieces[0].shape[1] // 2
    sums = []
    for matrix in matrices:
        total, col = None, 0
        for piece in pieces:
            size = piece.shape[0]
            term = matmul(matrix[row : row + block, col : col + size], piece[...])
            total = term if total is None else total + term
            col += size
        sums.append(total)
    value = sums[0]
    if mats == 2:
        real, imag = sums
        value = jnp.concatenate(
            [real[:, :half] - imag[:, half:], real[:, half:] + imag[:, :half]], axis=1
        )
    set_blocks(value, outs)


def apply(matrices, pieces, block, exact, row=None):
    rows, cols = matrices[0].shape
    count, mats = rows // block if row is None else 1, len(matrices)
    spec = pl.BlockSpec((block, cols), lambda j: (j, 0)) if row is None else whole()
    shapes = blocks_like(count, block, pieces[0].shape[1], exact) + [TOKEN]
    return pl.pallas_call(
        functools.partial(apply_kernel, mats, len(pieces), block, row or 0),
        grid=(count,),
        in_specs=[spec] * mats + [whole()] * len(pieces),
        out_specs=[whole()] * len(shapes),
        out_shape=shapes,
        compiler_params=params(row is not None),
        cost_estimate=cost(count * mats / 2),
    )(*matrices, *pieces)


def multiply(parts, pieces, block, resident=False):
    blocks, token = [], None
    for part in parts:
        for row in range(0, part[0].shape[0], block) if resident else [None]:
            *more, token = apply(part, pieces, block, not blocks, row)
            blocks += more
    return blocks, token


def sum_kernel(count, own_ref, *refs):
    total = own_ref[...]
    for ref in refs[:count]:
        total = total + ref[...].astype(F32)
    out_ref, rounded_ref, token_ref = refs[-3:]
    out_ref[...] = total
    rounded_ref[...] = total.astype(BF16)
    token_ref[...] = jnp.zeros_like(token_ref)


def sum_of(blocks, after):
    shape = blocks[0].shape
    return pl.pallas_call(
        functools.partial(sum_kernel, len(blocks) - 1),
        in_specs=[whole()] * (len(blocks) + len(after)),
        out_specs=[whole()] * 3,
        out_shape=[
            jax.ShapeDtypeStruct(shape, F32),
            jax.ShapeDtypeStruct(shape, BF16),
            TOKEN,
        ],
        compiler_params=PARAMS,
        cost_estimate=cost(1),
    )(*blocks, *after)


def potential_kernel(count, summed, weight_ref, own_ref, *refs):
    total = own_ref[...]
    for ref in refs[:count]:
        total = total + ref[...].astype(F32)
    out_ref, sum_ref, rounded_ref, token_ref = refs[-4:]
    potential = total.astype(BF16)
    out_ref[...] = potential
    value = weight_ref[0] * potential.astype(F32)
    if summed:
        value = value + refs[count][...]
    sum_ref[...] = value
    rounded_ref[...] = value.astype(BF16)
    token_ref[...] = jnp.zeros_like(token_ref)


def potential_of(weight, blocks, summed, after):
    shape = blocks[0].shape
    return pl.pallas_call(
        functools.partial(potential_kernel, len(blocks) - 1, len(summed)),
        in_specs=[pl.BlockSpec(memory_space=pltpu.SMEM)]
        + [whole()] * (len(blocks) + len(summed) + len(after)),
        out_specs=[whole()] * 4,
        out_shape=[
            jax.ShapeDtypeStruct(shape, BF16),
            jax.ShapeDtypeStruct(shape, F32),
            jax.ShapeDtypeStruct(shape, BF16),
            TOKEN,
        ],
        compiler_params=PARAMS,
        cost_estimate=cost(1),
    )(weight, *blocks, *summed, *after)


def charge_kernel(count, weight_ref, charge_ref, degree_ref, potential_ref, own_ref, *refs):
    around = own_ref[...]
    for ref in refs[:count]:
        around = around + ref[...].astype(F32)
    out_ref, rounded_ref, token_ref = refs[-3:]
    token_ref[...] = jnp.zeros_like(token_ref)
    change = degree_ref[:, 0:1] * potential_ref[...].astype(F32) - around
    value = charge_ref[...] - weight_ref[0] * change
    out_ref[...] = value
    rounded_ref[...] = value.astype(BF16)


def charge_of(weight, charge, degree, potential, blocks, after):
    return pl.pallas_call(
        functools.partial(charge_kernel, len(blocks) - 1),
        in_specs=[pl.BlockSpec(memory_space=pltpu.SMEM)] + [whole()] * (3 + len(blocks) + len(after)),
        out_specs=[whole()] * 3,
        out_shape=[
            jax.ShapeDtypeStruct(charge.shape, F32),
            jax.ShapeDtypeStruct(charge.shape, BF16),
            TOKEN,
        ],
        compiler_params=PARAMS,
        cost_estimate=cost(1),
    )(weight, charge, degree, potential, *blocks, *after)


def current_kernel(count, current_ref, own_ref, *refs):
    change = own_ref[...]
    for ref in refs[:count]:
        change = change + ref[...].astype(F32)
    refs[-1][...] = (current_ref[...].astype(F32) - change).astype(BF16)


def current_of(current, blocks):
    return pl.pallas_call(
        functools.partial(current_kernel, len(blocks) - 1),
        in_specs=[whole()] * (1 + len(blocks)),
        out_specs=whole(),
        out_shape=jax.ShapeDtypeStruct(current.shape, BF16),
        compiler_params=PARAMS,
        cost_estimate=cost(1),
    )(current, *blocks)


def per_device(layout, currents, incidence, centroids, sweep_weights):
    me = lax.axis_index(AXES).astype(I32).reshape(1)
    tri_dev = centroids.shape[1]
    edge_dev = currents.shape[0]
    devices, count = layout.devices, len(layout.plane)
    slots = 8 * tri_dev // devices
    sweeps = sweep_weights.shape[0]
    cols = layout.z * layout.core * tri_dev

    resident = count * 2 * tri_dev * cols * 2 <= 16 * 2**20

    across = layout.across(currents)
    form = Letter(edge_dev, tri_dev, count * slots)
    letters = letters_of(
        layout, form, incidence, centroids, slots, ()
    )
    letters = lax.all_to_all(letters, AXES, split_axis=0, concat_axis=0, tiled=True)
    labels = letters[:, form.starts[3] :, :].reshape(devices, -1)[:, : count * slots]
    labels = labels.reshape(devices, count, slots).transpose(1, 0, 2)
    labels = labels.reshape(count, 1, devices * slots)

    make = functools.partial(build, cols=cols, me=me)
    cut = (count + 1) // 2
    spans = [span for span in (range(cut), range(cut, count)) if span]

    def tile_part(span, token):
        *part, token = make(
            functools.partial(tile_kernel, layout, form, min(512, cols), span[0]),
            2,
            tri_dev,
            span,
            (letters, token),
            6,
            resident=resident,
            scratch=[pltpu.VMEM((16, cols), BF16)],
        )
        return part, token

    def adjacency_part(span, token):
        extra = () if span[0] else (jax.ShapeDtypeStruct((tri_dev, 128), F32),)
        *part, token = make(
            functools.partial(adjacency_kernel, layout, tri_dev, span[0]),
            1,
            tri_dev,
            span,
            (labels, token),
            6,
            extra=extra,
        )
        return part, token

    first, token = make(
        functools.partial(first_kernel, layout, form),
        1,
        tri_dev,
        range(layout.z),
        (letters, labels),
        3,
        cols=count * layout.core * edge_dev,
        resident=resident,
    )
    pieces = layout.gathered(currents, across, (token,))
    blocks, token = multiply([[first]], pieces, tri_dev, resident)
    tiles = []
    for span in spans:
        part, token = tile_part(span, token)
        tiles.append(part)
    charge, rounded, token = sum_of(layout.given_along(blocks), (token,))

    def incidence_parts(token):
        parts = []
        for span in spans:
            *part, token = make(
                functools.partial(incidence_kernel, layout, form, span[0]),
                1,
                edge_dev,
                span,
                (letters, token),
                3,
            )
            parts.append(part)
        return parts, token

    near, ends = [], None
    summed, potential = (), None
    for sweep in range(sweeps):
        weight = sweep_weights[sweep].reshape(1)
        last = sweep + 1 == sweeps
        build_now = not near and not last
        if build_now:
            (part, degree), token = adjacency_part(spans[0], token)
            near.append([part])
        pieces = layout.gathered(rounded, layout.along(rounded), (token,))
        blocks, token = multiply(tiles, pieces, tri_dev, resident)
        if build_now:
            for span in spans[1:]:
                part, token = adjacency_part(span, token)
                near.append(part)
        potential, *summed, weighted, token = potential_of(
            weight, layout.given(blocks), summed, (token,)
        )
        if last:
            break
        if build_now:
            ends, token = incidence_parts(token)
        pieces = layout.gathered(potential, layout.along(potential), (token,))
        blocks, token = multiply(near, pieces, tri_dev, resident)
        charge, rounded, token = charge_of(
            weight, charge, degree, potential, layout.given(blocks), (token,)
        )
    if ends is None:
        ends, token = incidence_parts(token)
    pieces = layout.gathered(weighted, layout.along(weighted), (token,))
    blocks, _ = multiply(ends, pieces, edge_dev, resident)
    return current_of(currents, layout.given(blocks)), potential


def solution(mesh):
    layout = Layout(mesh.shape["row"], mesh.shape["col"])
    in_specs = (P(AXES, None), P(None, AXES), P(None, AXES), P())
    out_specs = (P(AXES, None), P(AXES, None))
    return jax.shard_map(
        functools.partial(per_device, layout),
        mesh=mesh,
        in_specs=in_specs,
        out_specs=out_specs,
        check_vma=False,
    )
```

```python
import functools
import math

import jax
import jax.numpy as jnp
from jax import lax
from jax.experimental import pallas as pl
from jax.experimental.pallas import tpu as pltpu
from jax.sharding import PartitionSpec as P

SPACING = 0.2
TURNS = 32.0
AXES = ("row", "col")
ROUND = 12582912.0
COS = (
    0.9999992107823218,
    -19.738980355763992,
    64.92865742103312,
    -85.27162153429882,
    58.79049212013072,
    -21.07110562764302,
)
SIN = (
    6.283184916495431,
    -41.34158923268858,
    81.59994332978287,
    -76.61447253124996,
    41.342882354568324,
    -12.471243535026977,
)
SMALL, LARGE = 10 * 2**20, 24 * 2**20
PARAMS = pltpu.CompilerParams(vmem_limit_bytes=SMALL)
PEAK = 1.15e15
F32, BF16, I32 = jnp.float32, jnp.bfloat16, jnp.int32


def whole():
    return pl.BlockSpec(memory_space=pltpu.VMEM)


def fixed(array):
    return pl.BlockSpec(array.shape, lambda j: (0,) * len(array.shape))


def params(resident):
    return pltpu.CompilerParams(vmem_limit_bytes=SMALL if resident else LARGE)


def cost(microseconds):
    return pl.CostEstimate(
        flops=int(microseconds * 1e-6 * PEAK), bytes_accessed=0, transcendentals=0
    )


TOKEN = jax.ShapeDtypeStruct((8, 128), F32)


def token_spec():
    return pl.BlockSpec((8, 128), lambda *_: (0, 0))


def iota(shape, dim):
    return lax.broadcasted_iota(I32, shape, dim)


def ones_where(mask):
    return jnp.where(mask, jnp.ones((), F32), jnp.zeros((), F32)).astype(BF16)


def matmul(a, b):
    return jnp.dot(a, b, preferred_element_type=F32)


def matmul_nt(a, b):
    return lax.dot_general(a, b, (((1,), (1,)), ((), ())), preferred_element_type=F32)


class Layout:
    def __init__(self, n_row, n_col):
        self.core = 2 if n_row % 2 == 0 else 1
        self.x = n_row // self.core
        self.y = math.gcd(n_col, self.x)
        self.z = n_col // self.y
        self.devices = n_row * n_col
        self.plane = [(dx, dy) for dx in range(self.x) for dy in range(self.y)]

    def digits(self, index):
        y = index % self.y
        z = index // self.y % self.z
        core = index // (self.y * self.z) % self.core
        return index // (self.y * self.z * self.core), core, z, y

    def shift(self, value, dx=0, dc=0, dz=0, dy=0):
        pairs = []
        for i in range(self.devices):
            pairs.append((i, self.near(i, dx, dc, dz, dy)))
        return lax.ppermute(value, AXES, pairs)

    def by_core(self, value):
        return [value] + [self.shift(value, dc=-dc) for dc in range(1, self.core)]

    def along(self, value):
        return [self.shift(value, dz=-dz) for dz in range(1, self.z)]

    def across(self, value):
        return [self.shift(value, dx=-dx, dy=-dy) for dx, dy in self.plane[1:]]

    def gathered(self, value, others, after):
        return self.by_core(value) + (self.by_core(pack(others, after)) if others else [])

    def index(self, x, core, z, y):
        x, core, z, y = x % self.x, core % self.core, z % self.z, y % self.y
        return ((x * self.core + core) * self.z + z) * self.y + y

    def near(self, me, dx=0, dc=0, dz=0, dy=0):
        x, core, z, y = self.digits(me)
        return self.index(x + dx, core + dc, z + dz, y + dy)

    def in_line(self, me, k):
        if k < self.core:
            return self.near(me, dc=k)
        rest = k - self.core
        return self.near(me, dc=rest // (self.z - 1), dz=1 + rest % (self.z - 1))

    def in_plane(self, me, step):
        return self.near(me, dx=step // self.y, dy=step % self.y)

    def in_planes(self, me, k):
        if k < self.core:
            return self.near(me, dc=k)
        rest, others = k - self.core, len(self.plane) - 1
        dx, dy = self.plane[1 + rest % others]
        return self.near(me, dx=dx, dy=dy, dc=rest // others)

    def given_along(self, blocks):
        return [blocks[0]] + [
            self.shift(block, dz=1 + dz) for dz, block in enumerate(blocks[1:])
        ]

    def spot(self, me, step):
        x, _, _, y = self.digits(me)
        return (x + step // self.y) % self.x * self.y + (y + step % self.y) % self.y

    def given(self, blocks):
        return [blocks[0]] + [
            self.shift(block, dx=dx, dy=dy)
            for block, (dx, dy) in zip(blocks[1:], self.plane[1:])
        ]

    def place(self, triangle, tri_dev, me):
        x, core, z, y = self.digits(triangle // tri_dev)
        mx, mcore, mz, my = self.digits(me)
        dz, dc = (z - mz) % self.z, (core - mcore) % self.core
        block = jnp.where(dz == 0, dc, self.core + dc * (self.z - 1) + dz - 1)
        inside = (x == mx) & (y == my)
        return jnp.where(inside, block * tri_dev + triangle % tri_dev, -1)


class Letter:
    def __init__(self, edges, tri_dev, labels):
        self.edges, self.tri_dev, self.half = edges, tri_dev, -(-tri_dev // 2)
        sizes = [edges, tri_dev, self.half, labels]
        starts = [0]
        for size in sizes:
            starts.append(starts[-1] + -(-size // 128))
        self.starts, self.rows = starts[:4], -(-starts[4] // 8) * 8

    def take(self, letter, part, size):
        first = self.starts[part]
        parts = [letter[first + k : first + k + 1, :] for k in range(-(-size // 128))]
        return jnp.concatenate(parts, axis=1)[:, :size]

    def ends(self, letter):
        pair = self.take(letter, 0, self.edges)
        return pair & 0xFFFF, lax.shift_right_logical(pair, 16)

    def points(self, letter):
        first = self.take(letter, 1, self.tri_dev)
        third = self.take(letter, 2, self.half)
        third = jnp.concatenate([third & 0xFFFF, lax.shift_right_logical(third, 16)], axis=1)
        return jnp.concatenate(
            [first & 0xFFFF, lax.shift_right_logical(first, 16), third[:, : self.tri_dev]], axis=0
        )


def in_rows(row):
    size = row.shape[1]
    if size % 128:
        row = jnp.concatenate([row, jnp.zeros((1, -size % 128), I32)], axis=1)
    return [row[:, k : k + 128] for k in range(0, row.shape[1], 128)]


def letter_kernel(layout, form, slots, inc_ref, points_ref, *refs):
    letter_ref = refs[-1]
    edges, tri_dev, half = form.edges, form.tri_dev, form.half
    ends, devices = 2 * edges, layout.devices
    plus, minus = inc_ref[0:1, :], inc_ref[1:2, :]
    tri = jnp.concatenate([plus, minus], axis=1)
    other = jnp.concatenate([minus, plus], axis=1)
    owner = tri // tri_dev
    hits = iota((devices, ends), 0) == owner
    upper = ones_where(iota((ends, ends), 0) <= iota((ends, ends), 1))
    count = matmul(ones_where(hits), upper)
    rank = jnp.sum(jnp.where(hits, count, 0.0), axis=0, keepdims=True).astype(I32) - 1
    order = ones_where(iota((slots, ends), 0) == rank)
    label = jnp.zeros((devices, slots), I32)
    digits = ((tri % tri_dev + 1, 1), (other & 255, 65536), (other >> 8, 65536 * 256))
    for digit, weight in digits:
        spread = jnp.where(hits, digit.astype(F32), 0.0).astype(BF16)
        label = label + matmul_nt(spread, order).astype(I32) * weight
    third = points_ref[2:3, :]
    if tri_dev % 2:
        third = jnp.concatenate([third, jnp.zeros((1, 1), I32)], axis=1)
    common = (
        in_rows(plus + (minus << 16))
        + in_rows(points_ref[0:1, :] + (points_ref[1:2, :] << 16))
        + in_rows(third[:, :half] + (third[:, half:] << 16))
    )
    places = [(x, y) for x in range(layout.x) for y in range(layout.y)]
    for core in range(layout.core):
        for z in range(layout.z):
            there = [layout.index(x, core, z, y) for x, y in places]
            mine = in_rows(jnp.concatenate([label[d : d + 1, :] for d in there], axis=1))
            blank = form.rows - len(common) - len(mine)
            rows = common + mine + [jnp.zeros((1, 128), I32)] * blank
            letter = jnp.concatenate(rows, axis=0)
            for d in there:
                letter_ref[d] = letter


def letters_of(layout, form, incidence, centroids, slots, after):
    return pl.pallas_call(
        functools.partial(letter_kernel, layout, form, slots),
        in_specs=[whole()] * (2 + len(after)),
        out_specs=whole(),
        out_shape=jax.ShapeDtypeStruct((layout.devices, form.rows, 128), I32),
        compiler_params=PARAMS,
        cost_estimate=cost(1),
    )(incidence, centroids, *after)


def pack_kernel(count, *refs):
    out_ref = refs[-1]
    size = refs[0].shape[0]
    for k in range(count):
        out_ref[k * size : (k + 1) * size, :] = refs[k][...]


def pack(pieces, after):
    size, width = pieces[0].shape
    return pl.pallas_call(
        functools.partial(pack_kernel, len(pieces)),
        in_specs=[whole()] * (len(pieces) + len(after)),
        out_specs=whole(),
        out_shape=jax.ShapeDtypeStruct((len(pieces) * size, width), BF16),
        compiler_params=PARAMS,
        cost_estimate=cost(0.5),
    )(*pieces, *after)


def features(points, scale, first):
    rows, count = points.shape
    square = jnp.sum(points * points, axis=0, keepdims=True)
    norms = [square & 255, square & 0xFF00, square & 0xFF0000]
    ones = [jnp.ones_like(square)] * 3
    zeros = [jnp.zeros((16 - rows - 7, count), I32)]
    if first:
        parts = [-2 * points] + norms + ones + [ones[0]] + zeros
    else:
        parts = [points] + ones + norms + [ones[0]] + zeros
    return (jnp.concatenate(parts, axis=0).astype(F32) * scale).astype(BF16)


def poly(coefs, scale, u):
    value = jnp.full_like(u, coefs[-1] * scale)
    for coef in coefs[-2::-1]:
        value = value * u + coef * scale
    return value


def rows_at(ref, step, rows):
    if ref.shape[0] == rows:
        return ref
    return ref.at[pl.ds(pl.multiple_of(step * rows, rows), rows), :]


def tile_kernel(layout, form, block, first, me_ref, letter_ref, after_ref, *refs):
    real_ref, imag_ref, token_ref, col_ref = refs
    token_ref[...] = jnp.zeros_like(token_ref)
    me, step, size = me_ref[0], pl.program_id(0), form.tri_dev

    @pl.when(step == 0)
    def _():
        for k in range(layout.z * layout.core):
            letter = letter_ref[layout.in_line(me, k)]
            col_ref[:, k * size : (k + 1) * size] = features(form.points(letter), 1.0, False)

    real_ref, imag_ref = [rows_at(ref, step, size) for ref in (real_ref, imag_ref)]
    letter = letter_ref[layout.in_plane(me, first + step)]
    row = features(form.points(letter), 1.0 / (TURNS * TURNS), True)
    for base in range(0, col_ref.shape[1], block):
        cols = slice(base, base + block)
        square = lax.dot_general(
            row, col_ref[:, cols], (((0,), (0,)), ((), ())), preferred_element_type=F32
        )
        inverse = lax.rsqrt(square)
        turns = square * inverse
        frac = turns - ((turns + ROUND) - ROUND)
        u = frac * frac
        real_ref[:, cols] = (poly(COS, SPACING / TURNS, u) * inverse).astype(BF16)
        imag_ref[:, cols] = (poly(SIN, -SPACING / TURNS, u) * (frac * inverse)).astype(BF16)


def build(
    kernel, outs, rows, span, arrays, time, cols, me, resident=False, scratch=(), extra=()
):
    space = pltpu.VMEM if resident else pltpu.HBM
    block = whole() if resident else pl.BlockSpec((rows, cols), lambda j: (j, 0))
    return pl.pallas_call(
        kernel,
        grid=(len(span),),
        in_specs=[pl.BlockSpec(memory_space=pltpu.SMEM)] + [fixed(array) for array in arrays],
        out_specs=[block] * outs + [fixed(array) for array in extra] + [token_spec()],
        out_shape=[space((len(span) * rows, cols), BF16)] * outs + list(extra) + [TOKEN],
        scratch_shapes=scratch,
        compiler_params=params(resident),
        cost_estimate=cost(time),
    )(me, *arrays)


def pick(row, base, count):
    low = jnp.where((row >= base) & (row < base + count), row - base, -1)
    wanted = iota((count, row.shape[1]), 0).astype(F32).astype(BF16)
    same = wanted == low.astype(F32).astype(BF16)
    return jnp.where(same, jnp.ones((), BF16), jnp.zeros((), BF16))


def adjacency_kernel(layout, tri_dev, first, me_ref, label_ref, after_ref, out_ref, *refs):
    refs[-1][...] = jnp.zeros_like(refs[-1])
    me, step = me_ref[0], pl.program_id(0)
    rows, cols = tri_dev, out_ref.shape[1]
    out_ref = rows_at(out_ref, step, rows)
    label = label_ref[layout.spot(me, first + step)]
    mark = (label & 0xFFFF) - 1
    place = layout.place(lax.shift_right_logical(label, 16), tri_dev, me)
    place = jnp.where(mark >= 0, place, -1)
    low = pick(jnp.where(place >= 0, place % rows, -1), 0, rows)
    for base in range(0, cols, rows):
        inside = (place >= base) & (place < base + rows)
        here = pick(jnp.where(inside, mark, -1), 0, rows)
        out_ref[:, base : base + rows] = matmul_nt(here, low).astype(BF16)
    if first == 0:

        @pl.when(step == 0)
        def _():
            every = pick(mark, 0, rows)
            refs[0][...] = matmul(every, jnp.ones((every.shape[1], 128), BF16))


def incidence_kernel(layout, form, first, me_ref, letter_ref, after_ref, out_ref, token_ref):
    token_ref[...] = jnp.zeros_like(token_ref)
    me, step = me_ref[0], pl.program_id(0)
    edges, cols = form.edges, out_ref.shape[1]
    out_ref = rows_at(out_ref, step, edges)
    size = form.tri_dev
    letter = letter_ref[layout.in_plane(me, first + step)]
    plus, minus = [layout.place(end, size, me) for end in form.ends(letter)]
    eye = ones_where(iota((edges, edges), 0) == iota((edges, edges), 1))
    for base in range(0, cols, size):
        signed = pick(plus, base, size) - pick(minus, base, size)
        out_ref[:, base : base + size] = matmul_nt(eye, signed).astype(BF16)


def set_blocks(value, outs):
    for k, out in enumerate(outs):

        @pl.when(pl.program_id(0) == k)
        def _(out=out):
            out[...] = value.astype(out.dtype)


def blocks_like(count, rows, width, exact):
    return [
        jax.ShapeDtypeStruct((rows, width), F32 if exact and k == 0 else BF16)
        for k in range(count)
    ]


def first_kernel(layout, form, me_ref, letter_ref, after_ref, out_ref, token_ref):
    token_ref[...] = jnp.zeros_like(token_ref)
    me, step = me_ref[0], pl.program_id(0)
    size, edges = form.tri_dev, form.edges
    out_ref = rows_at(out_ref, step, size)
    base = layout.near(me, dz=step) * size
    for k in range(out_ref.shape[1] // edges):
        plus, minus = form.ends(letter_ref[layout.in_planes(me, k)])
        signed = pick(plus, base, size) - pick(minus, base, size)
        out_ref[:, k * edges : (k + 1) * edges] = signed


def apply_kernel(mats, fed, block, row, *refs):
    matrices, pieces, outs = refs[:mats], refs[mats : mats + fed], refs[mats + fed : -1]
    refs[-1][...] = jnp.zeros_like(refs[-1])
    half = pieces[0].shape[1] // 2
    sums = []
    for matrix in matrices:
        total, col = None, 0
        for piece in pieces:
            size = piece.shape[0]
            term = matmul(matrix[row : row + block, col : col + size], piece[...])
            total = term if total is None else total + term
            col += size
        sums.append(total)
    value = sums[0]
    if mats == 2:
        real, imag = sums
        value = jnp.concatenate(
            [real[:, :half] - imag[:, half:], real[:, half:] + imag[:, :half]], axis=1
        )
    set_blocks(value, outs)


def apply(matrices, pieces, block, exact, row=None):
    rows, cols = matrices[0].shape
    count, mats = rows // block if row is None else 1, len(matrices)
    spec = pl.BlockSpec((block, cols), lambda j: (j, 0)) if row is None else whole()
    shapes = blocks_like(count, block, pieces[0].shape[1], exact) + [TOKEN]
    return pl.pallas_call(
        functools.partial(apply_kernel, mats, len(pieces), block, row or 0),
        grid=(count,),
        in_specs=[spec] * mats + [whole()] * len(pieces),
        out_specs=[whole()] * len(shapes),
        out_shape=shapes,
        compiler_params=params(row is not None),
        cost_estimate=cost(count * mats / 2),
    )(*matrices, *pieces)


def multiply(parts, pieces, block, resident=False):
    blocks, token = [], None
    for part in parts:
        for row in range(0, part[0].shape[0], block) if resident else [None]:
            *more, token = apply(part, pieces, block, not blocks, row)
            blocks += more
    return blocks, token


def sum_kernel(count, own_ref, *refs):
    total = own_ref[...]
    for ref in refs[:count]:
        total = total + ref[...].astype(F32)
    out_ref, rounded_ref, token_ref = refs[-3:]
    out_ref[...] = total
    rounded_ref[...] = total.astype(BF16)
    token_ref[...] = jnp.zeros_like(token_ref)


def sum_of(blocks, after):
    shape = blocks[0].shape
    return pl.pallas_call(
        functools.partial(sum_kernel, len(blocks) - 1),
        in_specs=[whole()] * (len(blocks) + len(after)),
        out_specs=[whole()] * 3,
        out_shape=[
            jax.ShapeDtypeStruct(shape, F32),
            jax.ShapeDtypeStruct(shape, BF16),
            TOKEN,
        ],
        compiler_params=PARAMS,
        cost_estimate=cost(1),
    )(*blocks, *after)


def potential_kernel(count, summed, weight_ref, own_ref, *refs):
    total = own_ref[...]
    for ref in refs[:count]:
        total = total + ref[...].astype(F32)
    out_ref, sum_ref, rounded_ref, token_ref = refs[-4:]
    potential = total.astype(BF16)
    out_ref[...] = potential
    value = weight_ref[0] * potential.astype(F32)
    if summed:
        value = value + refs[count][...]
    sum_ref[...] = value
    rounded_ref[...] = value.astype(BF16)
    token_ref[...] = jnp.zeros_like(token_ref)


def potential_of(weight, blocks, summed, after):
    shape = blocks[0].shape
    return pl.pallas_call(
        functools.partial(potential_kernel, len(blocks) - 1, len(summed)),
        in_specs=[pl.BlockSpec(memory_space=pltpu.SMEM)]
        + [whole()] * (len(blocks) + len(summed) + len(after)),
        out_specs=[whole()] * 4,
        out_shape=[
            jax.ShapeDtypeStruct(shape, BF16),
            jax.ShapeDtypeStruct(shape, F32),
            jax.ShapeDtypeStruct(shape, BF16),
            TOKEN,
        ],
        compiler_params=PARAMS,
        cost_estimate=cost(1),
    )(weight, *blocks, *summed, *after)


def charge_kernel(count, weight_ref, charge_ref, degree_ref, potential_ref, own_ref, *refs):
    around = own_ref[...]
    for ref in refs[:count]:
        around = around + ref[...].astype(F32)
    out_ref, rounded_ref, token_ref = refs[-3:]
    token_ref[...] = jnp.zeros_like(token_ref)
    change = degree_ref[:, 0:1] * potential_ref[...].astype(F32) - around
    value = charge_ref[...] - weight_ref[0] * change
    out_ref[...] = value
    rounded_ref[...] = value.astype(BF16)


def charge_of(weight, charge, degree, potential, blocks, after):
    return pl.pallas_call(
        functools.partial(charge_kernel, len(blocks) - 1),
        in_specs=[pl.BlockSpec(memory_space=pltpu.SMEM)] + [whole()] * (3 + len(blocks) + len(after)),
        out_specs=[whole()] * 3,
        out_shape=[
            jax.ShapeDtypeStruct(charge.shape, F32),
            jax.ShapeDtypeStruct(charge.shape, BF16),
            TOKEN,
        ],
        compiler_params=PARAMS,
        cost_estimate=cost(1),
    )(weight, charge, degree, potential, *blocks, *after)


def current_kernel(count, current_ref, own_ref, *refs):
    change = own_ref[...]
    for ref in refs[:count]:
        change = change + ref[...].astype(F32)
    refs[-1][...] = (current_ref[...].astype(F32) - change).astype(BF16)


def current_of(current, blocks):
    return pl.pallas_call(
        functools.partial(current_kernel, len(blocks) - 1),
        in_specs=[whole()] * (1 + len(blocks)),
        out_specs=whole(),
        out_shape=jax.ShapeDtypeStruct(current.shape, BF16),
        compiler_params=PARAMS,
        cost_estimate=cost(1),
    )(current, *blocks)


def per_device(layout, currents, incidence, centroids, sweep_weights):
    me = lax.axis_index(AXES).astype(I32).reshape(1)
    tri_dev = centroids.shape[1]
    edge_dev = currents.shape[0]
    devices, count = layout.devices, len(layout.plane)
    slots = 8 * tri_dev // devices
    sweeps = sweep_weights.shape[0]
    cols = layout.z * layout.core * tri_dev

    resident = count * 2 * tri_dev * cols * 2 <= 16 * 2**20

    across = layout.across(currents)
    form = Letter(edge_dev, tri_dev, count * slots)
    letters = letters_of(
        layout, form, incidence, centroids, slots, ()
    )
    letters = lax.all_to_all(letters, AXES, split_axis=0, concat_axis=0, tiled=True)
    labels = letters[:, form.starts[3] :, :].reshape(devices, -1)[:, : count * slots]
    labels = labels.reshape(devices, count, slots).transpose(1, 0, 2)
    labels = labels.reshape(count, 1, devices * slots)

    make = functools.partial(build, cols=cols, me=me)
    cut = (count + 1) // 2
    spans = [span for span in (range(cut), range(cut, count)) if span]

    def tile_part(span, token):
        *part, token = make(
            functools.partial(tile_kernel, layout, form, min(512, cols), span[0]),
            2,
            tri_dev,
            span,
            (letters, token),
            6,
            resident=resident,
            scratch=[pltpu.VMEM((16, cols), BF16)],
        )
        return part, token

    def adjacency_part(span, token):
        extra = () if span[0] else (jax.ShapeDtypeStruct((tri_dev, 128), F32),)
        *part, token = make(
            functools.partial(adjacency_kernel, layout, tri_dev, span[0]),
            1,
            tri_dev,
            span,
            (labels, token),
            6,
            extra=extra,
        )
        return part, token

    first, token = make(
        functools.partial(first_kernel, layout, form),
        1,
        tri_dev,
        range(layout.z),
        (letters, labels),
        3,
        cols=count * layout.core * edge_dev,
        resident=resident,
    )
    pieces = layout.gathered(currents, across, (token,))
    blocks, token = multiply([[first]], pieces, tri_dev, resident)
    part, token = tile_part(spans[0], token)
    tiles = [part]
    charge, rounded, token = sum_of(layout.given_along(blocks), (token,))

    def incidence_parts(token):
        parts = []
        for span in spans:
            *part, token = make(
                functools.partial(incidence_kernel, layout, form, span[0]),
                1,
                edge_dev,
                span,
                (letters, token),
                3,
            )
            parts.append(part)
        return parts, token

    near, degree, ends = [], [], None

    def more_adjacency(goal, token):
        for row in range(len(near), goal):
            (part, *extra), token = adjacency_part(range(row, row + 1), token)
            near.append([part])
            degree.extend(extra)
        return token

    summed, potential = (), None
    for sweep in range(sweeps):
        weight = sweep_weights[sweep].reshape(1)
        last = sweep + 1 == sweeps
        for span in spans[len(tiles) :]:
            part, token = tile_part(span, token)
            tiles.append(part)
        if sweep > 0 and ends is None:
            ends, token = incidence_parts(token)
        if not last:
            token = more_adjacency(count // 4, token)
        pieces = layout.gathered(rounded, layout.along(rounded), (token,))
        blocks, token = multiply(tiles, pieces, tri_dev, resident)
        if not last:
            token = more_adjacency(count // 2, token)
        potential, *summed, weighted, token = potential_of(
            weight, layout.given(blocks), summed, (token,)
        )
        if last:
            break
        token = more_adjacency(count, token)
        pieces = layout.gathered(potential, layout.along(potential), (token,))
        blocks, token = multiply(near, pieces, tri_dev, resident)
        charge, rounded, token = charge_of(
            weight, charge, degree[0], potential, layout.given(blocks), (token,)
        )
    if ends is None:
        ends, token = incidence_parts(token)
    pieces = layout.gathered(weighted, layout.along(weighted), (token,))
    blocks, _ = multiply(ends, pieces, edge_dev, resident)
    return current_of(currents, layout.given(blocks)), potential


def solution(mesh):
    layout = Layout(mesh.shape["row"], mesh.shape["col"])
    in_specs = (P(AXES, None), P(None, AXES), P(None, AXES), P())
    out_specs = (P(AXES, None), P(AXES, None))
    return jax.shard_map(
        functools.partial(per_device, layout),
        mesh=mesh,
        in_specs=in_specs,
        out_specs=out_specs,
        check_vma=False,
    )
```

```python
import functools
import math

import jax
import jax.numpy as jnp
from jax import lax
from jax.experimental import pallas as pl
from jax.experimental.pallas import tpu as pltpu
from jax.sharding import PartitionSpec as P

SPACING = 0.2
TURNS = 32.0
AXES = ("row", "col")
ROUND = 12582912.0
COS = (
    0.9999992107823218,
    -19.738980355763992,
    64.92865742103312,
    -85.27162153429882,
    58.79049212013072,
    -21.07110562764302,
)
SIN = (
    6.283184916495431,
    -41.34158923268858,
    81.59994332978287,
    -76.61447253124996,
    41.342882354568324,
    -12.471243535026977,
)
SMALL, LARGE = 10 * 2**20, 24 * 2**20
PARAMS = pltpu.CompilerParams(vmem_limit_bytes=SMALL)
PEAK = 1.15e15
F32, BF16, I32 = jnp.float32, jnp.bfloat16, jnp.int32


def whole():
    return pl.BlockSpec(memory_space=pltpu.VMEM)


def fixed(array):
    return pl.BlockSpec(array.shape, lambda j: (0,) * len(array.shape))


def params(resident):
    return pltpu.CompilerParams(vmem_limit_bytes=SMALL if resident else LARGE)


def cost(microseconds):
    return pl.CostEstimate(
        flops=int(microseconds * 1e-6 * PEAK), bytes_accessed=0, transcendentals=0
    )


TOKEN = jax.ShapeDtypeStruct((8, 128), F32)


def token_spec():
    return pl.BlockSpec((8, 128), lambda *_: (0, 0))


def iota(shape, dim):
    return lax.broadcasted_iota(I32, shape, dim)


def ones_where(mask):
    return jnp.where(mask, jnp.ones((), F32), jnp.zeros((), F32)).astype(BF16)


def matmul(a, b):
    return jnp.dot(a, b, preferred_element_type=F32)


def matmul_nt(a, b):
    return lax.dot_general(a, b, (((1,), (1,)), ((), ())), preferred_element_type=F32)


class Layout:
    def __init__(self, n_row, n_col):
        self.core = 2 if n_row % 2 == 0 else 1
        self.x = n_row // self.core
        self.y = math.gcd(n_col, self.x)
        self.z = n_col // self.y
        self.devices = n_row * n_col
        self.plane = [(dx, dy) for dx in range(self.x) for dy in range(self.y)]

    def digits(self, index):
        y = index % self.y
        z = index // self.y % self.z
        core = index // (self.y * self.z) % self.core
        return index // (self.y * self.z * self.core), core, z, y

    def shift(self, value, dx=0, dc=0, dz=0, dy=0):
        pairs = []
        for i in range(self.devices):
            pairs.append((i, self.near(i, dx, dc, dz, dy)))
        return lax.ppermute(value, AXES, pairs)

    def by_core(self, value):
        return [value] + [self.shift(value, dc=-dc) for dc in range(1, self.core)]

    def along(self, value):
        return [self.shift(value, dz=-dz) for dz in range(1, self.z)]

    def across(self, value):
        return [self.shift(value, dx=-dx, dy=-dy) for dx, dy in self.plane[1:]]

    def gathered(self, value, others, after):
        return self.by_core(value) + (self.by_core(pack(others, after)) if others else [])

    def index(self, x, core, z, y):
        x, core, z, y = x % self.x, core % self.core, z % self.z, y % self.y
        return ((x * self.core + core) * self.z + z) * self.y + y

    def near(self, me, dx=0, dc=0, dz=0, dy=0):
        x, core, z, y = self.digits(me)
        return self.index(x + dx, core + dc, z + dz, y + dy)

    def in_line(self, me, k):
        if k < self.core:
            return self.near(me, dc=k)
        rest = k - self.core
        return self.near(me, dc=rest // (self.z - 1), dz=1 + rest % (self.z - 1))

    def in_plane(self, me, step):
        return self.near(me, dx=step // self.y, dy=step % self.y)

    def in_planes(self, me, k):
        if k < self.core:
            return self.near(me, dc=k)
        rest, others = k - self.core, len(self.plane) - 1
        dx, dy = self.plane[1 + rest % others]
        return self.near(me, dx=dx, dy=dy, dc=rest // others)

    def given_along(self, blocks):
        return [blocks[0]] + [
            self.shift(block, dz=1 + dz) for dz, block in enumerate(blocks[1:])
        ]

    def spot(self, me, step):
        x, _, _, y = self.digits(me)
        return (x + step // self.y) % self.x * self.y + (y + step % self.y) % self.y

    def given(self, blocks):
        return [blocks[0]] + [
            self.shift(block, dx=dx, dy=dy)
            for block, (dx, dy) in zip(blocks[1:], self.plane[1:])
        ]

    def place(self, triangle, tri_dev, me):
        x, core, z, y = self.digits(triangle // tri_dev)
        mx, mcore, mz, my = self.digits(me)
        dz, dc = (z - mz) % self.z, (core - mcore) % self.core
        block = jnp.where(dz == 0, dc, self.core + dc * (self.z - 1) + dz - 1)
        inside = (x == mx) & (y == my)
        return jnp.where(inside, block * tri_dev + triangle % tri_dev, -1)


class Letter:
    def __init__(self, edges, tri_dev, labels):
        self.edges, self.tri_dev, self.half = edges, tri_dev, -(-tri_dev // 2)
        sizes = [edges, tri_dev, self.half, labels]
        starts = [0]
        for size in sizes:
            starts.append(starts[-1] + -(-size // 128))
        self.starts, self.rows = starts[:4], -(-starts[4] // 8) * 8

    def take(self, letter, part, size):
        first = self.starts[part]
        parts = [letter[first + k : first + k + 1, :] for k in range(-(-size // 128))]
        return jnp.concatenate(parts, axis=1)[:, :size]

    def ends(self, letter):
        pair = self.take(letter, 0, self.edges)
        return pair & 0xFFFF, lax.shift_right_logical(pair, 16)

    def points(self, letter):
        first = self.take(letter, 1, self.tri_dev)
        third = self.take(letter, 2, self.half)
        third = jnp.concatenate([third & 0xFFFF, lax.shift_right_logical(third, 16)], axis=1)
        return jnp.concatenate(
            [first & 0xFFFF, lax.shift_right_logical(first, 16), third[:, : self.tri_dev]], axis=0
        )


def in_rows(row):
    size = row.shape[1]
    if size % 128:
        row = jnp.concatenate([row, jnp.zeros((1, -size % 128), I32)], axis=1)
    return [row[:, k : k + 128] for k in range(0, row.shape[1], 128)]


def letter_kernel(layout, form, slots, inc_ref, points_ref, *refs):
    letter_ref = refs[-1]
    edges, tri_dev, half = form.edges, form.tri_dev, form.half
    ends, devices = 2 * edges, layout.devices
    plus, minus = inc_ref[0:1, :], inc_ref[1:2, :]
    tri = jnp.concatenate([plus, minus], axis=1)
    other = jnp.concatenate([minus, plus], axis=1)
    owner = tri // tri_dev
    hits = iota((devices, ends), 0) == owner
    upper = ones_where(iota((ends, ends), 0) <= iota((ends, ends), 1))
    count = matmul(ones_where(hits), upper)
    rank = jnp.sum(jnp.where(hits, count, 0.0), axis=0, keepdims=True).astype(I32) - 1
    order = ones_where(iota((slots, ends), 0) == rank)
    label = jnp.zeros((devices, slots), I32)
    digits = ((tri % tri_dev + 1, 1), (other & 255, 65536), (other >> 8, 65536 * 256))
    for digit, weight in digits:
        spread = jnp.where(hits, digit.astype(F32), 0.0).astype(BF16)
        label = label + matmul_nt(spread, order).astype(I32) * weight
    third = points_ref[2:3, :]
    if tri_dev % 2:
        third = jnp.concatenate([third, jnp.zeros((1, 1), I32)], axis=1)
    common = (
        in_rows(plus + (minus << 16))
        + in_rows(points_ref[0:1, :] + (points_ref[1:2, :] << 16))
        + in_rows(third[:, :half] + (third[:, half:] << 16))
    )
    places = [(x, y) for x in range(layout.x) for y in range(layout.y)]
    for core in range(layout.core):
        for z in range(layout.z):
            there = [layout.index(x, core, z, y) for x, y in places]
            mine = in_rows(jnp.concatenate([label[d : d + 1, :] for d in there], axis=1))
            blank = form.rows - len(common) - len(mine)
            rows = common + mine + [jnp.zeros((1, 128), I32)] * blank
            letter = jnp.concatenate(rows, axis=0)
            for d in there:
                letter_ref[d] = letter


def letters_of(layout, form, incidence, centroids, slots, after):
    return pl.pallas_call(
        functools.partial(letter_kernel, layout, form, slots),
        in_specs=[whole()] * (2 + len(after)),
        out_specs=whole(),
        out_shape=jax.ShapeDtypeStruct((layout.devices, form.rows, 128), I32),
        compiler_params=PARAMS,
        cost_estimate=cost(1),
    )(incidence, centroids, *after)


def pack_kernel(count, *refs):
    out_ref = refs[-1]
    size = refs[0].shape[0]
    for k in range(count):
        out_ref[k * size : (k + 1) * size, :] = refs[k][...]


def pack(pieces, after):
    size, width = pieces[0].shape
    return pl.pallas_call(
        functools.partial(pack_kernel, len(pieces)),
        in_specs=[whole()] * (len(pieces) + len(after)),
        out_specs=whole(),
        out_shape=jax.ShapeDtypeStruct((len(pieces) * size, width), BF16),
        compiler_params=PARAMS,
        cost_estimate=cost(0.5),
    )(*pieces, *after)


def features(points, scale, first):
    rows, count = points.shape
    square = jnp.sum(points * points, axis=0, keepdims=True)
    norms = [square & 255, square & 0xFF00, square & 0xFF0000]
    ones = [jnp.ones_like(square)] * 3
    zeros = [jnp.zeros((16 - rows - 7, count), I32)]
    if first:
        parts = [-2 * points] + norms + ones + [ones[0]] + zeros
    else:
        parts = [points] + ones + norms + [ones[0]] + zeros
    return (jnp.concatenate(parts, axis=0).astype(F32) * scale).astype(BF16)


def poly(coefs, scale, u):
    value = jnp.full_like(u, coefs[-1] * scale)
    for coef in coefs[-2::-1]:
        value = value * u + coef * scale
    return value


def rows_at(ref, step, rows):
    if ref.shape[0] == rows:
        return ref
    return ref.at[pl.ds(pl.multiple_of(step * rows, rows), rows), :]


def tile_kernel(layout, form, block, first, me_ref, letter_ref, after_ref, *refs):
    real_ref, imag_ref, token_ref, col_ref = refs
    token_ref[...] = jnp.zeros_like(token_ref)
    me, step, size = me_ref[0], pl.program_id(0), form.tri_dev

    @pl.when(step == 0)
    def _():
        for k in range(layout.z * layout.core):
            letter = letter_ref[layout.in_line(me, k)]
            col_ref[:, k * size : (k + 1) * size] = features(form.points(letter), 1.0, False)

    real_ref, imag_ref = [rows_at(ref, step, size) for ref in (real_ref, imag_ref)]
    letter = letter_ref[layout.in_plane(me, first + step)]
    row = features(form.points(letter), 1.0 / (TURNS * TURNS), True)
    for base in range(0, col_ref.shape[1], block):
        cols = slice(base, base + block)
        square = lax.dot_general(
            row, col_ref[:, cols], (((0,), (0,)), ((), ())), preferred_element_type=F32
        )
        inverse = lax.rsqrt(square)
        turns = square * inverse
        frac = turns - ((turns + ROUND) - ROUND)
        u = frac * frac
        real_ref[:, cols] = (poly(COS, SPACING / TURNS, u) * inverse).astype(BF16)
        imag_ref[:, cols] = (poly(SIN, -SPACING / TURNS, u) * (frac * inverse)).astype(BF16)


def build(
    kernel, outs, rows, span, arrays, time, cols, me, resident=False, scratch=(), extra=()
):
    space = pltpu.VMEM if resident else pltpu.HBM
    block = whole() if resident else pl.BlockSpec((rows, cols), lambda j: (j, 0))
    return pl.pallas_call(
        kernel,
        grid=(len(span),),
        in_specs=[pl.BlockSpec(memory_space=pltpu.SMEM)] + [fixed(array) for array in arrays],
        out_specs=[block] * outs + [fixed(array) for array in extra] + [token_spec()],
        out_shape=[space((len(span) * rows, cols), BF16)] * outs + list(extra) + [TOKEN],
        scratch_shapes=scratch,
        compiler_params=params(resident),
        cost_estimate=cost(time),
    )(me, *arrays)


def pick(row, base, count):
    low = jnp.where((row >= base) & (row < base + count), row - base, -1)
    wanted = iota((count, row.shape[1]), 0).astype(F32).astype(BF16)
    same = wanted == low.astype(F32).astype(BF16)
    return jnp.where(same, jnp.ones((), BF16), jnp.zeros((), BF16))


def adjacency_kernel(layout, tri_dev, first, me_ref, label_ref, after_ref, out_ref, *refs):
    refs[-1][...] = jnp.zeros_like(refs[-1])
    me, step = me_ref[0], pl.program_id(0)
    rows, cols = tri_dev, out_ref.shape[1]
    out_ref = rows_at(out_ref, step, rows)
    label = label_ref[layout.spot(me, first + step)]
    mark = (label & 0xFFFF) - 1
    place = layout.place(lax.shift_right_logical(label, 16), tri_dev, me)
    place = jnp.where(mark >= 0, place, -1)
    low = pick(jnp.where(place >= 0, place % rows, -1), 0, rows)
    for base in range(0, cols, rows):
        inside = (place >= base) & (place < base + rows)
        here = pick(jnp.where(inside, mark, -1), 0, rows)
        out_ref[:, base : base + rows] = matmul_nt(here, low).astype(BF16)
    if first == 0:

        @pl.when(step == 0)
        def _():
            every = pick(mark, 0, rows)
            refs[0][...] = matmul(every, jnp.ones((every.shape[1], 128), BF16))


def incidence_kernel(layout, form, first, me_ref, letter_ref, after_ref, out_ref, token_ref):
    token_ref[...] = jnp.zeros_like(token_ref)
    me, step = me_ref[0], pl.program_id(0)
    edges, cols = form.edges, out_ref.shape[1]
    out_ref = rows_at(out_ref, step, edges)
    size = form.tri_dev
    letter = letter_ref[layout.in_plane(me, first + step)]
    plus, minus = [layout.place(end, size, me) for end in form.ends(letter)]
    eye = ones_where(iota((edges, edges), 0) == iota((edges, edges), 1))
    for base in range(0, cols, size):
        signed = pick(plus, base, size) - pick(minus, base, size)
        out_ref[:, base : base + size] = matmul_nt(eye, signed).astype(BF16)


def set_blocks(value, outs):
    for k, out in enumerate(outs):

        @pl.when(pl.program_id(0) == k)
        def _(out=out):
            out[...] = value.astype(out.dtype)


def blocks_like(count, rows, width, exact):
    return [
        jax.ShapeDtypeStruct((rows, width), F32 if exact and k == 0 else BF16)
        for k in range(count)
    ]


def first_kernel(layout, form, me_ref, letter_ref, after_ref, out_ref, token_ref):
    token_ref[...] = jnp.zeros_like(token_ref)
    me, step = me_ref[0], pl.program_id(0)
    size, edges = form.tri_dev, form.edges
    out_ref = rows_at(out_ref, step, size)
    base = layout.near(me, dz=step) * size
    for k in range(out_ref.shape[1] // edges):
        plus, minus = form.ends(letter_ref[layout.in_planes(me, k)])
        signed = pick(plus, base, size) - pick(minus, base, size)
        out_ref[:, k * edges : (k + 1) * edges] = signed


def apply_kernel(mats, fed, block, row, *refs):
    matrices, pieces, outs = refs[:mats], refs[mats : mats + fed], refs[mats + fed : -1]
    refs[-1][...] = jnp.zeros_like(refs[-1])
    half = pieces[0].shape[1] // 2
    sums = []
    for matrix in matrices:
        total, col = None, 0
        for piece in pieces:
            size = piece.shape[0]
            term = matmul(matrix[row : row + block, col : col + size], piece[...])
            total = term if total is None else total + term
            col += size
        sums.append(total)
    value = sums[0]
    if mats == 2:
        real, imag = sums
        value = jnp.concatenate(
            [real[:, :half] - imag[:, half:], real[:, half:] + imag[:, :half]], axis=1
        )
    set_blocks(value, outs)


def apply(matrices, pieces, block, exact, row=None):
    rows, cols = matrices[0].shape
    count, mats = rows // block if row is None else 1, len(matrices)
    spec = pl.BlockSpec((block, cols), lambda j: (j, 0)) if row is None else whole()
    shapes = blocks_like(count, block, pieces[0].shape[1], exact) + [TOKEN]
    return pl.pallas_call(
        functools.partial(apply_kernel, mats, len(pieces), block, row or 0),
        grid=(count,),
        in_specs=[spec] * mats + [whole()] * len(pieces),
        out_specs=[whole()] * len(shapes),
        out_shape=shapes,
        compiler_params=params(row is not None),
        cost_estimate=cost(count * mats / 2),
    )(*matrices, *pieces)


def multiply(parts, pieces, block, resident=False):
    blocks, token = [], None
    for part in parts:
        for row in range(0, part[0].shape[0], block) if resident else [None]:
            *more, token = apply(part, pieces, block, not blocks, row)
            blocks += more
    return blocks, token


def sum_kernel(count, own_ref, *refs):
    total = own_ref[...]
    for ref in refs[:count]:
        total = total + ref[...].astype(F32)
    out_ref, rounded_ref, token_ref = refs[-3:]
    out_ref[...] = total
    rounded_ref[...] = total.astype(BF16)
    token_ref[...] = jnp.zeros_like(token_ref)


def sum_of(blocks, after):
    shape = blocks[0].shape
    return pl.pallas_call(
        functools.partial(sum_kernel, len(blocks) - 1),
        in_specs=[whole()] * (len(blocks) + len(after)),
        out_specs=[whole()] * 3,
        out_shape=[
            jax.ShapeDtypeStruct(shape, F32),
            jax.ShapeDtypeStruct(shape, BF16),
            TOKEN,
        ],
        compiler_params=PARAMS,
        cost_estimate=cost(1),
    )(*blocks, *after)


def potential_kernel(count, summed, weight_ref, own_ref, *refs):
    total = own_ref[...]
    for ref in refs[:count]:
        total = total + ref[...].astype(F32)
    out_ref, sum_ref, token_ref = refs[-3:]
    potential = total.astype(BF16)
    out_ref[...] = potential
    value = weight_ref[0] * potential.astype(F32)
    if summed:
        value = value + refs[count][...]
    sum_ref[...] = value.astype(sum_ref.dtype)
    token_ref[...] = jnp.zeros_like(token_ref)


def potential_of(weight, blocks, summed, after, last):
    shape = blocks[0].shape
    return pl.pallas_call(
        functools.partial(potential_kernel, len(blocks) - 1, len(summed)),
        in_specs=[pl.BlockSpec(memory_space=pltpu.SMEM)]
        + [whole()] * (len(blocks) + len(summed) + len(after)),
        out_specs=[whole()] * 3,
        out_shape=[
            jax.ShapeDtypeStruct(shape, BF16),
            jax.ShapeDtypeStruct(shape, BF16 if last else F32),
            TOKEN,
        ],
        compiler_params=PARAMS,
        cost_estimate=cost(1),
    )(weight, *blocks, *summed, *after)


def charge_kernel(count, weight_ref, charge_ref, degree_ref, potential_ref, own_ref, *refs):
    around = own_ref[...]
    for ref in refs[:count]:
        around = around + ref[...].astype(F32)
    out_ref, rounded_ref, token_ref = refs[-3:]
    token_ref[...] = jnp.zeros_like(token_ref)
    change = degree_ref[:, 0:1] * potential_ref[...].astype(F32) - around
    value = charge_ref[...] - weight_ref[0] * change
    out_ref[...] = value
    rounded_ref[...] = value.astype(BF16)


def charge_of(weight, charge, degree, potential, blocks, after):
    return pl.pallas_call(
        functools.partial(charge_kernel, len(blocks) - 1),
        in_specs=[pl.BlockSpec(memory_space=pltpu.SMEM)] + [whole()] * (3 + len(blocks) + len(after)),
        out_specs=[whole()] * 3,
        out_shape=[
            jax.ShapeDtypeStruct(charge.shape, F32),
            jax.ShapeDtypeStruct(charge.shape, BF16),
            TOKEN,
        ],
        compiler_params=PARAMS,
        cost_estimate=cost(1),
    )(weight, charge, degree, potential, *blocks, *after)


def current_kernel(count, current_ref, own_ref, *refs):
    change = own_ref[...]
    for ref in refs[:count]:
        change = change + ref[...].astype(F32)
    refs[-1][...] = (current_ref[...].astype(F32) - change).astype(BF16)


def current_of(current, blocks):
    return pl.pallas_call(
        functools.partial(current_kernel, len(blocks) - 1),
        in_specs=[whole()] * (1 + len(blocks)),
        out_specs=whole(),
        out_shape=jax.ShapeDtypeStruct(current.shape, BF16),
        compiler_params=PARAMS,
        cost_estimate=cost(1),
    )(current, *blocks)


def per_device(layout, currents, incidence, centroids, sweep_weights):
    me = lax.axis_index(AXES).astype(I32).reshape(1)
    tri_dev = centroids.shape[1]
    edge_dev = currents.shape[0]
    devices, count = layout.devices, len(layout.plane)
    slots = 8 * tri_dev // devices
    sweeps = sweep_weights.shape[0]
    cols = layout.z * layout.core * tri_dev

    resident = count * 2 * tri_dev * cols * 2 <= 16 * 2**20

    across = layout.across(currents)
    form = Letter(edge_dev, tri_dev, count * slots)
    letters = letters_of(
        layout, form, incidence, centroids, slots, ()
    )
    letters = lax.all_to_all(letters, AXES, split_axis=0, concat_axis=0, tiled=True)
    labels = letters[:, form.starts[3] :, :].reshape(devices, -1)[:, : count * slots]
    labels = labels.reshape(devices, count, slots).transpose(1, 0, 2)
    labels = labels.reshape(count, 1, devices * slots)

    make = functools.partial(build, cols=cols, me=me)
    cut = (count + 1) // 2
    spans = [span for span in (range(cut), range(cut, count)) if span]

    def tile_part(span, token):
        *part, token = make(
            functools.partial(tile_kernel, layout, form, min(512, cols), span[0]),
            2,
            tri_dev,
            span,
            (letters, token),
            6,
            resident=resident,
            scratch=[pltpu.VMEM((16, cols), BF16)],
        )
        return part, token

    def adjacency_part(span, token):
        extra = () if span[0] else (jax.ShapeDtypeStruct((tri_dev, 128), F32),)
        *part, token = make(
            functools.partial(adjacency_kernel, layout, tri_dev, span[0]),
            1,
            tri_dev,
            span,
            (labels, token),
            6,
            extra=extra,
        )
        return part, token

    first, token = make(
        functools.partial(first_kernel, layout, form),
        1,
        tri_dev,
        range(layout.z),
        (letters, labels),
        3,
        cols=count * layout.core * edge_dev,
        resident=resident,
    )
    pieces = layout.gathered(currents, across, (token,))
    blocks, token = multiply([[first]], pieces, tri_dev, resident)
    part, token = tile_part(spans[0], token)
    tiles = [part]
    charge, rounded, token = sum_of(layout.given_along(blocks), (token,))

    def incidence_parts(token):
        parts = []
        for span in spans:
            *part, token = make(
                functools.partial(incidence_kernel, layout, form, span[0]),
                1,
                edge_dev,
                span,
                (letters, token),
                3,
            )
            parts.append(part)
        return parts, token

    near, degree, ends = [], [], None

    def more_adjacency(goal, token):
        for row in range(len(near), goal):
            (part, *extra), token = adjacency_part(range(row, row + 1), token)
            near.append([part])
            degree.extend(extra)
        return token

    summed, potential = (), None
    for sweep in range(sweeps):
        weight = sweep_weights[sweep].reshape(1)
        last = sweep + 1 == sweeps
        for span in spans[len(tiles) :]:
            part, token = tile_part(span, token)
            tiles.append(part)
        if sweep > 0 and ends is None:
            ends, token = incidence_parts(token)
        if not last:
            token = more_adjacency(count // 4, token)
        pieces = layout.gathered(rounded, layout.along(rounded), (token,))
        blocks, token = multiply(tiles, pieces, tri_dev, resident)
        if not last:
            token = more_adjacency(count // 2, token)
        potential, weighted, token = potential_of(
            weight, layout.given(blocks), summed, (token,), last
        )
        summed = (weighted,)
        if last:
            break
        token = more_adjacency(count, token)
        pieces = layout.gathered(potential, layout.along(potential), (token,))
        blocks, token = multiply(near, pieces, tri_dev, resident)
        charge, rounded, token = charge_of(
            weight, charge, degree[0], potential, layout.given(blocks), (token,)
        )
    if ends is None:
        ends, token = incidence_parts(token)
    pieces = layout.gathered(weighted, layout.along(weighted), (token,))
    blocks, _ = multiply(ends, pieces, edge_dev, resident)
    return current_of(currents, layout.given(blocks)), potential


def solution(mesh):
    layout = Layout(mesh.shape["row"], mesh.shape["col"])
    in_specs = (P(AXES, None), P(None, AXES), P(None, AXES), P())
    out_specs = (P(AXES, None), P(AXES, None))
    return jax.shard_map(
        functools.partial(per_device, layout),
        mesh=mesh,
        in_specs=in_specs,
        out_specs=out_specs,
        check_vma=False,
    )
```
